128 devices in a mesh: fsdp: 8 (over x, z_hi), seq: 16 (over y, z_lo, core).
Axes of the slice: x: 4, y: 4, z: 4 (z_hi: 2, z_lo: 2; z = z_hi * 2 + z_lo), core: 2. Of those that a mesh axis runs over, the one named last changes fastest.
Arguments:
- tokens: bfloat16 [16, 2048, 1024], P('fsdp', 'seq'), may hold values from -6 to 6
- teacher: bfloat16 [16, 2048, 1024], P('fsdp', 'seq'), may hold values from -6 to 6
- lengths: int32 [16], P('fsdp'), may hold values from 1024 to 2048, as said below
- attention_gain: bfloat16 [1024], P(('fsdp', 'seq')), may hold values from 0.5 to 1.5
- input_weight: bfloat16 [1024, 2048], P(('fsdp', 'seq')), may hold values from -0.1875 to 0.1875
- query_gain: bfloat16 [64], replicated, may hold values from 1 to 1.59375
- key_gain: bfloat16 [64], replicated, may hold values from 1 to 1.59375
- output_weight: bfloat16 [1024, 1024], P(None, ('fsdp', 'seq')), may hold values from -2 to 2
- feed_gain: bfloat16 [1024], P(('fsdp', 'seq')), may hold values from 0.5 to 1.5
- gate_weight: bfloat16 [1024, 4608], P(('fsdp', 'seq')), may hold values from -0.1875 to 0.1875
- up_weight: bfloat16 [1024, 4608], P(('fsdp', 'seq')), may hold values from -0.1875 to 0.1875
- down_weight: bfloat16 [4608, 1024], P(None, ('fsdp', 'seq')), may hold values from -0.09375 to 0.09375
Outputs:
- block_out: bfloat16 [16, 2048, 1024], P('fsdp', 'seq')
- loss: float32 [], replicated
- token_grads: float32 [16, 2048, 1024], P('fsdp', 'seq')
- attention_gain_grad: float32 [1024], P(('fsdp', 'seq'))
- input_weight_grad: float32 [1024, 2048], P(('fsdp', 'seq'))
- query_gain_grad: float32 [64], replicated
- key_gain_grad: float32 [64], replicated
- output_weight_grad: float32 [1024, 1024], P(None, ('fsdp', 'seq'))
- feed_gain_grad: float32 [1024], P(('fsdp', 'seq'))
- gate_weight_grad: float32 [1024, 4608], P(('fsdp', 'seq'))
- up_weight_grad: float32 [1024, 4608], P(('fsdp', 'seq'))
- down_weight_grad: float32 [4608, 1024], P(None, ('fsdp', 'seq'))
The draws below stay inside these ranges and needn't reach their ends.
Inputs may be any that keep to these rules, and one draw needn't show every extreme that they name: Of the 2 sequences that one index of fsdp holds, one (drawn) has all 2048 slots valid; the lengths of the others are drawn independently.
All inputs are finite; a program needn't handle non-finite values.
Results may differ from the reference program's by a relative error of at most 0.012.
The reference program's roundings to bfloat16 on the way count: a program that leaves them out, or rounds other values in their place, can miss the bound.
Values may be sent and summed in bfloat16 or wider, within the bound.
A program may use at most 192 MiB of HBM per device.

```python
import math
import jax
import jax.numpy as jnp
from jax import lax

D = 1024
HEADS = 16
KV_HEADS = 8
HEAD_DIM = 64
FF = 4608
SLOTS = 2048
MIN_LEN = 1024
GROUP_SEQS = 2
SEQUENCES = 16
ATTN_WIDTH = 1024
QKV = 2048


def draw_lengths(key, part):
    key = jax.random.fold_in(key, 11)
    first, second = jax.random.split(key)
    spans = jax.random.randint(first, (SEQUENCES,), MIN_LEN, SLOTS + 1, dtype=jnp.int32)
    chosen = jax.random.randint(second, (SEQUENCES // GROUP_SEQS,), 0, GROUP_SEQS, dtype=jnp.int32)
    places = jnp.arange(SEQUENCES, dtype=jnp.int32)
    full = places % GROUP_SEQS == jnp.repeat(chosen, GROUP_SEQS)
    return jnp.where(full, SLOTS, spans).astype(jnp.int32)


def raised(result, rng, source, target, parts, factor):
    def block_of(dim):
        return (jnp.arange(result.shape[dim]) // (result.shape[dim] // parts)).reshape((-1,) + (1,) * (result.ndim - 1 - dim))

    one_side = jax.random.permutation(rng, parts)[block_of(target)]
    far = (block_of(target) + parts // 2) % parts
    return jnp.where((block_of(source) == one_side) | (block_of(source) == far), factor * result, result)


def steps_of(rng, dims, cuts, least, top_value):
    level = 1.0
    for dim, shards_of in cuts:
        heights = jax.random.uniform(jax.random.fold_in(jax.random.fold_in(rng, 6), dim), (shards_of,), jnp.float32, least / len(cuts), top_value / len(cuts))
        level = level * jnp.repeat(jnp.exp(heights), dims[dim] // shards_of).reshape((-1,) + (1,) * (len(dims) - 1 - dim))
    return level


def noise(rng, dims, spread, limit, shards=(), kind=jnp.bfloat16):
    values = jax.random.normal(rng, dims, jnp.float32) * spread
    if len(shards) > 0:
        values = steps_of(rng, dims, shards, -0.22, 0.18) * values
    return jnp.clip(values, min=-limit, max=limit).astype(kind)


def bell_draw_with(own_key, extent, deviation, reach, cuts, heavy, kind=jnp.bfloat16):
    entries = deviation * jax.random.normal(own_key, extent, jnp.float32)
    if cuts:
        entries = entries * steps_of(own_key, extent, cuts, -0.22, 0.18)
    return jnp.clip(raised(entries, jax.random.fold_in(own_key, 3), *heavy), -reach, reach).astype(kind)


def setup_inputs(seed: int = 0) -> dict:
    key_of = jax.random.split(jax.random.key(seed), 13)
    return {
        "tokens": bell_draw_with(key_of[0], (SEQUENCES, SLOTS, D), 1.0, 6.0, ((0, 8), (1, 16)), (1, 2, 16, 2.0)),
        "teacher": bell_draw_with(key_of[1], (SEQUENCES, SLOTS, D), 1.0, 6.0, ((0, 8), (1, 16)), (1, 2, 16, 2.0)),
        "lengths": draw_lengths(jax.random.fold_in(key_of[12], 71), 0),
        "attention_gain": jnp.clip(1.0 + 0.1 * jax.random.normal(key_of[3], (D,), jnp.float32), 0.5, 1.5).astype(jnp.bfloat16),
        "input_weight": noise(key_of[4], (D, QKV), D ** -0.5, 0.1875, ((0, 128),)),
        "query_gain": jnp.clip(jax.random.uniform(key_of[5], (HEAD_DIM,), jnp.float32, 1.0, 1.59375), 1.0, 1.59375).astype(jnp.bfloat16),
        "key_gain": jnp.clip(jax.random.uniform(key_of[6], (HEAD_DIM,), jnp.float32, 1.0, 1.59375), 1.0, 1.59375).astype(jnp.bfloat16),
        "output_weight": noise(key_of[7], (ATTN_WIDTH, D), (max(1, ATTN_WIDTH * 16 // SLOTS)) ** -0.5, 2.0, ((1, 128),)),
        "feed_gain": jnp.clip(1.0 + 0.1 * jax.random.normal(key_of[8], (D,), jnp.float32), 0.5, 1.5).astype(jnp.bfloat16),
        "gate_weight": noise(key_of[9], (D, FF), D ** -0.5, 0.1875, ((0, 128),)),
        "up_weight": noise(key_of[10], (D, FF), D ** -0.5, 0.1875, ((0, 128),)),
        "down_weight": noise(key_of[11], (FF, D), FF ** -0.5, 0.09375, ((1, 128),)),
    }


EPS = 1e-05
THETA = 1000000.0
BIG = 1e+30
HIGH = lax.Precision.HIGHEST

@jax.custom_vjp
def low(v):
    return lax.optimization_barrier(v.astype(jnp.bfloat16)).astype(jnp.float32)

@jax.custom_vjp
def low_back(v):
    return v

def low_keep(v):
    return (low(v), None)

def low_pass(kept, grad):
    return (grad,)

def back_keep(v):
    return (v, None)

def back_low(kept, grad):
    return (low(grad),)
low.defvjp(low_keep, low_pass)
low_back.defvjp(back_keep, back_low)

def rotate(values):
    half = values.shape[-1] // 2
    return jnp.concatenate([-values[..., half:], values[..., :half]], axis=-1)

def rope_tables(positions, width):
    freqs = THETA ** (-(2.0 * jnp.arange(width // 2, dtype=jnp.float32)) / width)
    angles = positions.astype(jnp.float32)[:, None] * freqs[None, :]
    angles = jnp.concatenate([angles, angles], axis=-1)
    return (jnp.cos(angles), jnp.sin(angles))

def norm(values, gain):
    return values * lax.rsqrt(lax.optimization_barrier(jnp.mean(values * values, axis=-1, keepdims=True)) + EPS) * gain

def attend_block(query_all, key_all, value_all, length_all, start):
    block = min(512, SLOTS)
    query_block = lax.dynamic_slice_in_dim(query_all, start, block, 1)
    scores = jnp.einsum('pqhd,pkhd->phqk', query_block, key_all, precision=HIGH) * (1.0 / math.sqrt(HEAD_DIM))
    scores = low_back(scores)
    query_place = start + jnp.arange(block, dtype=jnp.int32)
    key_place = jnp.arange(SLOTS, dtype=jnp.int32)
    allowed = (key_place[None, None, :] <= query_place[None, :, None]) & (key_place[None, None, :] < length_all[:, None, None])
    scores = jnp.where(allowed[:, None], scores, -BIG)
    largest = lax.optimization_barrier(jnp.max(scores, axis=-1, keepdims=True))
    weights = jnp.exp(scores - largest)
    chances = weights / lax.optimization_barrier(jnp.sum(weights, axis=-1, keepdims=True))
    return jnp.einsum('phqk,pkhd->pqhd', low(chances), value_all, precision=HIGH)

def forward(params, inputs, target_pack, span_pack):
    attention_gain, input_weight, query_gain, key_gain, output_weight, feed_gain, gate_weight, up_weight, down_weight = params
    packed = inputs.shape[0]
    normed = low(norm(inputs, attention_gain))
    mixed = low_back(jnp.einsum('psd,de->pse', normed, input_weight, precision=HIGH))
    kv_width = KV_HEADS * HEAD_DIM
    queries = mixed[..., :ATTN_WIDTH].reshape(packed, SLOTS, HEADS, HEAD_DIM)
    keys = mixed[..., ATTN_WIDTH:ATTN_WIDTH + kv_width].reshape(packed, SLOTS, KV_HEADS, HEAD_DIM)
    values = mixed[..., ATTN_WIDTH + kv_width:].reshape(packed, SLOTS, KV_HEADS, HEAD_DIM)
    cosine, sine = rope_tables(jnp.arange(SLOTS, dtype=jnp.int32), HEAD_DIM)
    cosine = cosine[None, :, None, :]
    sine = sine[None, :, None, :]
    query_norm = norm(queries, query_gain)
    key_norm = norm(keys, key_gain)
    query_send = low(query_norm * cosine + rotate(query_norm) * sine)
    key_send = low(key_norm * cosine + rotate(key_norm) * sine)
    value_send = low(values)
    key_full = jnp.repeat(key_send, HEADS // KV_HEADS, axis=2)
    value_full = jnp.repeat(value_send, HEADS // KV_HEADS, axis=2)
    block = min(512, SLOTS)
    starts = jnp.arange(SLOTS // block, dtype=jnp.int32) * block
    checked = jax.checkpoint(attend_block)
    attended = lax.map(lambda start: checked(query_send, key_full, value_full, span_pack, start), starts)
    attended = jnp.moveaxis(attended, 0, 1).reshape(packed, SLOTS, ATTN_WIDTH)
    attended = low(low_back(attended))
    resid = inputs + low_back(jnp.einsum('pse,ed->psd', attended, output_weight, precision=HIGH))
    normed_feed = low(norm(resid, feed_gain))
    gate = low_back(jnp.einsum('psd,df->psf', normed_feed, gate_weight, precision=HIGH))
    up = low_back(jnp.einsum('psd,df->psf', normed_feed, up_weight, precision=HIGH))
    act = low(jax.nn.silu(gate) * up)
    final = resid + low_back(jnp.einsum('psf,fd->psd', act, down_weight, precision=HIGH))
    valid = (jnp.arange(SLOTS, dtype=jnp.int32)[None, :] < span_pack[:, None]).astype(jnp.float32)
    diff = (final - target_pack) * valid[..., None]
    squares = jnp.sum(diff * diff)
    return (squares / 2.0, (final, squares, jnp.sum(valid)))

def reference(tokens, teacher, lengths, attention_gain, input_weight, query_gain, key_gain, output_weight, feed_gain, gate_weight, up_weight, down_weight):
    params = tuple((item.astype(jnp.float32) for item in (attention_gain, input_weight, query_gain, key_gain, output_weight, feed_gain, gate_weight, up_weight, down_weight)))
    pack = math.gcd(SEQUENCES, max(1, 4096 // SLOTS))
    packs = SEQUENCES // pack
    inputs_all = tokens.astype(jnp.float32).reshape(packs, pack, SLOTS, D)
    targets_all = teacher.astype(jnp.float32).reshape(packs, pack, SLOTS, D)
    spans_all = lengths.astype(jnp.int32).reshape(packs, pack)

    def one_pack(sums, items):
        inputs_pack, target_pack, span_pack = items

        def closed(params_in, inputs_in):
            return forward(params_in, inputs_in, target_pack, span_pack)
        half, pullback, extra = jax.vjp(closed, params, inputs_pack, has_aux=True)
        grads_params, grads_inputs = pullback(jnp.ones((), jnp.float32))
        sums = tuple((left + right for left, right in zip(sums, grads_params)))
        final, squares, counted = extra
        return (sums, (final, grads_inputs, squares, counted))
    start_sums = tuple((jnp.zeros_like(item) for item in params))
    sums, (finals, grads_inputs, squares, counted) = lax.scan(one_pack, start_sums, (inputs_all, targets_all, spans_all))
    loss = jnp.sum(squares) / (jnp.sum(counted) * D)
    block_out = finals.reshape(SEQUENCES, SLOTS, D).astype(jnp.bfloat16)
    token_grads = grads_inputs.reshape(SEQUENCES, SLOTS, D)
    return (block_out, loss, token_grads, sums[0], sums[1], sums[2], sums[3], sums[4], sums[5], sums[6], sums[7], sums[8])
```

```python
import functools
import math

import jax
import jax.numpy as jnp
from jax import lax
from jax.experimental import pallas as pl
from jax.experimental.pallas import tpu as pltpu
from jax.sharding import PartitionSpec as P

EPS = 1e-05
THETA = 1000000.0
MESH = pl.DeviceIdType.MESH
F32 = jnp.float32
BF16 = jnp.bfloat16
WIDTHS = (512, 512, 640, 2304, 2304, 2304)
STARTS = (0, 512, 1024, 1664, 3968, 6272)
PACKED = 8576
ORDERS = ("xyz", "yzx", "zxy", "xyz", "yzx", "zxy")
LOG2E = 1.4426950408889634
HIGH = lax.Precision.HIGHEST


class Place:
    def __init__(self):
        self.fsdp = lax.axis_index("fsdp")
        self.seq = lax.axis_index("seq")
        self.x = self.fsdp // 2
        self.zh = self.fsdp % 2
        self.y = self.seq // 4
        self.zl = (self.seq // 2) % 2
        self.core = self.seq % 2
        self.chip = self.seq // 2
        self.z = self.zh * 2 + self.zl

    def sibling(self):
        return (self.fsdp, self.seq + 1 - 2 * self.core)

    def moved(self, axis, step):
        x, y, z = self.x, self.y, self.z
        if axis == "x":
            x = (x + step) % 4
        elif axis == "y":
            y = (y + step) % 4
        else:
            z = (z + step) % 4
        zh, zl = z // 2, z % 2
        return (x, zh, y, zl), (x * 2 + zh, y * 4 + zl * 2 + self.core)

    def block(self, whole):
        full = slice(None)
        return (
            full if "x" in whole else self.x,
            full if "z" in whole else self.zh,
            full if "y" in whole else self.y,
            full if "z" in whole else self.zl,
        )


def greet(place):
    barrier = pltpu.get_barrier_semaphore()
    for step in range(1, 16):
        pl.semaphore_signal(
            barrier, inc=1, device_id=(place.fsdp, (place.seq + step) % 16), device_id_type=MESH
        )
    for step in range(1, 4):
        pl.semaphore_signal(barrier, inc=1, device_id=place.moved("x", step)[1], device_id_type=MESH)
    other = place.x * 2 + 1 - place.zh
    for low in range(2):
        pl.semaphore_signal(
            barrier,
            inc=1,
            device_id=(other, place.y * 4 + low * 2 + place.core),
            device_id_type=MESH,
        )
    pl.semaphore_wait(barrier, 20)


class Gather:
    def __init__(self, place, part, order, ref, send, recv):
        self.place, self.part, self.order, self.ref = place, part, order, ref
        self.send, self.recv = send, recv
        self.copies = []

    def start(self, stage, source=None):
        here = self.place.block(self.order[:stage])
        block = self.ref.at[here]
        row = []
        for step in (1, 3, 2):
            copy = pltpu.make_async_remote_copy(
                src_ref=block if source is None else source,
                dst_ref=block,
                send_sem=self.send.at[self.part, stage, step - 1],
                recv_sem=self.recv.at[self.part, stage, step - 1],
                device_id=self.place.moved(self.order[stage], step)[1],
                device_id_type=MESH,
            )
            copy.start()
            row.append(copy)
        self.copies.append(row)

    def wait_recv(self, stage):
        for copy in self.copies[stage]:
            copy.wait_recv()

    def wait_send(self):
        for row in self.copies:
            for copy in row:
                copy.wait_send()


def lanes_of(rows):
    return lax.broadcasted_iota(jnp.int32, (rows, 128), 1)


def head_means(squares):
    left = lax.broadcasted_iota(jnp.int32, (128, 128), 0) // 64
    right = lax.broadcasted_iota(jnp.int32, (128, 128), 1) // 64
    mean = jnp.where(left == right, 1.0 / 64, 0.0).astype(F32)
    return lax.dot_general(
        squares, mean, (((1,), (0,)), ((), ())), precision=HIGH, preferred_element_type=F32
    )


def nt(left, right):
    return lax.dot_general(left, right, (((1,), (1,)), ((), ())), preferred_element_type=F32)


def nn(left, right):
    return lax.dot_general(left, right, (((1,), (0,)), ((), ())), preferred_element_type=F32)


def tn(left, right):
    return lax.dot_general(left, right, (((0,), (0,)), ((), ())), preferred_element_type=F32)


def turn(values, low_half):
    return jnp.where(low_half, pltpu.roll(values, 96, 1), pltpu.roll(values, 32, 1))


def forward_kernel(
    len_ref, x_ref, t_ref, w_ref, qg_ref, kg_ref, cos_ref, sin_ref,
    xp_ref, tp_ref, mixed_ref, h1_ref, gains_ref, qkv_ref, oh_ref, l_ref, ot_ref, h_ref, h2_ref,
    in0_ref, in1_ref, out_ref, gate_ref, up_ref, down_ref,
    wr_ref, ffb_ref, send_ref, kk_ref, v0_ref, v1_ref, ob_ref, part_ref, ps_ref, pr_ref,
    ag_send, ag_recv, ff_own, w_sem, x_send, x_recv, t_send, t_recv, t_own,
    q_send, q_recv, o_send, o_recv, p_send, p_recv,
):
    place = Place()
    core, chip = place.core, place.chip
    greet(place)
    sibling = place.sibling()

    def to_sibling(src, dst, send, recv):
        return pltpu.make_async_remote_copy(
            src_ref=src, dst_ref=dst, send_sem=send, recv_sem=recv, device_id=sibling, device_id_type=MESH
        )

    w_copy = to_sibling(w_ref.at[1 - core], wr_ref, w_sem.at[0], w_sem.at[1])
    w_copy.start()
    x_copies, t_copies, t_owns = [], [], []
    for seq in range(2):
        copy = to_sibling(x_ref.at[seq], xp_ref.at[seq, core], x_send.at[seq], x_recv.at[seq])
        copy.start()
        x_copies.append(copy)
    for seq in range(2):
        copy = to_sibling(t_ref.at[seq], tp_ref.at[seq, core], t_send.at[seq], t_recv.at[seq])
        copy.start()
        t_copies.append(copy)
        copy = pltpu.make_async_copy(t_ref.at[seq], tp_ref.at[seq, core], t_own.at[seq])
        copy.start()
        t_owns.append(copy)
    for seq in range(2):
        xp_ref[seq, core] = x_ref[seq]
    w_copy.wait_recv()

    refs = (in0_ref, in1_ref, out_ref, gate_ref, up_ref, down_ref)
    gathers = [Gather(place, i, ORDERS[i], refs[i], ag_send, ag_recv) for i in range(6)]
    own_copies = []
    first = jnp.where(core == 0, 1.0, 0.0).astype(F32)
    for i in range(6):
        lanes = pl.ds(STARTS[i], WIDTHS[i])
        mine = w_ref[core, :, lanes]
        theirs = wr_ref[:, lanes]
        low = jnp.where(first > 0.5, mine, theirs)
        high = jnp.where(first > 0.5, theirs, mine)
        both = jnp.concatenate([low, high], axis=0).astype(BF16)
        if i < 3:
            refs[i][place.x, place.zh, place.y, place.zl] = both
            gathers[i].start(0)
        else:
            ffb_ref[i - 3] = both
            copy = pltpu.make_async_copy(ffb_ref.at[i - 3], refs[i].at[place.block("")], ff_own.at[i - 3])
            copy.start()
            own_copies.append(copy)
    for i in range(3, 6):
        gathers[i].start(0, ffb_ref.at[i - 3])
    for i in range(3):
        gathers[i].wait_recv(0)
        gathers[i].start(1)
    for i in range(3):
        gathers[i].wait_recv(1)
        gathers[i].start(2)
    for i in range(3, 6):
        own_copies[i - 3].wait()
        gathers[i].wait_recv(0)
        gathers[i].start(1)
    for i in (2, 0, 1):
        gathers[i].wait_recv(2)
    for copy in x_copies:
        copy.wait_recv()

    columns = out_ref[:, :, :, :, :, pl.ds(512, 128)].reshape(1024, 128).astype(F32)
    gains_ref[...] = jnp.transpose(columns)[:8]
    for i in range(3, 6):
        gathers[i].wait_recv(1)
        gathers[i].start(2)

    def first_norm(step, carry):
        seq, half = step // 4, (step // 2) % 2
        rows = pl.ds((step % 2) * 64, 64)
        inputs = xp_ref[seq, half, rows, :].astype(F32)
        scale = lax.rsqrt(jnp.mean(inputs * inputs, axis=-1, keepdims=True) + EPS)
        h1_ref[pl.ds(step * 64, 64), :] = (inputs * scale * gains_ref[0:1, :]).astype(BF16)
        return carry

    lax.fori_loop(0, 8, first_norm, 0)

    low_half = lanes_of(256) % 64 < 32
    first_head = lanes_of(256) < 64

    def send_copy(kv, seq):
        target = (4 * core + kv) * 2 + seq
        slot = kv * 2 + seq
        return target, pltpu.make_async_remote_copy(
            src_ref=send_ref.at[slot],
            dst_ref=qkv_ref.at[chip],
            send_sem=q_send.at[slot],
            recv_sem=q_recv.at[chip],
            device_id=(place.fsdp, target),
            device_id_type=MESH,
        ), pltpu.make_async_copy(send_ref.at[slot], qkv_ref.at[chip], q_recv.at[chip])

    for kv in range(4):
        weights = (in0_ref, in1_ref)[kv // 2][:, :, :, :, :, pl.ds((kv % 2) * 256, 256)].reshape(1024, 256)

        def project(seq, carry, kv=kv, weights=weights):
            rows = pl.ds(seq * 256, 256)
            raw = nn(h1_ref[rows, :], weights)
            mixed_ref[kv, rows, :] = raw
            query, other = raw[:, :128], raw[:, 128:]
            query_norm = query * lax.rsqrt(head_means(query * query) + EPS) * qg_ref[...]
            other_norm = other * lax.rsqrt(head_means(other * other) + EPS) * kg_ref[...]
            query_rot = query_norm * cos_ref[...] + turn(query_norm, low_half) * sin_ref[...]
            other_rot = other_norm * cos_ref[...] + turn(other_norm, low_half) * sin_ref[...]
            slot = kv * 2 + seq
            send_ref[slot, :, 0:128] = query_rot.astype(BF16)
            send_ref[slot, :, 128:256] = jnp.where(first_head, other_rot, other).astype(BF16)
            target, remote, local = send_copy(kv, seq)

            @pl.when(target != place.seq)
            def _():
                remote.start()

            @pl.when(target == place.seq)
            def _():
                local.start()

            return carry

        lax.fori_loop(0, 2, project, 0)

    length = len_ref[core]
    factor = LOG2E / 8.0

    def out_copy(block):
        target = block * 2 + chip // 4
        return target, pltpu.make_async_remote_copy(
            src_ref=ob_ref.at[block],
            dst_ref=ot_ref.at[chip % 4, core],
            send_sem=o_send.at[block],
            recv_sem=o_recv.at[chip % 4, core],
            device_id=(place.fsdp, target),
            device_id_type=MESH,
        ), pltpu.make_async_copy(ob_ref.at[block], ot_ref.at[chip % 4, core], o_recv.at[chip % 4, core])

    def attend(block, carry):
        pltpu.make_async_copy(qkv_ref.at[block], qkv_ref.at[block], q_recv.at[block]).wait()
        rows = pl.ds(pl.multiple_of(block * 256, 256), 256)
        other = qkv_ref[block, :, 128:256].astype(F32)
        swapped = pltpu.roll(other, 64, 1)
        place_of = block * 256 + lax.broadcasted_iota(jnp.int32, (256, 128), 0)
        there = place_of < length
        kk_ref[rows, :] = jnp.where(first_head, other, swapped).astype(BF16)
        v0_ref[rows, :] = jnp.where(there, jnp.where(first_head, swapped, 1.0), 0.0).astype(BF16)
        v1_ref[rows, :] = jnp.where(there, jnp.where(first_head, 1.0, other), 0.0).astype(BF16)
        query = qkv_ref[block, :, 0:128]
        nothing = jnp.zeros_like(query)
        query0 = jnp.where(first_head, query, nothing)
        query1 = jnp.where(first_head, nothing, query)

        def step(key_block, sums, diagonal=False):
            keys = pl.ds(pl.multiple_of(key_block * 256, 256), 256)
            kk = kk_ref[keys, :]
            new = []
            for query_h, values, total in ((query0, v0_ref, sums[0]), (query1, v1_ref, sums[1])):
                weights = jnp.exp2(nt(query_h, kk) * factor)
                if diagonal:
                    row = lax.broadcasted_iota(jnp.int32, (256, 256), 0)
                    column = lax.broadcasted_iota(jnp.int32, (256, 256), 1)
                    weights = jnp.where(column <= row, weights, 0.0)
                new.append(total + nn(weights.astype(BF16), values[keys, :]))
            return tuple(new)

        zero = jnp.zeros((256, 128), F32)
        sums = lax.fori_loop(0, block, step, (zero, zero))
        sum0, sum1 = step(block, sums, True)
        total = jnp.where(first_head, pltpu.roll(sum0, 64, 1), pltpu.roll(sum1, 64, 1))
        mixed = jnp.where(first_head, sum0, sum1) / total
        oh_ref[rows, :] = mixed
        l_ref[rows, :] = total
        ob_ref[block] = mixed.astype(BF16)
        target, remote, local = out_copy(block)

        @pl.when(target != place.seq)
        def _():
            remote.start()

        @pl.when(target == place.seq)
        def _():
            local.start()

        return carry

    lax.fori_loop(0, 8, attend, 0)

    for kv in range(4):
        for seq in range(2):
            pltpu.make_async_copy(ot_ref.at[kv, seq], ot_ref.at[kv, seq], o_recv.at[kv, seq]).wait()
    attended = jnp.concatenate([ot_ref[kv].reshape(512, 128) for kv in range(4)], axis=1)
    p_copies = []
    for tile in range(4):
        weights = out_ref[tile, :, :, :, :, pl.ds(0, 512)].reshape(256, 512)
        part = nt(attended, weights)
        part_ref[tile] = part
        ps_ref[tile] = part.astype(BF16)
        copy = to_sibling(ps_ref.at[tile], pr_ref.at[tile], p_send.at[tile], p_recv.at[tile])
        copy.start()
        p_copies.append(copy)
    for copy in p_copies:
        copy.wait_recv()

    def second_norm(step, carry):
        seq, half = step // 8, (step // 4) % 2
        inputs = xp_ref[seq, half, pl.ds((step % 4) * 32, 32), :].astype(F32)
        rows = pl.ds(step * 32, 32)
        resid = jnp.concatenate(
            [part_ref[tile, rows, :] + pr_ref[tile, rows, :].astype(F32) for tile in range(4)], axis=1
        )
        resid = resid + inputs
        scale = lax.rsqrt(jnp.mean(resid * resid, axis=-1, keepdims=True) + EPS)
        h_ref[rows, :] = resid
        h2_ref[rows, :] = (resid * scale * gains_ref[1:2, :]).astype(BF16)
        return carry

    lax.fori_loop(0, 16, second_norm, 0)

    w_copy.wait_send()
    for copy in x_copies + p_copies:
        copy.wait_send()
    for copy in t_copies:
        copy.wait()
    for copy in t_owns:
        copy.wait()
    for slot in range(8):
        target, remote, _ = send_copy(slot // 2, slot % 2)

        @pl.when(target != place.seq)
        def _(remote=remote):
            remote.wait_send()

    for block in range(8):
        target, remote, _ = out_copy(block)

        @pl.when(target != place.seq)
        def _(remote=remote):
            remote.wait_send()

    for i in range(3, 6):
        gathers[i].wait_recv(2)
    for gather in gathers:
        gather.wait_send()


def forward(tokens, teacher, lengths, packed, query_gain, key_gain, cosine, sine):
    any_space = pl.BlockSpec(memory_space=pl.ANY)
    vmem = pl.BlockSpec(memory_space=pltpu.VMEM)
    smem = pl.BlockSpec(memory_space=pltpu.SMEM)

    def shape(dims, kind):
        return jax.ShapeDtypeStruct(dims, kind)

    dma = pltpu.SemaphoreType.DMA
    return pl.pallas_call(
        forward_kernel,
        out_shape=(
            shape((2, 2, 128, 1024), BF16),
            shape((2, 2, 128, 1024), BF16),
            shape((4, 512, 256), F32),
            shape((512, 1024), BF16),
            shape((8, 1024), F32),
            shape((8, 256, 256), BF16),
            shape((2048, 128), F32),
            shape((2048, 128), F32),
            shape((4, 2, 256, 128), BF16),
            shape((512, 1024), F32),
            shape((512, 1024), BF16),
        )
        + tuple(shape((4, 2, 4, 2, 16, n), BF16) for n in WIDTHS),
        in_specs=[smem, vmem, any_space, vmem, vmem, vmem, vmem, vmem],
        out_specs=(vmem, any_space) + (vmem,) * 9 + (vmem,) * 3 + (any_space,) * 3,
        scratch_shapes=[
            pltpu.VMEM((8, PACKED), F32),
            pltpu.VMEM((3, 16, 2304), BF16),
            pltpu.VMEM((8, 256, 256), BF16),
            pltpu.VMEM((2048, 128), BF16),
            pltpu.VMEM((2048, 128), BF16),
            pltpu.VMEM((2048, 128), BF16),
            pltpu.VMEM((8, 256, 128), BF16),
            pltpu.VMEM((4, 512, 256), F32),
            pltpu.VMEM((4, 512, 256), BF16),
            pltpu.VMEM((4, 512, 256), BF16),
            dma((6, 3, 3)), dma((6, 3, 3)), dma((3,)), dma((2,)),
            dma((2,)), dma((2,)), dma((2,)), dma((2,)), dma((2,)),
            dma((8,)), dma((8,)), dma((8,)), dma((4, 2)), dma((4,)), dma((4,)),
        ],
        name="forward_attention",
        compiler_params=pltpu.CompilerParams(
            collective_id=0, has_side_effects=True, vmem_limit_bytes=56 * 1024 * 1024
        ),
    )(lengths, tokens, teacher, packed, query_gain, key_gain, cosine, sine)


def pack_weights(attention_gain, input_weight, output_weight, feed_gain, gate_weight, up_weight, down_weight):
    rows = input_weight.shape[0]

    def halves(item):
        return jnp.moveaxis(item.reshape(rows, 2, -1), 1, 0)

    mixing = jnp.concatenate(
        [
            input_weight[:, :1024].reshape(rows, 8, 128),
            input_weight[:, 1024:1536].reshape(rows, 8, 64),
            input_weight[:, 1536:].reshape(rows, 8, 64),
        ],
        axis=-1,
    ).reshape(rows, 2048)
    gains = jnp.stack([attention_gain, feed_gain], axis=-1)
    gains = jnp.broadcast_to(jnp.pad(gains, ((0, 0), (0, 126)))[None], (2, rows, 128))
    return jnp.concatenate(
        [
            halves(mixing),
            halves(output_weight.T),
            gains,
            halves(gate_weight),
            halves(up_weight),
            halves(down_weight.T),
        ],
        axis=-1,
    ).astype(F32)


def rope_tables():
    positions = (lax.axis_index("seq") // 2) * 256 + jnp.arange(256, dtype=jnp.int32)
    freqs = THETA ** (-(2.0 * jnp.arange(32, dtype=F32)) / 64)
    angles = positions.astype(F32)[:, None] * freqs[None, :]
    cosine, sine = jnp.cos(angles), jnp.sin(angles)
    return (
        jnp.concatenate([cosine] * 4, axis=-1),
        jnp.concatenate([-sine, sine, -sine, sine], axis=-1),
    )
BACK_WIDTHS = (512, 640, 512, 2304, 2304, 2304)
BACK_STARTS = (0, 512, 1152, 1664, 3968, 6272)


def remaining(order, stage):
    sizes = (("x", 4), ("z", 2), ("y", 4), ("z", 2))
    return tuple(size for axis, size in sizes if axis not in order[:stage])


class Scatter:
    def __init__(self, place, part, order, sources, landed, send, recv):
        self.place, self.part, self.order = place, part, order
        self.sources, self.landed, self.send, self.recv = sources, landed, send, recv
        self.copies = []

    def index(self, stage, where):
        index = []
        for axis, value in zip("xzyz", where):
            if axis in self.order[:stage]:
                continue
            index.append(value if axis == self.order[stage] else slice(None))
        return tuple(index)

    def own(self, stage):
        place = self.place
        return self.index(stage, (place.x, place.zh, place.y, place.zl))

    def start(self, stage):
        row = []
        for step in (1, 3, 2):
            where, device = self.place.moved(self.order[stage], step)
            copy = pltpu.make_async_remote_copy(
                src_ref=self.sources[stage].at[self.index(stage, where)],
                dst_ref=self.landed[stage].at[step - 1],
                send_sem=self.send.at[self.part, stage, step - 1],
                recv_sem=self.recv.at[self.part, stage, step - 1],
                device_id=device,
                device_id_type=MESH,
            )
            copy.start()
            row.append(copy)
        self.copies.append(row)

    def add(self, stage, mine, target):
        for copy in self.copies[stage]:
            copy.wait_recv()
        landed = self.landed[stage]
        sizes = remaining(self.order, stage + 1)
        count = math.prod(sizes)

        def one(step, carry):
            index, rest = [], step
            for size in reversed(sizes):
                index.insert(0, rest % size)
                rest = rest // size
            index = tuple(index)
            total = mine[index].astype(F32)
            for other in range(3):
                total = total + landed[(other,) + index].astype(F32)
            target[index] = total.astype(target.dtype)
            return carry

        if count == 1:
            total = mine[...].astype(F32)
            for other in range(3):
                total = total + landed[other].astype(F32)
            target[...] = total.astype(target.dtype)
        else:
            lax.fori_loop(0, count, one, 0)

    def wait_send(self):
        for row in self.copies:
            for copy in row:
                copy.wait_send()


def backward_kernel(
    dhb_ref, dh_ref, x_ref, in0_ref, in1_ref, out_ref, qkv_ref, oh_ref, l_ref, ot_ref, mixed_ref, h1_ref,
    gains_ref, cos_ref, sin_ref, qg_ref, kg_ref, feed_ref, small_ref, gate_ref, up_ref, down_ref,
    tok_ref, wg_ref, total_ref,
    dsend_ref, do_ref, rhs_ref, lse_ref, dd_ref, dq_ref, gsend_ref, gr_ref, dqkv_ref,
    dps_ref, dpr_ref, dpo_ref, fin_ref, pair_ref, ring_ref, smalls_ref,
    win0, win1, wout, own3, own4, own5,
    land00, land01, land02, land10, land11, land12, land20, land21, land22,
    land30, land31, land32, land40, land41, land42, land50, land51, land52,
    mid01, mid02, mid11, mid12, mid21, mid22, mid32, mid42, mid52,
    rs_send, rs_recv, own_sem, do_send, do_recv, g_send, g_recv, dp_send, dp_recv,
    fin_sem, pair_sem, ring_send, ring_recv,
):
    place = Place()
    core, chip = place.core, place.chip
    greet(place)
    sibling = place.sibling()
    lands = (
        (land00, land01, land02), (land10, land11, land12), (land20, land21, land22),
        (land30, land31, land32), (land40, land41, land42), (land50, land51, land52),
    )
    sources = (
        (win0, mid01, mid02), (win1, mid11, mid12), (wout, mid21, mid22),
        (gate_ref, own3, mid32), (up_ref, own4, mid42), (down_ref, own5, mid52),
    )
    scatters = [Scatter(place, i, ORDERS[i], sources[i], lands[i], rs_send, rs_recv) for i in range(6)]
    own_copies = []
    for i in range(3, 6):
        scatters[i].start(0)
        copy = pltpu.make_async_copy(
            sources[i][0].at[scatters[i].own(0)], sources[i][1], own_sem.at[i - 3]
        )
        copy.start()
        own_copies.append(copy)

    def do_copy(kv, seq):
        target = (4 * core + kv) * 2 + seq
        slot = kv * 2 + seq
        return target, pltpu.make_async_remote_copy(
            src_ref=dsend_ref.at[slot],
            dst_ref=do_ref.at[chip],
            send_sem=do_send.at[slot],
            recv_sem=do_recv.at[chip],
            device_id=(place.fsdp, target),
            device_id_type=MESH,
        ), pltpu.make_async_copy(dsend_ref.at[slot], do_ref.at[chip], do_recv.at[chip])

    def start_either(target, remote, local):
        @pl.when(target != place.seq)
        def _():
            remote.start()

        @pl.when(target == place.seq)
        def _():
            local.start()

    for kv in range(4):
        weights = out_ref[:, :, :, :, :, pl.ds(kv * 128, 128)].reshape(1024, 128)
        grad = nn(dhb_ref[...], weights).astype(BF16)
        for seq in range(2):
            dsend_ref[kv * 2 + seq] = grad[seq * 256 : seq * 256 + 256]
            start_either(*do_copy(kv, seq))

    for kv in range(4):
        grad = tn(dhb_ref[...], ot_ref[kv].reshape(512, 128))
        wout[:, :, :, :, :, pl.ds(kv * 128, 128)] = grad.astype(BF16).reshape(4, 2, 4, 2, 16, 128)
    scatters[2].start(0)

    first_head = lanes_of(256) < 64
    low_half = lanes_of(256) % 64 < 32
    head_row = lax.broadcasted_iota(jnp.int32, (8, 128), 0)
    head_lane = lax.broadcasted_iota(jnp.int32, (8, 128), 1)
    pick = jnp.where(head_lane == head_row * 64, 1.0, 0.0).astype(F32)
    spread = jnp.where(head_lane // 64 == head_row, 1.0, 0.0).astype(F32)
    factor = LOG2E / 8.0

    def nt_high(left, right):
        return lax.dot_general(
            left, right, (((1,), (1,)), ((), ())), precision=HIGH, preferred_element_type=F32
        )

    def prepare(block, carry):
        rows = pl.ds(pl.multiple_of(block * 256, 256), 256)
        pltpu.make_async_copy(do_ref.at[block], do_ref.at[block], do_recv.at[block]).wait()
        query = qkv_ref[block, :, 0:128].astype(F32)
        grad = do_ref[block].astype(F32)
        zero = jnp.zeros_like(query)
        lse_ref[block] = jnp.log2(jnp.maximum(nt_high(pick, l_ref[rows, :]), 1e-30))
        dd_ref[block] = nt_high(spread, grad * oh_ref[rows, :])
        rhs_ref[block, pl.ds(0, 256), :] = jnp.where(first_head, query, zero).astype(BF16)
        rhs_ref[block, pl.ds(256, 256), :] = jnp.where(first_head, pltpu.roll(query, 64, 1), zero).astype(BF16)
        rhs_ref[block, pl.ds(512, 256), :] = jnp.where(first_head, zero, pltpu.roll(grad, 64, 1)).astype(BF16)
        rhs_ref[block, pl.ds(768, 256), :] = jnp.where(first_head, zero, grad).astype(BF16)
        dq_ref[block] = zero
        return carry

    lax.fori_loop(0, 8, prepare, 0)

    def g_copy(block):
        target = block * 2 + chip // 4
        return target, pltpu.make_async_remote_copy(
            src_ref=gsend_ref.at[block],
            dst_ref=gr_ref.at[chip % 4, core],
            send_sem=g_send.at[block],
            recv_sem=g_recv.at[chip % 4, core],
            device_id=(place.fsdp, target),
            device_id_type=MESH,
        ), pltpu.make_async_copy(gsend_ref.at[block], gr_ref.at[chip % 4, core], g_recv.at[chip % 4, core])

    def attend_back(key_block, carry):
        other = qkv_ref[key_block, :, 128:256].astype(F32)
        swapped = pltpu.roll(other, 64, 1)
        zero = jnp.zeros_like(other)
        keys0 = jnp.where(first_head, other, zero).astype(BF16)
        keys1 = jnp.where(first_head, zero, swapped).astype(BF16)
        values0 = jnp.where(first_head, swapped, zero).astype(BF16)
        values1 = jnp.where(first_head, zero, other).astype(BF16)
        keys = jnp.concatenate([keys0, keys1], axis=0)

        def step(block, total, diagonal=False):
            query = qkv_ref[block, :, 0:128]
            grad = do_ref[block]
            chances, grads = [], []
            for head, keys_h, values_h in ((0, keys0, values0), (1, keys1, values1)):
                chance = jnp.exp2(nt(keys_h, query) * factor - lse_ref[block, head : head + 1, :])
                if diagonal:
                    row = lax.broadcasted_iota(jnp.int32, (256, 256), 0)
                    column = lax.broadcasted_iota(jnp.int32, (256, 256), 1)
                    chance = jnp.where(row <= column, chance, 0.0)
                inner = nt(values_h, grad) - dd_ref[block, head : head + 1, :]
                chances.append(chance.astype(BF16))
                grads.append((chance * inner).astype(BF16))
            left = jnp.concatenate(grads + chances, axis=1)
            dq_ref[block] = dq_ref[block] + tn(jnp.concatenate(grads, axis=0), keys)
            return total + nn(left, rhs_ref[block])

        total = step(key_block, zero, True)
        total = lax.fori_loop(key_block + 1, 8, step, total)
        gsend_ref[key_block, :, 0:128] = (dq_ref[key_block] * 0.125).astype(BF16)
        gsend_ref[key_block, :, 128:256] = jnp.where(first_head, total * 0.125, total).astype(BF16)
        start_either(*g_copy(key_block))
        return carry

    lax.fori_loop(0, 8, attend_back, 0)

    for i in range(3, 6):
        own_copies[i - 3].wait()
        scatters[i].add(0, sources[i][1], sources[i][1])
        scatters[i].start(1)
    scatters[2].add(0, wout.at[scatters[2].own(0)], mid21)
    scatters[2].start(1)

    smalls_ref[...] = small_ref[...]
    for kv in range(4):
        for seq in range(2):
            pltpu.make_async_copy(gr_ref.at[kv, seq], gr_ref.at[kv, seq], g_recv.at[kv, seq]).wait()

        def back(seq, carry, kv=kv):
            rows = pl.ds(pl.multiple_of(seq * 256, 256), 256)
            raws = mixed_ref[kv, rows, :]
            grads = gr_ref[kv, seq].astype(F32)
            results = []
            for part, gain_ref in ((0, qg_ref), (1, kg_ref)):
                lanes = slice(part * 128, part * 128 + 128)
                raw, grad = raws[:, lanes], grads[:, lanes]
                scale = lax.rsqrt(head_means(raw * raw) + EPS)
                grad_norm = grad * cos_ref[...] + turn(grad * sin_ref[...], low_half)
                gain_sum = jnp.sum(grad_norm * raw * scale, axis=0, keepdims=True)
                smalls_ref[part : part + 1, :] = smalls_ref[part : part + 1, :] + gain_sum
                inner = grad_norm * gain_ref[...]
                result = scale * inner - raw * (scale * scale * scale) * head_means(inner * raw)
                if part == 1:
                    result = jnp.where(first_head, result, grad)
                results.append(result)
            dqkv_ref[kv, rows, :] = jnp.concatenate(results, axis=1).astype(BF16)
            return carry

        lax.fori_loop(0, 2, back, 0)

    def exchange(step, carry):
        rows = pl.ds(pl.multiple_of(step * 128, 128), 128)
        total = jnp.zeros((128, 1024), F32)
        for kv in range(4):
            weights = (in0_ref, in1_ref)[kv // 2][:, :, :, :, :, pl.ds((kv % 2) * 256, 256)].reshape(1024, 256)
            total = total + nt(dqkv_ref[kv, rows, :], weights)
        dpo_ref[step % 2, step // 2] = total
        dps_ref[step % 2, step // 2] = total.astype(BF16)
        return carry

    lax.fori_loop(0, 4, exchange, 0)
    dp_copy = pltpu.make_async_remote_copy(
        src_ref=dps_ref.at[1 - core],
        dst_ref=dpr_ref,
        send_sem=dp_send.at[0],
        recv_sem=dp_recv.at[0],
        device_id=sibling,
        device_id_type=MESH,
    )
    dp_copy.start()

    for i in range(2, 6):
        scatters[i].add(1, sources[i][1].at[scatters[i].own(1)], sources[i][2])
        scatters[i].start(2)

    for kv in range(4):
        grad = tn(h1_ref[...], dqkv_ref[kv]).astype(BF16).reshape(4, 2, 4, 2, 16, 256)
        (win0, win1)[kv // 2][:, :, :, :, :, pl.ds((kv % 2) * 256, 256)] = grad
    scatters[0].start(0)

    dp_copy.wait_recv()

    def last(step, carry):
        seq, rows = step // 2, pl.ds((step % 2) * 64, 64)
        inputs = x_ref[seq, rows, :].astype(F32)
        scale = lax.rsqrt(jnp.mean(inputs * inputs, axis=-1, keepdims=True) + EPS)
        grad = dpo_ref[core, seq, rows, :] + dpr_ref[seq, rows, :].astype(F32)
        inner = grad * gains_ref[0:1, :]
        mean = jnp.mean(inner * inputs, axis=-1, keepdims=True)
        tok_ref[seq, rows, :] = dh_ref[seq, rows, :] + scale * inner - inputs * (scale * scale * scale) * mean
        return carry + jnp.sum(grad * inputs * scale, axis=0, keepdims=True)

    gain_grad = lax.fori_loop(0, 4, last, jnp.zeros((1, 1024), F32))
    both = jnp.concatenate([gain_grad, feed_ref[...], jnp.zeros((126, 1024), F32)], axis=0)
    win1[:, :, :, :, :, pl.ds(512, 128)] = jnp.transpose(both).astype(BF16).reshape(4, 2, 4, 2, 16, 128)
    scatters[1].start(0)

    pair_ref[core] = smalls_ref[...]
    pair_copy = pltpu.make_async_remote_copy(
        src_ref=smalls_ref,
        dst_ref=pair_ref.at[core],
        send_sem=pair_sem.at[0],
        recv_sem=pair_sem.at[1],
        device_id=sibling,
        device_id_type=MESH,
    )
    pair_copy.start()

    def ring_start(stage, value):
        axis = "xyz"[stage]
        here = {"x": place.x, "y": place.y, "z": place.z}[axis]
        ring_ref[stage, here] = value
        copies = []
        for step in (1, 3, 2):
            copy = pltpu.make_async_remote_copy(
                src_ref=ring_ref.at[stage, here],
                dst_ref=ring_ref.at[stage, here],
                send_sem=ring_send.at[stage, step - 1],
                recv_sem=ring_recv.at[stage, step - 1],
                device_id=place.moved(axis, step)[1],
                device_id_type=MESH,
            )
            copy.start()
            copies.append(copy)
        return copies

    def ring_sum(stage, copies):
        for copy in copies:
            copy.wait_recv()
        total = ring_ref[stage, 0]
        for other in range(1, 4):
            total = total + ring_ref[stage, other]
        return total

    pair_copy.wait_recv()
    rings = [ring_start(0, pair_ref[0] + pair_ref[1])]
    for i in range(2):
        scatters[i].add(0, sources[i][0].at[scatters[i].own(0)], sources[i][1])
        scatters[i].start(1)
    rings.append(ring_start(1, ring_sum(0, rings[0])))

    def finish(i):
        final = fin_ref.at[:, :, pl.ds(BACK_STARTS[i], BACK_WIDTHS[i])]
        for copy in scatters[i].copies[2]:
            copy.wait_recv()
        total = sources[i][2][scatters[i].own(2)].astype(F32)
        for other in range(3):
            total = total + lands[i][2][other].astype(F32)
        final[...] = total.reshape(2, 8, BACK_WIDTHS[i])

    for i in range(2, 6):
        finish(i)
    for i in range(2):
        scatters[i].add(1, sources[i][1].at[scatters[i].own(1)], sources[i][2])
        scatters[i].start(2)
    rings.append(ring_start(2, ring_sum(1, rings[1])))
    for i in range(2):
        finish(i)
    fin_copy = pltpu.make_async_remote_copy(
        src_ref=fin_ref.at[1 - core],
        dst_ref=wg_ref.at[core],
        send_sem=fin_sem.at[0],
        recv_sem=fin_sem.at[1],
        device_id=sibling,
        device_id_type=MESH,
    )
    fin_copy.start()
    wg_ref[core] = fin_ref[core]
    total_ref[...] = ring_sum(2, rings[2])
    fin_copy.wait()
    dp_copy.wait_send()
    pair_copy.wait_send()
    for copies in rings:
        for copy in copies:
            copy.wait_send()
    for slot in range(8):
        target, remote, _ = do_copy(slot // 2, slot % 2)

        @pl.when(target != place.seq)
        def _(remote=remote):
            remote.wait_send()

    for block in range(8):
        target, remote, _ = g_copy(block)

        @pl.when(target != place.seq)
        def _(remote=remote):
            remote.wait_send()

    for scatter in scatters:
        scatter.wait_send()


def backward(*operands):
    any_space = pl.BlockSpec(memory_space=pl.ANY)
    vmem = pl.BlockSpec(memory_space=pltpu.VMEM)

    def shape(dims, kind):
        return jax.ShapeDtypeStruct(dims, kind)

    dma = pltpu.SemaphoreType.DMA
    whole = (4, 2, 4, 2)
    lands, mids = [], []
    for order, n in zip(ORDERS, BACK_WIDTHS):
        for stage in range(3):
            lands.append(pltpu.VMEM((3,) + remaining(order, stage + 1) + (16, n), BF16))
    for i, (order, n) in enumerate(zip(ORDERS, BACK_WIDTHS)):
        for stage in (1, 2) if i < 3 else (2,):
            mids.append(pltpu.VMEM(remaining(order, stage) + (16, n), BF16))
    return pl.pallas_call(
        backward_kernel,
        out_shape=(shape((2, 128, 1024), F32), shape((2, 8, PACKED), F32), shape((8, 128), F32)),
        in_specs=[vmem] * 19 + [any_space] * 3,
        out_specs=(vmem,) * 3,
        scratch_shapes=[
            pltpu.VMEM((8, 256, 128), BF16),
            pltpu.VMEM((8, 256, 128), BF16),
            pltpu.VMEM((8, 1024, 128), BF16),
            pltpu.VMEM((8, 8, 256), F32),
            pltpu.VMEM((8, 8, 256), F32),
            pltpu.VMEM((8, 256, 128), F32),
            pltpu.VMEM((8, 256, 256), BF16),
            pltpu.VMEM((4, 2, 256, 256), BF16),
            pltpu.VMEM((4, 512, 256), BF16),
            pltpu.VMEM((2, 2, 128, 1024), BF16),
            pltpu.VMEM((2, 128, 1024), BF16),
            pltpu.VMEM((2, 2, 128, 1024), F32),
            pltpu.VMEM((2, 8, PACKED), F32),
            pltpu.VMEM((2, 8, 128), F32),
            pltpu.VMEM((3, 4, 8, 128), F32),
            pltpu.VMEM((8, 128), F32),
            pltpu.VMEM(whole + (16, 512), BF16),
            pltpu.VMEM(whole + (16, 640), BF16),
            pltpu.VMEM(whole + (16, 512), BF16),
        ]
        + [pltpu.VMEM(remaining(ORDERS[i], 1) + (16, 2304), BF16) for i in range(3, 6)]
        + lands
        + mids
        + [
            dma((6, 3, 3)), dma((6, 3, 3)), dma((3,)), dma((8,)), dma((8,)), dma((8,)), dma((4, 2)),
            dma((1,)), dma((1,)), dma((2,)), dma((2,)), dma((3, 3)), dma((3, 3)),
        ],
        name="backward_attention",
        compiler_params=pltpu.CompilerParams(
            collective_id=1, has_side_effects=True, vmem_limit_bytes=60 * 1024 * 1024
        ),
    )(*operands)


def unpack_grads(packed):
    rows = packed.shape[1]

    def joined(i, width):
        start = BACK_STARTS[i]
        return jnp.moveaxis(packed[:, :, start : start + width], 0, 1)

    mixing = jnp.concatenate([joined(0, 512), joined(1, 512)], axis=-1).reshape(rows, 8, 256)
    input_grad = jnp.concatenate(
        [
            mixing[:, :, :128].reshape(rows, 1024),
            mixing[:, :, 128:192].reshape(rows, 512),
            mixing[:, :, 192:].reshape(rows, 512),
        ],
        axis=-1,
    )
    output_grad = joined(2, 512).reshape(rows, 1024).T
    gate_grad, up_grad, down_grad = (joined(i, 2304).reshape(rows, 4608) for i in range(3, 6))
    first = BACK_STARTS[1] + 512
    attention_gain = packed[0, :, first] + packed[1, :, first]
    feed_gain = packed[0, :, first + 1]
    return attention_gain, input_grad, output_grad, feed_gain, gate_grad, up_grad, down_grad.T


def paired(part):
    pairs = [(i, i ^ 1) for i in range(16)]
    return part + lax.ppermute(part.astype(BF16), "seq", pairs).astype(F32)


def body(
    tokens, teacher, lengths, attention_gain, input_weight, query_gain, key_gain,
    output_weight, feed_gain, gate_weight, up_weight, down_weight,
):
    packed = pack_weights(
        attention_gain, input_weight, output_weight, feed_gain, gate_weight, up_weight, down_weight
    )
    cosine, sine = rope_tables()
    query_row = jnp.concatenate([query_gain, query_gain]).astype(F32)[None]
    key_row = jnp.concatenate([key_gain, key_gain]).astype(F32)[None]
    (
        _, teacher_pair, mixed, h1, gains, qkv, attended_heads, totals, attended, h, h2,
        in0, in1, out, gate_full, up_full, down_full,
    ) = forward(tokens, teacher, lengths, packed, query_row, key_row, cosine, sine)
    core, chip = lax.axis_index("seq") % 2, lax.axis_index("seq") // 2
    gate_w, up_w, down_w = (item.reshape(1024, 2304) for item in (gate_full, up_full, down_full))
    gate, up = nn(h2, gate_w), nn(h2, up_w)
    sigma = jax.nn.sigmoid(gate)
    silu = gate * sigma
    act = (silu * up).astype(BF16)
    final = h + paired(nt(act, down_w))
    slots = chip * 256 + jnp.arange(256, dtype=jnp.int32)
    valid = (slots[None, :] < lengths[:, None]).astype(F32).reshape(512, 1)
    diff = (final - teacher_pair.reshape(512, 1024).astype(F32)) * valid

    def mine(item):
        return lax.dynamic_index_in_dim(item.reshape(2, 2, 128, -1), core, 1, False)

    block_out = mine(final).astype(BF16)
    squares = jnp.sum(jnp.square(mine(diff)))
    counted = jnp.sum(mine(valid))
    low = diff.astype(BF16)
    grad_act = nn(low, down_w)
    down_grad = tn(low, act).astype(BF16)
    grad_gate = (grad_act * up * sigma * (1.0 + gate * (1.0 - sigma))).astype(BF16)
    grad_up = (grad_act * silu).astype(BF16)
    gate_grad = tn(h2, grad_gate).astype(BF16)
    up_grad = tn(h2, grad_up).astype(BF16)
    grad_feed = paired(nt(grad_gate, gate_w) + nt(grad_up, up_w))
    scale = lax.rsqrt(jnp.mean(h * h, axis=-1, keepdims=True) + EPS)
    feed_sum = jnp.sum(grad_feed * h * scale, axis=0, keepdims=True)
    inner = grad_feed * gains[1:2]
    grad_h = diff + scale * inner - h * (scale * scale * scale) * jnp.mean(inner * h, axis=-1, keepdims=True)
    small = jnp.zeros((8, 128), F32).at[2, 0].set(squares).at[3, 0].set(counted)
    blocks = (4, 2, 4, 2, 16, 2304)
    token_grads, weight_grads, sums = backward(
        grad_h.astype(BF16), mine(grad_h), tokens, in0, in1, out, qkv, attended_heads, totals, attended, mixed, h1,
        gains, cosine, sine, query_row, key_row, feed_sum, small,
        gate_grad.reshape(blocks), up_grad.reshape(blocks), down_grad.reshape(blocks),
    )
    loss = sums[2, 0] / (sums[3, 0] * 1024)
    attention_gain_grad, input_grad, output_grad, feed_gain_grad, gate_g, up_g, down_g = unpack_grads(weight_grads)
    return (
        block_out, loss, token_grads, attention_gain_grad, input_grad,
        sums[0, :64] + sums[0, 64:], sums[1, :64],
        output_grad, feed_gain_grad, gate_g, up_g, down_g,
    )


def solution(mesh):
    tokens, split = P("fsdp", "seq", None), P(("fsdp", "seq"))
    rows, columns = P(("fsdp", "seq"), None), P(None, ("fsdp", "seq"))
    return jax.shard_map(
        body,
        mesh=mesh,
        in_specs=(
            tokens, tokens, P("fsdp"), split, rows, P(), P(), columns, split, rows, rows, columns,
        ),
        out_specs=(
            tokens, P(), tokens, split, rows, P(), P(), columns, split, rows, rows, columns,
        ),
        check_vma=False,
    )
```

```python
import functools
import math

import jax
import jax.numpy as jnp
import numpy as np
from jax import lax
from jax.experimental import pallas as pl
from jax.experimental.pallas import tpu as pltpu
from jax.sharding import PartitionSpec as P

EPS = 1e-05
THETA = 1000000.0
MESH = pl.DeviceIdType.MESH
F32 = jnp.float32
BF16 = jnp.bfloat16
LOG2E = 1.4426950408889634
HIGH = lax.Precision.HIGHEST
BLOCKS = (4, 2, 4, 2, 16)
PACKED = 8576
IN_AT, OUT_AT, UP_AT, GATE_AT, DOWN_AT = 0, 1152, 1664, 3968, 6272


class Place:
    def __init__(self):
        self.fsdp = lax.axis_index("fsdp")
        self.seq = lax.axis_index("seq")
        self.x = self.fsdp // 2
        self.zh = self.fsdp % 2
        self.y = self.seq // 4
        self.zl = (self.seq // 2) % 2
        self.core = self.seq % 2
        self.chip = self.seq // 2
        self.z = self.zh * 2 + self.zl
        self.here = (self.x, self.zh, self.y, self.zl)

    def sibling(self):
        return (self.fsdp, self.seq + 1 - 2 * self.core)

    def moved(self, axis, step):
        x, y, z = self.x, self.y, self.z
        if axis == "x":
            x = (x + step) % 4
        elif axis == "y":
            y = (y + step) % 4
        else:
            z = (z + step) % 4
        zh, zl = z // 2, z % 2
        return (x, zh, y, zl), (x * 2 + zh, y * 4 + zl * 2 + self.core)


def greet(place):
    barrier = pltpu.get_barrier_semaphore()
    for step in range(1, 16):
        pl.semaphore_signal(
            barrier, inc=1, device_id=(place.fsdp, (place.seq + step) % 16), device_id_type=MESH
        )
    for step in range(1, 4):
        pl.semaphore_signal(barrier, inc=1, device_id=place.moved("x", step)[1], device_id_type=MESH)
    other = place.x * 2 + 1 - place.zh
    for low in range(2):
        pl.semaphore_signal(
            barrier,
            inc=1,
            device_id=(other, place.y * 4 + low * 2 + place.core),
            device_id_type=MESH,
        )


def greeted():
    pl.semaphore_wait(pltpu.get_barrier_semaphore(), 20)


def axes_index(order, stage, here, where, cut=None, half=0):
    index = []
    for axis, mine, other in zip("xzyz", here, where):
        if axis in order[:stage]:
            index.append(mine)
        elif axis == order[stage]:
            index.append(other)
        else:
            index.append(pl.ds(2 * half, 2) if axis == cut else slice(None))
    return tuple(index)


def rest(order, stage, cut=None):
    sizes = (("x", 4), ("z", 2), ("y", 4), ("z", 2))
    return tuple(2 if axis == cut else size for axis, size in sizes if axis not in order[: stage + 1])


def accumulate(sizes, target, others):
    def one(step, carry):
        index, left = [], step
        for size in reversed(sizes):
            index.insert(0, left % size)
            left = left // size
        index = tuple(index)
        total = target[index].astype(F32)
        for other in others:
            total = total + other[index].astype(F32)
        target[index] = total.astype(BF16)
        return carry

    lax.fori_loop(0, math.prod(sizes), one, 0)


class Scatter:
    def __init__(self, place, part, order, ref, lanes, lands, sems, wide=None):
        self.place, self.part, self.order, self.ref, self.lanes = place, part, order, ref, lanes
        self.lands = lands
        self.send, self.recv, self.free = sems
        self.cut = "y" if order[0] == "x" else "x"
        self.wide = wide
        self.copies = {}

    def at(self, stage, where, half=None):
        cut = None if half is None else self.cut
        index = axes_index(self.order, stage, self.place.here, where, cut, half)
        return self.ref.at[index + (slice(None), self.lanes)]

    def step(self, stage, step, half=None):
        return self.at(stage, self.place.moved(self.order[stage], step)[0], half)

    def copy(self, stage, slot, step, src, dst):
        copy = pltpu.make_async_remote_copy(
            src_ref=src,
            dst_ref=dst,
            send_sem=self.send.at[self.part, stage, slot],
            recv_sem=self.recv.at[self.part, stage, slot],
            device_id=self.place.moved(self.order[stage], step)[1],
            device_id_type=MESH,
        )
        copy.start()
        self.copies[stage, slot] = copy

    def direct(self, stage):
        for slot, step in enumerate((1, 3, 2)):
            self.copy(stage, slot, step, self.step(stage, step), self.lands[stage].at[slot])

    def add(self, stage):
        for slot in range(3):
            self.copies[stage, slot].wait_recv()
        others = [self.lands[stage].at[slot] for slot in range(3)]
        accumulate(rest(self.order, stage), self.at(stage, self.place.here), others)

    def far(self):
        for slot, step in enumerate((1, 3)):
            self.copy(0, slot, step, self.step(0, 2, slot), self.lands[0].at[slot])

    def credit(self):
        for slot, step in enumerate((3, 1)):
            pl.semaphore_signal(
                self.free.at[self.part, slot],
                inc=1,
                device_id=self.place.moved(self.order[0], step)[1],
                device_id_type=MESH,
            )

    def near(self):
        for slot, step in enumerate((1, 3)):
            self.copies[0, slot].wait_recv()
            sizes = rest(self.order, 0, self.cut)
            accumulate(sizes, self.step(0, step, slot), [self.lands[0].at[slot]])
            pl.semaphore_wait(self.free.at[self.part, slot], 1)
            self.copy(0, 2 + slot, step, self.step(0, step), self.wide.at[slot])

    def own(self):
        for slot in range(2):
            self.copies[0, 2 + slot].wait_recv()
        accumulate(rest(self.order, 0), self.at(0, self.place.here), [self.wide.at[0], self.wide.at[1]])

    def final(self):
        total = self.at(2, self.place.here)[...].astype(F32)
        for slot in range(3):
            self.copies[2, slot].wait_recv()
            total = total + self.lands[2][slot].astype(F32)
        return total

    def sent(self):
        for copy in self.copies.values():
            copy.wait_send()


class Gather:
    def __init__(self, place, part, order, ref, lanes, send, recv):
        self.place, self.part, self.order, self.ref, self.lanes = place, part, order, ref, lanes
        self.send, self.recv = send, recv
        self.copies = {}

    def at(self, stage, where, half=None):
        index = []
        cut = "y" if self.order[2] == "x" else "x"
        for axis, value in zip("xzyz", where):
            if axis in self.order[:stage]:
                index.append(slice(None) if half is None or axis != cut else pl.ds(2 * half, 2))
            else:
                index.append(value)
        return self.ref.at[tuple(index) + (slice(None), self.lanes)]

    def copy(self, stage, slot, step, block):
        copy = pltpu.make_async_remote_copy(
            src_ref=block,
            dst_ref=block,
            send_sem=self.send.at[self.part, stage, slot],
            recv_sem=self.recv.at[self.part, stage, slot],
            device_id=self.place.moved(self.order[stage], step)[1],
            device_id_type=MESH,
        )
        copy.start()
        self.copies[stage, slot] = copy

    def direct(self, stage):
        for slot, step in enumerate((1, 3, 2)):
            self.copy(stage, slot, step, self.at(stage, self.place.here))

    def near(self):
        for slot, step in enumerate((1, 3)):
            self.copy(2, slot, step, self.at(2, self.place.here))

    def far(self):
        for slot, step in enumerate((1, 3)):
            self.copies[2, slot].wait_recv()
            self.copy(2, 2 + slot, step, self.at(2, self.place.moved(self.order[2], 4 - step)[0], slot))

    def arrived(self, stage):
        for (of, slot), copy in self.copies.items():
            if of == stage and not (stage == 2 and slot < 2 and (2, 3) in self.copies):
                copy.wait_recv()

    def sent(self):
        for copy in self.copies.values():
            copy.wait_send()


def lanes_of(rows):
    return lax.broadcasted_iota(jnp.int32, (rows, 128), 1)


def head_means(squares):
    left = lax.broadcasted_iota(jnp.int32, (128, 128), 0) // 64
    right = lax.broadcasted_iota(jnp.int32, (128, 128), 1) // 64
    mean = jnp.where(left == right, 1.0 / 64, 0.0).astype(F32)
    return lax.dot_general(
        squares, mean, (((1,), (0,)), ((), ())), precision=HIGH, preferred_element_type=F32
    )


def nt(left, right):
    return lax.dot_general(left, right, (((1,), (1,)), ((), ())), preferred_element_type=F32)


def nn(left, right):
    return lax.dot_general(left, right, (((1,), (0,)), ((), ())), preferred_element_type=F32)


def tn(left, right):
    return lax.dot_general(left, right, (((0,), (0,)), ((), ())), preferred_element_type=F32)


def turn(values, low_half):
    return jnp.where(low_half, pltpu.roll(values, 96, 1), pltpu.roll(values, 32, 1))


def columns(ref, start, width):
    return ref[:, :, :, :, :, pl.ds(start, width)].reshape(1024, width)


LOW, REST = 1024, 1280
GATHERED = (
    ("in", 0, 384, "xyz"), ("in", 384, 384, "yzx"), ("in", 768, 384, "zxy"), ("out", 0, 512, "yzx"),
    ("up", 0, 1152, "yzx"), ("up", 1152, 1152, "zyx"), ("gate", 0, LOW, "zxy"), ("gate", LOW, REST, "yxz"),
    ("down", 0, LOW, "xzy"), ("down", LOW, REST, "xyz"),
)
SCATTERED = (
    ("in", 0, 384, "xyz"), ("in", 384, 384, "yzx"), ("in", 768, 384, "zxy"), ("out", 0, 512, "xyz"),
    ("up", 0, 2304, "xyz"), ("gate", 0, LOW, "yzx"), ("gate", LOW, REST, "zxy"),
    ("down", 0, LOW, "yzx"), ("down", LOW, REST, "zxy"),
)
WIDE = 4
STARTS = {"in": 0, "out": 1152, "up": 1664, "gate": 3968, "down": 6272}


def step_kernel(
    len_ref, x_ref, t_ref, iw_ref, ow_ref, gw_ref, uw_ref, dw_ref, cols_ref, rows_ref, freq_ref,
    bo_ref, tok_ref, giw_ref, gow_ref, ggw_ref, guw_ref, gdw_ref, gcols_ref, total_ref,
    win_ref, wout_ref, up_ref, gate_ref, down_ref, w_ref, wr_ref, xp_ref, tp_ref, send_ref, qkv_ref,
    kk_ref, v0_ref, v1_ref, v2_ref, ob_ref, ot_ref, do_ref, oh_ref, lse_ref, dd_ref, mixed_ref, h1_ref, gains_ref,
    cos_ref, sin_ref, part_ref, part2_ref, ps_ref, pr0_ref, pr1_ref, h_ref, h2_ref, low_ref,
    acty_ref, actz_ref, dgy_ref, dgz_ref, du_ref, gr_ref, smalls_ref, pair_ref, ring_ref, *others,
):
    lands = [others[3 * i : 3 * i + 3] for i in range(9)]
    (
        ag_send, ag_recv, rs_send, rs_recv, free_sem, w_sem, x_send, x_recv, x_own, q_send, q_recv, o_send, o_recv,
        p_send, p_recv, do_send, do_recv, g_send, g_recv, fin_sem, pair_sem, ring_send, ring_recv,
    ) = others[27:]
    place = Place()
    core, chip = place.core, place.chip
    greet(place)
    sibling = place.sibling()
    gathered = {"in": win_ref, "out": wout_ref, "up": up_ref, "gate": gate_ref, "down": down_ref}

    low_lanes = lanes_of(8) < 64
    for half in range(2):
        for kv in range(4):
            head = half * 4 + kv
            at = kv * 256
            w_ref[half, :, pl.ds(at, 128)] = iw_ref[:, pl.ds(head * 128, 128)].astype(F32)
            keys = iw_ref[:, pl.ds(1024 + head // 2 * 128, 128)].astype(F32)
            values = iw_ref[:, pl.ds(1536 + head // 2 * 128, 128)].astype(F32)
            if head % 2 == 0:
                both = jnp.where(low_lanes, keys, pltpu.roll(values, 64, 1))
            else:
                both = jnp.where(low_lanes, pltpu.roll(keys, 64, 1), values)
            w_ref[half, :, pl.ds(at + 128, 128)] = both
        w_ref[half, :, pl.ds(1024, 128)] = cols_ref[...]
        w_ref[half, :, pl.ds(STARTS["out"], 512)] = ow_ref[:, pl.ds(half * 512, 512)].astype(F32)
        for name, ref in (("up", uw_ref), ("gate", gw_ref), ("down", dw_ref)):
            w_ref[half, :, pl.ds(STARTS[name], 2304)] = ref[:, pl.ds(half * 2304, 2304)].astype(F32)
    greeted()

    def to_sibling(src, dst, send, recv):
        copy = pltpu.make_async_remote_copy(
            src_ref=src, dst_ref=dst, send_sem=send, recv_sem=recv, device_id=sibling, device_id_type=MESH
        )
        copy.start()
        return copy

    w_copy = to_sibling(w_ref.at[1 - core], wr_ref, w_sem.at[0], w_sem.at[1])
    pair_copies, own_copies = [], []
    for i, (src, dst) in enumerate(((x_ref, xp_ref), (t_ref, tp_ref))):
        for seq in range(2):
            n = 2 * i + seq
            pair_copies.append(to_sibling(src.at[seq], dst.at[seq, core], x_send.at[n], x_recv.at[n]))
            copy = pltpu.make_async_copy(src.at[seq], dst.at[seq, core], x_own.at[n])
            copy.start()
            own_copies.append(copy)

    gathers = [
        Gather(place, i, order, gathered[name], pl.ds(start, width), ag_send, ag_recv)
        for i, (name, start, width, order) in enumerate(GATHERED)
    ]
    mixing, output, ups, gates, downs = gathers[:3], gathers[3], gathers[4:6], gathers[6:8], gathers[8:]
    early = ups + gates

    w_copy.wait_recv()
    first = jnp.where(core == 0, 1.0, 0.0).astype(F32)
    for name, width in (("in", 1152), ("out", 512), ("up", 2304), ("gate", 2304), ("down", 2304)):
        lanes = pl.ds(STARTS[name], width)
        mine = w_ref[core, :, lanes]
        theirs = wr_ref[:, lanes]
        above = jnp.where(first > 0.5, mine, theirs)
        below = jnp.where(first > 0.5, theirs, mine)
        gathered[name][place.here] = jnp.concatenate([above, below], axis=0).astype(BF16)
        if name == "in":
            for item in mixing:
                item.direct(0)
    for item in mixing:
        item.arrived(0)
        item.direct(1)
    for item in early:
        item.direct(0)

    slots = chip * 256 + lax.broadcasted_iota(jnp.int32, (256, 128), 0)
    angles = slots.astype(F32) * freq_ref[...]
    cos_ref[...] = jnp.cos(angles)
    sine = jnp.sin(angles)
    low_half = lanes_of(256) % 64 < 32
    first_head = lanes_of(256) < 64
    sin_ref[...] = jnp.where(low_half, -sine, sine)

    for item in mixing:
        item.arrived(1)
        item.direct(2)
    output.direct(0)
    for item in early:
        item.arrived(0)
        item.direct(1)
    for n in range(2):
        pair_copies[n].wait_recv()
        own_copies[n].wait()
    for item in mixing:
        item.arrived(2)

    gains_ref[...] = jnp.transpose(columns(win_ref, 1024, 128).astype(F32))[:8]

    def first_norm(step, carry):
        seq, half = step // 4, (step // 2) % 2
        rows = pl.ds((step % 2) * 64, 64)
        inputs = xp_ref[seq, half, rows, :].astype(F32)
        scale = lax.rsqrt(jnp.mean(inputs * inputs, axis=-1, keepdims=True) + EPS)
        h1_ref[pl.ds(step * 64, 64), :] = (inputs * scale * gains_ref[0:1, :]).astype(BF16)
        return carry

    lax.fori_loop(0, 8, first_norm, 0)

    def to_heads(slot, src_ref, dst_ref, send, recv):
        target = (4 * core + slot // 2) * 2 + slot % 2
        return target, pltpu.make_async_remote_copy(
            src_ref=src_ref.at[slot],
            dst_ref=dst_ref.at[chip],
            send_sem=send.at[slot],
            recv_sem=recv.at[chip],
            device_id=(place.fsdp, target),
            device_id_type=MESH,
        ), pltpu.make_async_copy(src_ref.at[slot], dst_ref.at[chip], recv.at[chip])

    def to_tokens(block, src_ref, dst_ref, send, recv):
        target = block * 2 + chip // 4
        return target, pltpu.make_async_remote_copy(
            src_ref=src_ref.at[block],
            dst_ref=dst_ref.at[chip % 4, core],
            send_sem=send.at[block],
            recv_sem=recv.at[chip % 4, core],
            device_id=(place.fsdp, target),
            device_id_type=MESH,
        ), pltpu.make_async_copy(src_ref.at[block], dst_ref.at[chip % 4, core], recv.at[chip % 4, core])

    def start_either(target, remote, local):
        @pl.when(target != place.seq)
        def _():
            remote.start()

        @pl.when(target == place.seq)
        def _():
            local.start()

    def sent_either(target, remote, local):
        @pl.when(target != place.seq)
        def _():
            remote.wait_send()

    q_refs = (send_ref, qkv_ref, q_send, q_recv)
    o_refs = (ob_ref, ot_ref, o_send, o_recv)
    do_refs = (ob_ref, do_ref, do_send, do_recv)
    g_refs = (send_ref, gr_ref, g_send, g_recv)

    for kv in range(4):
        weights = columns(win_ref, kv * 256, 256)

        def project(seq, carry, kv=kv, weights=weights):
            rows = pl.ds(pl.multiple_of(seq * 256, 256), 256)
            raw = nn(h1_ref[rows, :], weights)
            mixed_ref[kv, rows, :] = raw
            query, other = raw[:, :128], raw[:, 128:]
            query_norm = query * lax.rsqrt(head_means(query * query) + EPS) * rows_ref[0:1, :]
            other_norm = other * lax.rsqrt(head_means(other * other) + EPS) * rows_ref[1:2, :]
            query_rot = query_norm * cos_ref[...] + turn(query_norm, low_half) * sin_ref[...]
            other_rot = other_norm * cos_ref[...] + turn(other_norm, low_half) * sin_ref[...]
            slot = kv * 2 + seq
            send_ref[slot, :, 0:128] = query_rot.astype(BF16)
            send_ref[slot, :, 128:256] = jnp.where(first_head, other_rot, other).astype(BF16)
            start_either(*to_heads(slot, *q_refs))
            return carry

        lax.fori_loop(0, 2, project, 0)

    for item in early:
        item.arrived(1)
        item.near()
    output.arrived(0)
    output.direct(1)
    for item in downs:
        item.direct(0)

    length = len_ref[core]
    factor = LOG2E / 8.0
    head_row = lax.broadcasted_iota(jnp.int32, (8, 128), 0)
    head_lane = lax.broadcasted_iota(jnp.int32, (8, 128), 1)
    pick = jnp.where(head_lane == head_row * 64, 1.0, 0.0).astype(F32)
    spread = jnp.where(head_lane // 64 == head_row, 1.0, 0.0).astype(F32)

    def nt_high(left, right):
        return lax.dot_general(
            left, right, (((1,), (1,)), ((), ())), precision=HIGH, preferred_element_type=F32
        )

    def attend(block, carry):
        pltpu.make_async_copy(qkv_ref.at[block], qkv_ref.at[block], q_recv.at[block]).wait()
        rows = pl.ds(pl.multiple_of(block * 256, 256), 256)
        other = qkv_ref[block, :, 128:256].astype(F32)
        swapped = pltpu.roll(other, 64, 1)
        place_of = block * 256 + lax.broadcasted_iota(jnp.int32, (256, 128), 0)
        there = place_of < length
        kk_ref[block] = jnp.where(first_head, other, swapped).astype(BF16)
        v0_ref[block] = jnp.where(there, jnp.where(first_head, swapped, 1.0), 0.0).astype(BF16)
        v1_ref[block] = jnp.where(there, jnp.where(first_head, 1.0, other), 0.0).astype(BF16)
        query = qkv_ref[block, :, 0:128]
        nothing = jnp.zeros_like(query)
        query0 = jnp.where(first_head, query, nothing)
        query1 = jnp.where(first_head, nothing, query)

        def step(key_block, sums, diagonal=False):
            kk = kk_ref[key_block]
            new = []
            for query_h, values, total in ((query0, v0_ref, sums[0]), (query1, v1_ref, sums[1])):
                weights = jnp.exp2(nt(query_h, kk) * factor)
                if diagonal:
                    row = lax.broadcasted_iota(jnp.int32, (256, 256), 0)
                    column = lax.broadcasted_iota(jnp.int32, (256, 256), 1)
                    weights = jnp.where(column <= row, weights, 0.0)
                new.append(total + nn(weights.astype(BF16), values[key_block]))
            return tuple(new)

        zero = jnp.zeros((256, 128), F32)
        sums = lax.fori_loop(0, block, step, (zero, zero))
        sum0, sum1 = step(block, sums, True)
        total = jnp.where(first_head, pltpu.roll(sum0, 64, 1), pltpu.roll(sum1, 64, 1))
        mixed = jnp.where(first_head, sum0, sum1) / total
        oh_ref[block] = mixed
        lse_ref[block] = jnp.log2(jnp.maximum(nt_high(pick, total), 1e-30))
        ob_ref[block] = mixed.astype(BF16)
        start_either(*to_tokens(block, *o_refs))

        return carry

    lax.fori_loop(0, 8, attend, 0)

    for item in gates + ups:
        item.far()
    output.arrived(1)
    output.direct(2)
    for item in downs:
        item.arrived(0)
        item.direct(1)
    output.arrived(2)
    for kv in range(4):
        for seq in range(2):
            pltpu.make_async_copy(ot_ref.at[kv, seq], ot_ref.at[kv, seq], o_recv.at[kv, seq]).wait()
    attended = jnp.concatenate([ot_ref[kv].reshape(512, 128) for kv in range(4)], axis=1)

    def send_part(tile, landing, number):
        return pltpu.make_async_remote_copy(
            src_ref=ps_ref.at[tile],
            dst_ref=landing.at[tile],
            send_sem=p_send.at[number, tile],
            recv_sem=p_recv.at[number, tile],
            device_id=sibling,
            device_id_type=MESH,
        )

    def share(tile, part, keep, landing, number):
        keep[tile] = part
        ps_ref[tile] = part.astype(BF16)
        send_part(tile, landing, number).start()

    def shared(landing, number):
        for tile in range(4):
            send_part(tile, landing, number).wait()

    for tile in range(4):
        share(tile, nt(attended, wout_ref[tile].reshape(256, 512)), part_ref, pr0_ref, 0)
    for item in downs:
        item.arrived(1)
        item.near()
    shared(pr0_ref, 0)

    def paired(rows, keep, landing):
        return jnp.concatenate(
            [keep[tile, rows, :] + landing[tile, rows, :].astype(F32) for tile in range(4)], axis=1
        )

    def second_norm(step, carry):
        seq, half = step // 8, (step // 4) % 2
        inputs = xp_ref[seq, half, pl.ds((step % 4) * 32, 32), :].astype(F32)
        rows = pl.ds(step * 32, 32)
        resid = paired(rows, part_ref, pr0_ref) + inputs
        scale = lax.rsqrt(jnp.mean(resid * resid, axis=-1, keepdims=True) + EPS)
        h_ref[rows, :] = resid
        h2_ref[rows, :] = (resid * scale * gains_ref[1:2, :]).astype(BF16)
        return carry

    lax.fori_loop(0, 16, second_norm, 0)

    for item in ups + gates:
        item.arrived(2)

    def tiles(function):
        def low_tile(tile, carry):
            at = pl.multiple_of(tile * 256, 256)
            return function(at, acty_ref, dgy_ref, at, (2, 4, 2, 2, 16, 256), (slice(None),) * 5)

        def rest_tile(tile, carry):
            at = pl.multiple_of(tile * 256, 256)
            at_all = pl.multiple_of(tile * 256 + LOW, 256)
            return function(at_all, actz_ref, dgz_ref, at, (2, 4, 4, 16, 256), (slice(None),) * 4)

        lax.fori_loop(0, LOW // 256, low_tile, 0)
        lax.fori_loop(0, REST // 256, rest_tile, 0)

    whole = (slice(None),) * 5
    du_shape = (2, 2, 4, 2, 16, 256)

    def feed(at, act, dg, at_part, dims, full):
        lanes, lanes_part = pl.ds(at, 256), pl.ds(at_part, 256)
        up = nn(h2_ref[...], columns(up_ref, at, 256))
        gate = nn(h2_ref[...], columns(gate_ref, at, 256))
        sigma = jax.nn.sigmoid(gate)
        silu = gate * sigma
        act[full + (lanes_part,)] = (silu * up).astype(BF16).reshape(dims)
        dg[full + (lanes_part,)] = (up * sigma * (1.0 + gate * (1.0 - sigma))).astype(BF16).reshape(dims)
        du_ref[whole + (lanes,)] = silu.astype(BF16).reshape(du_shape)
        return 0

    tiles(feed)
    for item in downs:
        item.far()
    for item in downs:
        item.arrived(2)

    def lower(tile, carry):
        weights = down_ref[tile].reshape(256, 2304)
        part = nt(acty_ref[...].reshape(512, LOW), weights[:, :LOW])
        part = part + nt(actz_ref[...].reshape(512, REST), weights[:, LOW:])
        share(tile, part, part_ref, pr1_ref, 1)
        return carry

    lax.fori_loop(0, 4, lower, 0)
    for n in range(2, 4):
        pair_copies[n].wait_recv()
        own_copies[n].wait()
    shared(pr1_ref, 1)

    def errors(step, carry):
        squares, counted = carry
        seq, half, at = step // 8, (step // 4) % 2, pl.ds((step % 4) * 32, 32)
        rows = pl.ds(step * 32, 32)
        final = h_ref[rows, :] + paired(rows, part_ref, pr1_ref)
        slot = chip * 256 + (step % 8) * 32 + lax.broadcasted_iota(jnp.int32, (32, 1024), 0)
        valid = jnp.where(slot < len_ref[seq], 1.0, 0.0).astype(F32)
        diff = (final - tp_ref[seq, half, at, :].astype(F32)) * valid
        low_ref[rows, :] = diff.astype(BF16)

        @pl.when(half == core)
        def _():
            bo_ref[seq, at, :] = final.astype(BF16)

        mine = jnp.where(half == core, 1.0, 0.0)
        for tile in range(4):
            part_ref[tile, rows, :] = diff[:, tile * 256 : tile * 256 + 256]
        squares = squares + mine * jnp.sum(diff * diff, axis=0, keepdims=True)
        counted = counted + mine * jnp.sum(valid[:, :128], axis=0, keepdims=True)
        return squares, counted

    squares, counted = lax.fori_loop(
        0, 16, errors, (jnp.zeros((1, 1024), F32), jnp.zeros((1, 128), F32))
    )
    folded = squares[:, 0:128]
    for tile in range(1, 8):
        folded = folded + squares[:, tile * 128 : tile * 128 + 128]
    smalls_ref[...] = jnp.concatenate(
        [jnp.zeros((2, 128), F32), folded, counted, jnp.zeros((4, 128), F32)], axis=0
    )
    w_copy.wait_send()
    for item in gathers:
        item.sent()

    wides = {4: du_ref, 5: dgy_ref, 6: dgz_ref, 7: acty_ref, 8: actz_ref}
    scatters = [
        Scatter(
            place, i, order, gathered[name], pl.ds(start, width), lands[i], (rs_send, rs_recv, free_sem), wides.get(i)
        )
        for i, (name, start, width, order) in enumerate(SCATTERED)
    ]
    mix_s, out_s, up_s, gate_s, down_s = scatters[:3], scatters[3], scatters[4], scatters[5:7], scatters[7:]

    def raise_back(at, act, dg, at_part, dims, full):
        lanes, lanes_part = pl.ds(at, 256), pl.ds(at_part, 256)
        grad_act = nn(low_ref[...], columns(down_ref, at, 256))
        dg_at, du_at = full + (lanes_part,), whole + (lanes,)
        dg[dg_at] = (grad_act * dg[dg_at].reshape(512, 256).astype(F32)).astype(BF16).reshape(dims)
        du_ref[du_at] = (grad_act * du_ref[du_at].reshape(512, 256).astype(F32)).astype(BF16).reshape(du_shape)
        grad = tn(low_ref[...], act[full + (lanes_part,)].reshape(512, 256))
        down_ref[whole + (lanes,)] = grad.astype(BF16).reshape(BLOCKS + (256,))
        return 0

    tiles(raise_back)
    for item in down_s:
        item.credit()
        item.far()

    def feed_back(tile, carry):
        weights = gate_ref[tile].reshape(256, 2304)
        part = nt(dgy_ref[...].reshape(512, LOW), weights[:, :LOW])
        part = part + nt(dgz_ref[...].reshape(512, REST), weights[:, LOW:])
        part = part + nt(du_ref[...].reshape(512, 2304), up_ref[tile].reshape(256, 2304))
        share(tile, part, part2_ref, pr0_ref, 2)
        return carry

    lax.fori_loop(0, 4, feed_back, 0)
    for item in down_s:
        item.near()

    def up_grads(tile, carry):
        lanes = pl.ds(pl.multiple_of(tile * 256, 256), 256)
        grad = tn(h2_ref[...], du_ref[whole + (lanes,)].reshape(512, 256))
        up_ref[whole + (lanes,)] = grad.astype(BF16).reshape(BLOCKS + (256,))
        return carry

    lax.fori_loop(0, 9, up_grads, 0)
    up_s.credit()
    up_s.far()
    shared(pr0_ref, 2)

    def second_back(step, carry):
        seq, half, at = step // 8, (step // 4) % 2, pl.ds((step % 4) * 32, 32)
        rows = pl.ds(step * 32, 32)
        grad = paired(rows, part2_ref, pr0_ref)
        diff = jnp.concatenate([part_ref[tile, rows, :] for tile in range(4)], axis=1)
        resid = h_ref[rows, :]
        scale = lax.rsqrt(jnp.mean(resid * resid, axis=-1, keepdims=True) + EPS)
        inner = grad * gains_ref[1:2, :]
        mean = jnp.mean(inner * resid, axis=-1, keepdims=True)
        result = diff + scale * inner - resid * (scale * scale * scale) * mean
        low_ref[rows, :] = result.astype(BF16)

        @pl.when(half == core)
        def _():
            tok_ref[seq, at, :] = result

        return carry + jnp.sum(grad * resid * scale, axis=0, keepdims=True)

    feed_sum = lax.fori_loop(0, 16, second_back, jnp.zeros((1, 1024), F32))

    for slot in range(8):
        sent_either(*to_heads(slot, *q_refs))
    for block in range(8):
        sent_either(*to_tokens(block, *o_refs))
    for kv in range(4):
        grad = nn(low_ref[...], columns(wout_ref, kv * 128, 128)).astype(BF16)
        for seq in range(2):
            ob_ref[kv * 2 + seq] = grad[seq * 256 : seq * 256 + 256]
            start_either(*to_heads(kv * 2 + seq, *do_refs))
    for kv in range(4):
        grad = tn(low_ref[...], ot_ref[kv].reshape(512, 128))
        wout_ref[whole + (pl.ds(kv * 128, 128),)] = grad.astype(BF16).reshape(BLOCKS + (128,))
    out_s.direct(0)

    def gate_grads(at, act, dg, at_part, dims, full):
        grad = tn(h2_ref[...], dg[full + (pl.ds(at_part, 256),)].reshape(512, 256))
        gate_ref[whole + (pl.ds(at, 256),)] = grad.astype(BF16).reshape(BLOCKS + (256,))
        return 0

    tiles(gate_grads)
    for item in gate_s:
        item.credit()
        item.far()
    up_s.near()

    rhs = (kk_ref, v0_ref, v1_ref, v2_ref)

    def prepare(block, carry):
        pltpu.make_async_copy(do_ref.at[block], do_ref.at[block], do_recv.at[block]).wait()
        query = qkv_ref[block, :, 0:128].astype(F32)
        grad = do_ref[block].astype(F32)
        zero = jnp.zeros_like(query)
        dd_ref[block] = nt_high(spread, grad * oh_ref[block])
        kk_ref[block] = jnp.where(first_head, query, zero).astype(BF16)
        v0_ref[block] = jnp.where(first_head, pltpu.roll(query, 64, 1), zero).astype(BF16)
        v1_ref[block] = jnp.where(first_head, zero, pltpu.roll(grad, 64, 1)).astype(BF16)
        v2_ref[block] = jnp.where(first_head, zero, grad).astype(BF16)
        oh_ref[block] = zero
        return carry

    lax.fori_loop(0, 8, prepare, 0)

    def attend_back(key_block, carry):
        other = qkv_ref[key_block, :, 128:256].astype(F32)
        swapped = pltpu.roll(other, 64, 1)
        zero = jnp.zeros_like(other)
        keys0 = jnp.where(first_head, other, zero).astype(BF16)
        keys1 = jnp.where(first_head, zero, swapped).astype(BF16)
        values0 = jnp.where(first_head, swapped, zero).astype(BF16)
        values1 = jnp.where(first_head, zero, other).astype(BF16)
        keys = jnp.concatenate([keys0, keys1], axis=0)

        def step(block, total, diagonal=False):
            query = qkv_ref[block, :, 0:128]
            grad = do_ref[block]
            chances, grads = [], []
            for head, keys_h, values_h in ((0, keys0, values0), (1, keys1, values1)):
                chance = jnp.exp2(nt(keys_h, query) * factor - lse_ref[block, head : head + 1, :])
                if diagonal:
                    row = lax.broadcasted_iota(jnp.int32, (256, 256), 0)
                    column = lax.broadcasted_iota(jnp.int32, (256, 256), 1)
                    chance = jnp.where(row <= column, chance, 0.0)
                inner = nt(values_h, grad) - dd_ref[block, head : head + 1, :]
                chances.append(chance.astype(BF16))
                grads.append((chance * inner).astype(BF16))
            left = jnp.concatenate(grads + chances, axis=1)
            right = jnp.concatenate([ref[block] for ref in rhs], axis=0)
            oh_ref[block] = oh_ref[block] + tn(jnp.concatenate(grads, axis=0), keys)
            return total + nn(left, right)

        total = step(key_block, zero, True)
        total = lax.fori_loop(key_block + 1, 8, step, total)
        send_ref[key_block, :, 0:128] = (oh_ref[key_block] * 0.125).astype(BF16)
        send_ref[key_block, :, 128:256] = jnp.where(first_head, total * 0.125, total).astype(BF16)
        start_either(*to_tokens(key_block, *g_refs))
        return carry

    lax.fori_loop(0, 8, attend_back, 0)

    for item in gate_s:
        item.near()
    for item in down_s:
        item.own()
        item.direct(1)
    out_s.add(0)
    out_s.direct(1)

    for kv in range(4):
        for seq in range(2):
            pltpu.make_async_copy(gr_ref.at[kv, seq], gr_ref.at[kv, seq], g_recv.at[kv, seq]).wait()

        def back(seq, carry, kv=kv):
            rows = pl.ds(pl.multiple_of(seq * 256, 256), 256)
            raws = mixed_ref[kv, rows, :]
            grads = gr_ref[kv, seq].astype(F32)
            results = []
            for part in range(2):
                lanes = slice(part * 128, part * 128 + 128)
                raw, grad = raws[:, lanes], grads[:, lanes]
                scale = lax.rsqrt(head_means(raw * raw) + EPS)
                grad_norm = grad * cos_ref[...] + turn(grad * sin_ref[...], low_half)
                gain_sum = jnp.sum(grad_norm * raw * scale, axis=0, keepdims=True)
                smalls_ref[part : part + 1, :] = smalls_ref[part : part + 1, :] + gain_sum
                inner = grad_norm * rows_ref[part : part + 1, :]
                result = scale * inner - raw * (scale * scale * scale) * head_means(inner * raw)
                if part == 1:
                    result = jnp.where(first_head, result, grad)
                results.append(result)
            h2_ref[rows, pl.ds(kv * 256, 256)] = jnp.concatenate(results, axis=1).astype(BF16)
            return carry

        lax.fori_loop(0, 2, back, 0)

    def mix_back(tile, carry):
        weights = win_ref[tile, :, :, :, :, pl.ds(0, 1024)].reshape(256, 1024)
        share(tile, nt(h2_ref[...], weights), part2_ref, pr1_ref, 3)
        return carry

    lax.fori_loop(0, 4, mix_back, 0)

    def mix_grads(kv, carry):
        at = pl.multiple_of(kv * 256, 256)
        grad = tn(h1_ref[...], h2_ref[:, pl.ds(at, 256)])
        win_ref[whole + (pl.ds(at, 256),)] = grad.astype(BF16).reshape(BLOCKS + (256,))
        return carry

    lax.fori_loop(0, 4, mix_grads, 0)
    mix_s[0].direct(0)
    mix_s[1].direct(0)
    shared(pr1_ref, 3)

    def last(step, carry):
        seq, at = step // 4, (step % 4) * 32
        rows = pl.ds(seq * 256 + core * 128 + at, 32)
        at = pl.ds(at, 32)
        inputs = xp_ref[seq, core, at, :].astype(F32)
        scale = lax.rsqrt(jnp.mean(inputs * inputs, axis=-1, keepdims=True) + EPS)
        grad = paired(rows, part2_ref, pr1_ref)
        inner = grad * gains_ref[0:1, :]
        mean = jnp.mean(inner * inputs, axis=-1, keepdims=True)
        tok_ref[seq, at, :] = tok_ref[seq, at, :] + scale * inner - inputs * (scale * scale * scale) * mean
        return carry + jnp.sum(grad * inputs * scale, axis=0, keepdims=True)

    gain_grad = lax.fori_loop(0, 8, last, jnp.zeros((1, 1024), F32))
    both = jnp.concatenate([gain_grad, feed_sum, jnp.zeros((126, 1024), F32)], axis=0)
    win_ref[whole + (pl.ds(1024, 128),)] = jnp.transpose(both).astype(BF16).reshape(BLOCKS + (128,))
    mix_s[2].direct(0)

    pair_ref[core] = smalls_ref[...]
    pair_copy = to_sibling(smalls_ref, pair_ref.at[core], pair_sem.at[0], pair_sem.at[1])

    def ring_start(stage, value):
        axis = "xyz"[stage]
        here = {"x": place.x, "y": place.y, "z": place.z}[axis]
        ring_ref[stage, here] = value
        copies = []
        for step in (1, 3, 2):
            copy = pltpu.make_async_remote_copy(
                src_ref=ring_ref.at[stage, here],
                dst_ref=ring_ref.at[stage, here],
                send_sem=ring_send.at[stage, step - 1],
                recv_sem=ring_recv.at[stage, step - 1],
                device_id=place.moved(axis, step)[1],
                device_id_type=MESH,
            )
            copy.start()
            copies.append(copy)
        return copies

    def ring_sum(stage, copies):
        for copy in copies:
            copy.wait_recv()
        total = ring_ref[stage, 0]
        for other in range(1, 4):
            total = total + ring_ref[stage, other]
        return total

    pair_copy.wait_recv()
    rings = [ring_start(0, pair_ref[0] + pair_ref[1])]

    up_s.own()
    up_s.direct(1)
    for item in gate_s:
        item.own()
        item.direct(1)
    for item in [out_s] + down_s:
        item.add(1)
        item.direct(2)
    for item in mix_s:
        item.add(0)
        item.direct(1)
    rings.append(ring_start(1, ring_sum(0, rings[0])))
    for item in [up_s] + gate_s:
        item.add(1)
        item.direct(2)
    for item in mix_s:
        item.add(1)
        item.direct(2)
    rings.append(ring_start(2, ring_sum(1, rings[1])))

    for i, (name, start, width, _) in reversed(list(enumerate(SCATTERED))):
        w_ref[:, :, pl.ds(STARTS[name] + start, width)] = scatters[i].final().reshape(2, 8, width)
    fin_copy = to_sibling(w_ref.at[1 - core], wr_ref, fin_sem.at[0], fin_sem.at[1])

    sums = ring_sum(2, rings[2])
    query_sum, key_sum, loss_sum, count = sums[0:1], sums[1:2], sums[2:3], sums[3:4]
    loss = jnp.sum(loss_sum, axis=1, keepdims=True) / (count * 1024.0)
    total_ref[...] = jnp.concatenate(
        [query_sum + pltpu.roll(query_sum, 64, 1), key_sum, loss, jnp.zeros((5, 128), F32)], axis=0
    )

    fin_copy.wait_recv()
    first = jnp.where(core == 0, 1.0, 0.0).astype(F32)

    def half_of(half, at, width):
        mine, theirs = w_ref[core, :, pl.ds(at, width)], wr_ref[:, pl.ds(at, width)]
        return jnp.where(first > 0.5, mine, theirs) if half == 0 else jnp.where(first > 0.5, theirs, mine)

    for half in range(2):
        gow_ref[:, pl.ds(half * 512, 512)] = half_of(half, STARTS["out"], 512)
        for name, ref in (("up", guw_ref), ("gate", ggw_ref), ("down", gdw_ref)):
            ref[:, pl.ds(half * 2304, 2304)] = half_of(half, STARTS[name], 2304)
        pairs = [half_of(half, kv * 256, 256) for kv in range(4)]
        for kv in range(4):
            giw_ref[:, pl.ds((half * 4 + kv) * 128, 128)] = pairs[kv][:, :128]
        for pair in range(2):
            even, odd = pairs[2 * pair][:, 128:], pairs[2 * pair + 1][:, 128:]
            at = (half * 2 + pair) * 128
            giw_ref[:, pl.ds(1024 + at, 128)] = jnp.where(low_lanes, even, pltpu.roll(odd, 64, 1))
            giw_ref[:, pl.ds(1536 + at, 128)] = jnp.where(low_lanes, pltpu.roll(even, 64, 1), odd)
    cols0, cols1 = w_ref[core, :, pl.ds(1024, 128)], wr_ref[:, pl.ds(1024, 128)]
    gcols_ref[...] = jnp.where(lanes_of(8) == 0, cols0 + cols1, cols0)

    for copy in [fin_copy, pair_copy] + pair_copies:
        copy.wait_send()
    for copies in rings:
        for copy in copies:
            copy.wait_send()
    for slot in range(8):
        sent_either(*to_heads(slot, *do_refs))
        sent_either(*to_tokens(slot, *g_refs))
    for item in scatters:
        item.sent()


def step_call(*operands):
    any_space = pl.BlockSpec(memory_space=pl.ANY)
    vmem = pl.BlockSpec(memory_space=pltpu.VMEM)
    smem = pl.BlockSpec(memory_space=pltpu.SMEM)

    def shape(dims, kind=F32):
        return jax.ShapeDtypeStruct(dims, kind)

    def room(dims, kind=BF16):
        return pltpu.VMEM(dims, kind)

    dma = pltpu.SemaphoreType.DMA
    lands = []
    for i, (_, _, n, order) in enumerate(SCATTERED):
        cut = "y" if order[0] == "x" else "x"
        if i < WIDE:
            lands.append(room((3,) + rest(order, 0) + (16, n)))
        else:
            lands.append(room((2,) + rest(order, 0, cut) + (16, n)))
        lands += [room((3,) + rest(order, 1) + (16, n)), room((3, 16, n))]
    heads, tokens = (8, 256, 128), (2, 2, 128, 1024)
    return pl.pallas_call(
        step_kernel,
        out_shape=(
            shape((2, 128, 1024), BF16), shape((2, 128, 1024)), shape((8, 2048)), shape((8, 1024)),
            shape((8, 4608)), shape((8, 4608)), shape((8, 4608)), shape((8, 128)), shape((8, 128)),
        ),
        in_specs=[smem, any_space, any_space] + [vmem] * 8,
        out_specs=(vmem,) * 9,
        scratch_shapes=[
            room(BLOCKS + (1152,)), room(BLOCKS + (512,)),
            room(BLOCKS + (2304,)), room(BLOCKS + (2304,)), room(BLOCKS + (2304,)),
            room((2, 8, PACKED), F32), room((8, PACKED), F32), room(tokens), room(tokens),
            room((8, 256, 256)), room((8, 256, 256)),
            room(heads), room(heads), room(heads), room(heads), room(heads), room((4, 2, 256, 128)), room(heads),
            room(heads, F32), room((8, 8, 256), F32), room((8, 8, 256), F32),
            room((4, 512, 256), F32), room((512, 1024)), room((8, 1024), F32), room((256, 128), F32), room((256, 128), F32),
            room((4, 512, 256), F32), room((4, 512, 256), F32), room((4, 512, 256)),
            room((4, 512, 256)), room((4, 512, 256)),
            room((512, 1024), F32), room((512, 1024)), room((512, 1024)),
            room((2, 4, 2, 2, 16, LOW)), room((2, 4, 4, 16, REST)),
            room((2, 4, 2, 2, 16, LOW)), room((2, 4, 4, 16, REST)), room((2, 2, 4, 2, 16, 2304)),
            room((4, 2, 256, 256)), room((8, 128), F32), room((2, 8, 128), F32), room((3, 4, 8, 128), F32),
        ]
        + lands
        + [
            dma((10, 3, 4)), dma((10, 3, 4)), dma((9, 3, 4)), dma((9, 3, 4)), pltpu.SemaphoreType.REGULAR((9, 2)),
            dma((2,)), dma((4,)), dma((4,)), dma((4,)), dma((8,)), dma((8,)), dma((8,)), dma((4, 2)),
            dma((4, 4)), dma((4, 4)), dma((8,)), dma((8,)), dma((8,)), dma((4, 2)),
            dma((2,)), dma((2,)), dma((3, 3)), dma((3, 3)),
        ],
        name="whole_step",
        compiler_params=pltpu.CompilerParams(
            collective_id=0, has_side_effects=True, vmem_limit_bytes=64 * 1024 * 1024 - 65536
        ),
    )(*operands)


def body(
    tokens, teacher, lengths, attention_gain, input_weight, query_gain, key_gain,
    output_weight, feed_gain, gate_weight, up_weight, down_weight,
):
    columns_in = jnp.pad(jnp.stack([attention_gain, feed_gain], axis=-1).astype(F32), ((0, 0), (0, 126)))
    rows_in = jnp.stack([query_gain, key_gain]).astype(F32)
    rows_in = jnp.pad(jnp.concatenate([rows_in, rows_in], axis=-1), ((0, 6), (0, 0)))
    freqs = np.float64(THETA) ** (-(2.0 * np.arange(32)) / 64)
    freqs = jnp.asarray(np.tile(freqs.astype(np.float32), 4)[None])
    (
        block_out, token_grads, input_grad, output_grad, gate_grad, up_grad, down_grad, gain_grads, sums,
    ) = step_call(
        lengths, tokens, teacher, input_weight, output_weight.T, gate_weight, up_weight, down_weight.T,
        columns_in, rows_in, freqs,
    )
    return (
        block_out, sums[2, 0], token_grads, gain_grads[:, 0], input_grad, sums[0, :64], sums[1, :64],
        output_grad.T, gain_grads[:, 1], gate_grad, up_grad, down_grad.T,
    )


def solution(mesh):
    tokens, split = P("fsdp", "seq", None), P(("fsdp", "seq"))
    rows, columns = P(("fsdp", "seq"), None), P(None, ("fsdp", "seq"))
    return jax.shard_map(
        body,
        mesh=mesh,
        in_specs=(
            tokens, tokens, P("fsdp"), split, rows, P(), P(), columns, split, rows, rows, columns,
        ),
        out_specs=(
            tokens, P(), tokens, split, rows, P(), P(), columns, split, rows, rows, columns,
        ),
        check_vma=False,
    )
```

```python
import functools
import math

import jax
import jax.numpy as jnp
import numpy as np
from jax import lax
from jax.experimental import pallas as pl
from jax.experimental.pallas import tpu as pltpu
from jax.sharding import PartitionSpec as P

EPS = 1e-05
THETA = 1000000.0
MESH = pl.DeviceIdType.MESH
F32 = jnp.float32
BF16 = jnp.bfloat16
LOG2E = 1.4426950408889634
HIGH = lax.Precision.HIGHEST
BLOCKS = (4, 2, 4, 2, 16)
PACKED = 8576
IN_AT, OUT_AT, UP_AT, GATE_AT, DOWN_AT = 0, 1152, 1664, 3968, 6272


class Place:
    def __init__(self):
        self.fsdp = lax.axis_index("fsdp")
        self.seq = lax.axis_index("seq")
        self.x = self.fsdp // 2
        self.zh = self.fsdp % 2
        self.y = self.seq // 4
        self.zl = (self.seq // 2) % 2
        self.core = self.seq % 2
        self.chip = self.seq // 2
        self.z = self.zh * 2 + self.zl
        self.here = (self.x, self.zh, self.y, self.zl)

    def sibling(self):
        return (self.fsdp, self.seq + 1 - 2 * self.core)

    def moved(self, axis, step):
        x, y, z = self.x, self.y, self.z
        if axis == "x":
            x = (x + step) % 4
        elif axis == "y":
            y = (y + step) % 4
        else:
            z = (z + step) % 4
        zh, zl = z // 2, z % 2
        return (x, zh, y, zl), (x * 2 + zh, y * 4 + zl * 2 + self.core)


def greet(place):
    barrier = pltpu.get_barrier_semaphore()
    for step in range(1, 16):
        pl.semaphore_signal(
            barrier, inc=1, device_id=(place.fsdp, (place.seq + step) % 16), device_id_type=MESH
        )
    for step in range(1, 4):
        pl.semaphore_signal(barrier, inc=1, device_id=place.moved("x", step)[1], device_id_type=MESH)
    other = place.x * 2 + 1 - place.zh
    for low in range(2):
        pl.semaphore_signal(
            barrier,
            inc=1,
            device_id=(other, place.y * 4 + low * 2 + place.core),
            device_id_type=MESH,
        )


def greeted():
    pl.semaphore_wait(pltpu.get_barrier_semaphore(), 20)


def axes_index(order, stage, here, where, cut=None, half=0):
    index = []
    for axis, mine, other in zip("xzyz", here, where):
        if axis in order[:stage]:
            index.append(mine)
        elif axis == order[stage]:
            index.append(other)
        else:
            index.append(pl.ds(2 * half, 2) if axis == cut else slice(None))
    return tuple(index)


def rest(order, stage, cut=None):
    sizes = (("x", 4), ("z", 2), ("y", 4), ("z", 2))
    return tuple(2 if axis == cut else size for axis, size in sizes if axis not in order[: stage + 1])


def accumulate(sizes, target, others):
    def one(step, carry):
        index, left = [], step
        for size in reversed(sizes):
            index.insert(0, left % size)
            left = left // size
        index = tuple(index)
        total = target[index].astype(F32)
        for other in others:
            total = total + other[index].astype(F32)
        target[index] = total.astype(BF16)
        return carry

    lax.fori_loop(0, math.prod(sizes), one, 0)


class Scatter:
    def __init__(self, place, part, order, ref, lanes, lands, sems, wide=None):
        self.place, self.part, self.order, self.ref, self.lanes = place, part, order, ref, lanes
        self.lands = lands
        self.send, self.recv, self.free = sems
        self.cut = "y" if order[0] == "x" else "x"
        self.wide = wide
        self.copies = {}

    def at(self, stage, where, half=None):
        cut = None if half is None else self.cut
        index = axes_index(self.order, stage, self.place.here, where, cut, half)
        return self.ref.at[index + (slice(None), self.lanes)]

    def step(self, stage, step, half=None):
        return self.at(stage, self.place.moved(self.order[stage], step)[0], half)

    def copy(self, stage, slot, step, src, dst):
        copy = pltpu.make_async_remote_copy(
            src_ref=src,
            dst_ref=dst,
            send_sem=self.send.at[self.part, stage, slot],
            recv_sem=self.recv.at[self.part, stage, slot],
            device_id=self.place.moved(self.order[stage], step)[1],
            device_id_type=MESH,
        )
        copy.start()
        self.copies[stage, slot] = copy

    def direct(self, stage):
        for slot, step in enumerate((1, 3, 2)):
            self.copy(stage, slot, step, self.step(stage, step), self.lands[stage].at[slot])

    def add(self, stage):
        for slot in range(3):
            self.copies[stage, slot].wait_recv()
        others = [self.lands[stage].at[slot] for slot in range(3)]
        accumulate(rest(self.order, stage), self.at(stage, self.place.here), others)

    def far(self):
        for slot, step in enumerate((1, 3)):
            self.copy(0, slot, step, self.step(0, 2, slot), self.lands[0].at[slot])

    def credit(self):
        for slot, step in enumerate((3, 1)):
            pl.semaphore_signal(
                self.free.at[self.part, slot],
                inc=1,
                device_id=self.place.moved(self.order[0], step)[1],
                device_id_type=MESH,
            )

    def near(self):
        for slot, step in enumerate((1, 3)):
            self.copies[0, slot].wait_recv()
            sizes = rest(self.order, 0, self.cut)
            accumulate(sizes, self.step(0, step, slot), [self.lands[0].at[slot]])
            pl.semaphore_wait(self.free.at[self.part, slot], 1)
            self.copy(0, 2 + slot, step, self.step(0, step), self.wide.at[slot])

    def own(self):
        for slot in range(2):
            self.copies[0, 2 + slot].wait_recv()
        accumulate(rest(self.order, 0), self.at(0, self.place.here), [self.wide.at[0], self.wide.at[1]])

    def final(self):
        total = self.at(2, self.place.here)[...].astype(F32)
        for slot in range(3):
            self.copies[2, slot].wait_recv()
            total = total + self.lands[2][slot].astype(F32)
        return total

    def sent(self):
        for copy in self.copies.values():
            copy.wait_send()


class Gather:
    def __init__(self, place, part, order, ref, lanes, send, recv):
        self.place, self.part, self.order, self.ref, self.lanes = place, part, order, ref, lanes
        self.send, self.recv = send, recv
        self.copies = {}

    def at(self, stage, where, half=None):
        index = []
        cut = "y" if self.order[2] == "x" else "x"
        for axis, value in zip("xzyz", where):
            if axis in self.order[:stage]:
                index.append(slice(None) if half is None or axis != cut else pl.ds(2 * half, 2))
            else:
                index.append(value)
        return self.ref.at[tuple(index) + (slice(None), self.lanes)]

    def copy(self, stage, slot, step, block):
        copy = pltpu.make_async_remote_copy(
            src_ref=block,
            dst_ref=block,
            send_sem=self.send.at[self.part, stage, slot],
            recv_sem=self.recv.at[self.part, stage, slot],
            device_id=self.place.moved(self.order[stage], step)[1],
            device_id_type=MESH,
        )
        copy.start()
        self.copies[stage, slot] = copy

    def direct(self, stage):
        for slot, step in enumerate((1, 3, 2)):
            self.copy(stage, slot, step, self.at(stage, self.place.here))

    def near(self):
        for slot, step in enumerate((1, 3)):
            self.copy(2, slot, step, self.at(2, self.place.here))

    def far(self):
        for slot, step in enumerate((1, 3)):
            self.copies[2, slot].wait_recv()
            self.copy(2, 2 + slot, step, self.at(2, self.place.moved(self.order[2], 4 - step)[0], slot))

    def arrived(self, stage):
        for (of, slot), copy in self.copies.items():
            if of == stage and not (stage == 2 and slot < 2 and (2, 3) in self.copies):
                copy.wait_recv()

    def sent(self):
        for copy in self.copies.values():
            copy.wait_send()


def lanes_of(rows):
    return lax.broadcasted_iota(jnp.int32, (rows, 128), 1)


def head_means(squares):
    left = lax.broadcasted_iota(jnp.int32, (128, 128), 0) // 64
    right = lax.broadcasted_iota(jnp.int32, (128, 128), 1) // 64
    mean = jnp.where(left == right, 1.0 / 64, 0.0).astype(F32)
    return lax.dot_general(
        squares, mean, (((1,), (0,)), ((), ())), precision=HIGH, preferred_element_type=F32
    )


def nt(left, right):
    return lax.dot_general(left, right, (((1,), (1,)), ((), ())), preferred_element_type=F32)


def nn(left, right):
    return lax.dot_general(left, right, (((1,), (0,)), ((), ())), preferred_element_type=F32)


def tn(left, right):
    return lax.dot_general(left, right, (((0,), (0,)), ((), ())), preferred_element_type=F32)


def turn(values, low_half):
    return jnp.where(low_half, pltpu.roll(values, 96, 1), pltpu.roll(values, 32, 1))


def columns(ref, start, width):
    return ref[:, :, :, :, :, pl.ds(start, width)].reshape(1024, width)


LOW, REST = 1024, 1280
GATHERED = (
    ("in", 0, 384, "xyz"), ("in", 384, 384, "yzx"), ("in", 768, 384, "zxy"), ("out", 0, 512, "yzx"),
    ("up", 0, 1152, "yzx"), ("up", 1152, 1152, "zyx"), ("gate", 0, LOW, "zxy"), ("gate", LOW, REST, "yxz"),
    ("down", 0, LOW, "xzy"), ("down", LOW, REST, "xyz"),
)
SCATTERED = (
    ("in", 0, 384, "xyz"), ("in", 384, 384, "yzx"), ("in", 768, 256, "zyx"), ("in", 1024, 128, "zyx"),
    ("out", 0, 512, "xyz"), ("up", 0, 1152, "xyz"), ("up", 1152, 1152, "xzy"),
    ("gate", 0, LOW, "yxz"), ("gate", LOW, REST, "zxy"), ("down", 0, LOW, "yxz"), ("down", LOW, REST, "zyx"),
)
PARTS = len(SCATTERED)
WIDE = 5
STARTS = {"in": 0, "out": 1152, "up": 1664, "gate": 3968, "down": 6272}


def step_kernel(
    len_ref, x_ref, t_ref, iw_ref, ow_ref, gw_ref, uw_ref, dw_ref, cols_ref, rows_ref, freq_ref,
    bo_ref, tok_ref, giw_ref, gow_ref, ggw_ref, guw_ref, gdw_ref, gcols_ref, total_ref,
    win_ref, wout_ref, up_ref, gate_ref, down_ref, w_ref, wr_ref, xp_ref, send_ref, qkv_ref,
    kk_ref, v0_ref, v1_ref, ob_ref, ot_ref, do_ref, oh_ref, lse_ref, dd_ref, mixed_ref, h1_ref, gains_ref,
    cos_ref, sin_ref, part_ref, part2_ref, ps_ref, pr0_ref, pr1_ref, h_ref, h2_ref, low_ref,
    acty_ref, actz_ref, dgy_ref, dgz_ref, du_ref, gr_ref, smalls_ref, pair_ref, ring_ref, *others,
):
    lands = [others[3 * i : 3 * i + 3] for i in range(PARTS)]
    (
        ag_send, ag_recv, rs_send, rs_recv, free_sem, w_sem, x_send, x_recv, x_own, q_send, q_recv, o_send, o_recv,
        p_send, p_recv, do_send, do_recv, g_send, g_recv, fin_sem, pair_sem, ring_send, ring_recv,
    ) = others[3 * PARTS :]
    place = Place()
    core, chip = place.core, place.chip
    greet(place)
    sibling = place.sibling()
    gathered = {"in": win_ref, "out": wout_ref, "up": up_ref, "gate": gate_ref, "down": down_ref}

    low_lanes = lanes_of(8) < 64
    for half in range(2):
        for kv in range(4):
            head = half * 4 + kv
            at = kv * 256
            w_ref[half, :, pl.ds(at, 128)] = iw_ref[:, pl.ds(head * 128, 128)].astype(F32)
            keys = iw_ref[:, pl.ds(1024 + head // 2 * 128, 128)].astype(F32)
            values = iw_ref[:, pl.ds(1536 + head // 2 * 128, 128)].astype(F32)
            if head % 2 == 0:
                both = jnp.where(low_lanes, keys, pltpu.roll(values, 64, 1))
            else:
                both = jnp.where(low_lanes, pltpu.roll(keys, 64, 1), values)
            w_ref[half, :, pl.ds(at + 128, 128)] = both
        w_ref[half, :, pl.ds(1024, 128)] = cols_ref[...]
        w_ref[half, :, pl.ds(STARTS["out"], 512)] = ow_ref[:, pl.ds(half * 512, 512)].astype(F32)
        for name, ref in (("up", uw_ref), ("gate", gw_ref), ("down", dw_ref)):
            w_ref[half, :, pl.ds(STARTS[name], 2304)] = ref[:, pl.ds(half * 2304, 2304)].astype(F32)
    greeted()

    def to_sibling(src, dst, send, recv):
        copy = pltpu.make_async_remote_copy(
            src_ref=src, dst_ref=dst, send_sem=send, recv_sem=recv, device_id=sibling, device_id_type=MESH
        )
        copy.start()
        return copy

    w_copy = to_sibling(w_ref.at[1 - core], wr_ref, w_sem.at[0], w_sem.at[1])
    ends = [(x_ref.at[seq], xp_ref.at[seq, core]) for seq in range(2)]
    for seq in range(2):
        for tile in range(4):
            slab = gr_ref.at[(seq * 2 + core) * 2 + tile // 2, pl.ds(tile % 2 * 128, 128), :]
            ends.append((t_ref.at[seq, :, pl.ds(tile * 256, 256)], slab))
    pair_copies, own_copies = [], []
    for n, (src, dst) in enumerate(ends):
        pair_copies.append(to_sibling(src, dst, x_send.at[n], x_recv.at[n]))
        copy = pltpu.make_async_copy(src, dst, x_own.at[n])
        copy.start()
        own_copies.append(copy)

    gathers = [
        Gather(place, i, order, gathered[name], pl.ds(start, width), ag_send, ag_recv)
        for i, (name, start, width, order) in enumerate(GATHERED)
    ]
    mixing, output, ups, gates, downs = gathers[:3], gathers[3], gathers[4:6], gathers[6:8], gathers[8:]
    early = ups + gates

    w_copy.wait_recv()
    first = jnp.where(core == 0, 1.0, 0.0).astype(F32)
    for name, width in (("in", 1152), ("out", 512), ("up", 2304), ("gate", 2304), ("down", 2304)):
        lanes = pl.ds(STARTS[name], width)
        mine = w_ref[core, :, lanes]
        theirs = wr_ref[:, lanes]
        above = jnp.where(first > 0.5, mine, theirs)
        below = jnp.where(first > 0.5, theirs, mine)
        gathered[name][place.here] = jnp.concatenate([above, below], axis=0).astype(BF16)
        if name == "in":
            for item in mixing:
                item.direct(0)
    for item in early + [output] + downs:
        item.direct(0)
    for item in mixing:
        item.arrived(0)
        item.direct(1)
    for item in early + [output]:
        item.arrived(0)
        item.direct(1)

    slots = chip * 256 + lax.broadcasted_iota(jnp.int32, (256, 128), 0)
    angles = slots.astype(F32) * freq_ref[...]
    cos_ref[...] = jnp.cos(angles)
    sine = jnp.sin(angles)
    low_half = lanes_of(256) % 64 < 32
    first_head = lanes_of(256) < 64
    sin_ref[...] = jnp.where(low_half, -sine, sine)

    for item in mixing:
        item.arrived(1)
        item.direct(2)
    for item in downs:
        item.arrived(0)
        item.direct(1)
    output.arrived(1)
    output.direct(2)
    for item in early:
        item.arrived(1)
        item.near()
    for n in range(2):
        pair_copies[n].wait_recv()
        own_copies[n].wait()
    for item in mixing:
        item.arrived(2)

    gains_ref[...] = jnp.transpose(columns(win_ref, 1024, 128).astype(F32))[:8]

    def first_norm(step, carry):
        seq, half = step // 4, (step // 2) % 2
        rows = pl.ds((step % 2) * 64, 64)
        inputs = xp_ref[seq, half, rows, :].astype(F32)
        scale = lax.rsqrt(jnp.mean(inputs * inputs, axis=-1, keepdims=True) + EPS)
        h1_ref[pl.ds(step * 64, 64), :] = (inputs * scale * gains_ref[0:1, :]).astype(BF16)
        return carry

    lax.fori_loop(0, 8, first_norm, 0)

    def to_heads(slot, src_ref, dst_ref, send, recv):
        target = (4 * core + slot // 2) * 2 + slot % 2
        return target, pltpu.make_async_remote_copy(
            src_ref=src_ref.at[slot],
            dst_ref=dst_ref.at[chip],
            send_sem=send.at[slot],
            recv_sem=recv.at[chip],
            device_id=(place.fsdp, target),
            device_id_type=MESH,
        ), pltpu.make_async_copy(src_ref.at[slot], dst_ref.at[chip], recv.at[chip])

    def to_tokens(block, src_ref, dst_ref, send, recv):
        target = block * 2 + chip // 4
        return target, pltpu.make_async_remote_copy(
            src_ref=src_ref.at[block],
            dst_ref=dst_ref.at[chip % 4 * 2 + core],
            send_sem=send.at[block],
            recv_sem=recv.at[chip % 4, core],
            device_id=(place.fsdp, target),
            device_id_type=MESH,
        ), pltpu.make_async_copy(src_ref.at[block], dst_ref.at[chip % 4 * 2 + core], recv.at[chip % 4, core])

    def start_either(target, remote, local):
        @pl.when(target != place.seq)
        def _():
            remote.start()

        @pl.when(target == place.seq)
        def _():
            local.start()

    def sent_either(target, remote, local):
        @pl.when(target != place.seq)
        def _():
            remote.wait_send()

    q_refs = (send_ref, qkv_ref, q_send, q_recv)
    o_refs = (ob_ref, ot_ref, o_send, o_recv)
    do_refs = (ob_ref, do_ref, do_send, do_recv)
    g_refs = (send_ref, gr_ref, g_send, g_recv)

    for kv in range(4):
        weights = columns(win_ref, kv * 256, 256)

        def project(seq, carry, kv=kv, weights=weights):
            rows = pl.ds(pl.multiple_of(seq * 256, 256), 256)
            raw = nn(h1_ref[rows, :], weights)
            mixed_ref[kv, rows, :] = raw
            query, other = raw[:, :128], raw[:, 128:]
            query_norm = query * lax.rsqrt(head_means(query * query) + EPS) * rows_ref[0:1, :]
            other_norm = other * lax.rsqrt(head_means(other * other) + EPS) * rows_ref[1:2, :]
            query_rot = query_norm * cos_ref[...] + turn(query_norm, low_half) * sin_ref[...]
            other_rot = other_norm * cos_ref[...] + turn(other_norm, low_half) * sin_ref[...]
            slot = kv * 2 + seq
            send_ref[slot, :, 0:128] = query_rot.astype(BF16)
            send_ref[slot, :, 128:256] = jnp.where(first_head, other_rot, other).astype(BF16)
            start_either(*to_heads(slot, *q_refs))
            return carry

        lax.fori_loop(0, 2, project, 0)

    for item in gates:
        item.far()

    length = len_ref[core]
    factor = LOG2E / 8.0
    head_row = lax.broadcasted_iota(jnp.int32, (8, 128), 0)
    head_lane = lax.broadcasted_iota(jnp.int32, (8, 128), 1)
    pick = jnp.where(head_lane == head_row * 64, 1.0, 0.0).astype(F32)
    spread = jnp.where(head_lane // 64 == head_row, 1.0, 0.0).astype(F32)

    def nt_high(left, right):
        return lax.dot_general(
            left, right, (((1,), (1,)), ((), ())), precision=HIGH, preferred_element_type=F32
        )

    row = lax.broadcasted_iota(jnp.int32, (256, 256), 0)
    column = lax.broadcasted_iota(jnp.int32, (256, 256), 1)

    def chunks(low, high):
        return [(at, min(at + 4, high)) for at in range(low, high, 4)]

    for block in range(8):
        pltpu.make_async_copy(qkv_ref.at[block], qkv_ref.at[block], q_recv.at[block]).wait()
        other = qkv_ref[block, :, 128:256].astype(F32)
        swapped = pltpu.roll(other, 64, 1)
        there = block * 256 + lax.broadcasted_iota(jnp.int32, (256, 128), 0) < length
        kk_ref[block] = jnp.where(first_head, other, swapped).astype(BF16)
        v0_ref[block] = jnp.where(there, jnp.where(first_head, swapped, 1.0), 0.0).astype(BF16)
        v1_ref[block] = jnp.where(there, jnp.where(first_head, 1.0, other), 0.0).astype(BF16)
        query = qkv_ref[block, :, 0:128]
        nothing = jnp.zeros_like(query)
        sums = []
        for query_h, values in (
            (jnp.where(first_head, query, nothing), v0_ref),
            (jnp.where(first_head, nothing, query), v1_ref),
        ):
            total = jnp.zeros((256, 128), F32)
            for low, high in chunks(0, block + 1):
                size = (high - low) * 256
                weights = jnp.exp2(nt(query_h, kk_ref[low:high].reshape(size, 128)) * factor)
                if high == block + 1:
                    last = jnp.where(column <= row, weights[:, size - 256 :], 0.0)
                    weights = last if size == 256 else jnp.concatenate([weights[:, : size - 256], last], axis=1)
                total = total + nn(weights.astype(BF16), values[low:high].reshape(size, 128))
            sums.append(total)
        sum0, sum1 = sums
        total = jnp.where(first_head, pltpu.roll(sum0, 64, 1), pltpu.roll(sum1, 64, 1))
        mixed = jnp.where(first_head, sum0, sum1) / total
        oh_ref[block] = mixed
        lse_ref[:, block * 256 : block * 256 + 256] = jnp.log2(jnp.maximum(nt_high(pick, total), 1e-30))
        ob_ref[block] = mixed.astype(BF16)
        start_either(*to_tokens(block, *o_refs))

    for item in downs:
        item.arrived(1)
        item.near()
    ups[0].far()
    output.arrived(2)
    for slot in range(8):
        pltpu.make_async_copy(ot_ref.at[slot], ot_ref.at[slot], o_recv.at[slot // 2, slot % 2]).wait()
    attended = jnp.concatenate([ot_ref[2 * kv : 2 * kv + 2].reshape(512, 128) for kv in range(4)], axis=1)

    def send_part(tile, landing, number):
        return pltpu.make_async_remote_copy(
            src_ref=ps_ref.at[tile],
            dst_ref=landing.at[tile],
            send_sem=p_send.at[number, tile],
            recv_sem=p_recv.at[number, tile],
            device_id=sibling,
            device_id_type=MESH,
        )

    def share(tile, part, keep, landing, number):
        keep[tile] = part
        ps_ref[tile] = part.astype(BF16)
        send_part(tile, landing, number).start()

    def shared(landing, number):
        for tile in range(4):
            send_part(tile, landing, number).wait()

    for tile in range(4):
        share(tile, nt(attended, wout_ref[tile].reshape(256, 512)), part_ref, pr0_ref, 0)
    ups[1].far()
    shared(pr0_ref, 0)

    def paired(rows, keep, landing):
        return jnp.concatenate(
            [keep[tile, rows, :] + landing[tile, rows, :].astype(F32) for tile in range(4)], axis=1
        )

    def second_norm(step, carry):
        seq, half = step // 8, (step // 4) % 2
        inputs = xp_ref[seq, half, pl.ds((step % 4) * 32, 32), :].astype(F32)
        rows = pl.ds(step * 32, 32)
        resid = paired(rows, part_ref, pr0_ref) + inputs
        scale = lax.rsqrt(jnp.mean(resid * resid, axis=-1, keepdims=True) + EPS)
        h_ref[rows, :] = resid
        h2_ref[rows, :] = (resid * scale * gains_ref[1:2, :]).astype(BF16)
        return carry

    lax.fori_loop(0, 16, second_norm, 0)

    for item in ups + gates:
        item.arrived(2)

    def tiles(function, after=lambda n: None):
        def low_tile(tile, carry):
            at = pl.multiple_of(tile * 256, 256)
            return function(at, acty_ref, dgy_ref, at, (2, 4, 2, 2, 16, 256), (slice(None),) * 5)

        def rest_tile(tile, carry):
            at = pl.multiple_of(tile * 256, 256)
            at_all = pl.multiple_of(tile * 256 + LOW, 256)
            return function(at_all, actz_ref, dgz_ref, at, (2, 4, 4, 16, 256), (slice(None),) * 4)

        lax.fori_loop(0, LOW // 256, low_tile, 0)
        after(0)
        lax.fori_loop(0, REST // 256, rest_tile, 0)
        after(1)

    whole = (slice(None),) * 5
    du_shape = (2, 2, 4, 2, 16, 256)

    def feed(at, act, dg, at_part, dims, full):
        lanes, lanes_part = pl.ds(at, 256), pl.ds(at_part, 256)
        up = nn(h2_ref[...], columns(up_ref, at, 256))
        gate = nn(h2_ref[...], columns(gate_ref, at, 256))
        sigma = jax.nn.sigmoid(gate)
        silu = gate * sigma
        act[full + (lanes_part,)] = (silu * up).astype(BF16).reshape(dims)
        dg[full + (lanes_part,)] = (up * sigma * (1.0 + gate * (1.0 - sigma))).astype(BF16).reshape(dims)
        du_ref[whole + (lanes,)] = silu.astype(BF16).reshape(du_shape)
        return 0

    tiles(feed, lambda n: downs[n].far())
    for item in downs:
        item.arrived(2)

    def lower(tile, carry):
        weights = down_ref[tile].reshape(256, 2304)
        part = nt(acty_ref[...].reshape(512, LOW), weights[:, :LOW])
        part = part + nt(actz_ref[...].reshape(512, REST), weights[:, LOW:])
        share(tile, part, part_ref, pr1_ref, 1)
        return carry

    lax.fori_loop(0, 4, lower, 0)
    for n in range(2, 10):
        pair_copies[n].wait_recv()
        own_copies[n].wait()
    shared(pr1_ref, 1)

    def errors(step, carry):
        squares, counted = carry
        seq, half, at = step // 8, (step // 4) % 2, pl.ds((step % 4) * 32, 32)
        rows = pl.ds(step * 32, 32)
        final = h_ref[rows, :] + paired(rows, part_ref, pr1_ref)
        slot = chip * 256 + (step % 8) * 32 + lax.broadcasted_iota(jnp.int32, (32, 1024), 0)
        valid = jnp.where(slot < len_ref[seq], 1.0, 0.0).astype(F32)
        slab = (seq * 2 + half) * 2
        teacher = jnp.concatenate(
            [
                gr_ref[slab + tile // 2, pl.ds(tile % 2 * 128 + (step % 4) * 32, 32), :].astype(F32)
                for tile in range(4)
            ],
            axis=1,
        )
        diff = (final - teacher) * valid
        low_ref[rows, :] = diff.astype(BF16)

        @pl.when(half == core)
        def _():
            bo_ref[seq, at, :] = final.astype(BF16)

        mine = jnp.where(half == core, 1.0, 0.0)
        for tile in range(4):
            part_ref[tile, rows, :] = diff[:, tile * 256 : tile * 256 + 256]
        squares = squares + mine * jnp.sum(diff * diff, axis=0, keepdims=True)
        counted = counted + mine * jnp.sum(valid[:, :128], axis=0, keepdims=True)
        return squares, counted

    squares, counted = lax.fori_loop(
        0, 16, errors, (jnp.zeros((1, 1024), F32), jnp.zeros((1, 128), F32))
    )
    folded = squares[:, 0:128]
    for tile in range(1, 8):
        folded = folded + squares[:, tile * 128 : tile * 128 + 128]
    smalls_ref[...] = jnp.concatenate(
        [jnp.zeros((2, 128), F32), folded, counted, jnp.zeros((4, 128), F32)], axis=0
    )
    w_copy.wait_send()
    for item in gathers:
        item.sent()

    wides = {
        5: du_ref.at[:, :, :, :, :, pl.ds(0, 1152)], 6: du_ref.at[:, :, :, :, :, pl.ds(1152, 1152)],
        7: dgy_ref, 8: dgz_ref, 9: acty_ref, 10: actz_ref,
    }
    scatters = [
        Scatter(
            place, i, order, gathered[name], pl.ds(start, width), lands[i], (rs_send, rs_recv, free_sem), wides.get(i)
        )
        for i, (name, start, width, order) in enumerate(SCATTERED)
    ]
    mix_s, gain_s, out_s = scatters[:3], scatters[3], scatters[4]
    up_s, gate_s, down_s = scatters[5:7], scatters[7:9], scatters[9:]

    def raise_back(at, act, dg, at_part, dims, full):
        lanes, lanes_part = pl.ds(at, 256), pl.ds(at_part, 256)
        grad_act = nn(low_ref[...], columns(down_ref, at, 256))
        dg_at, du_at = full + (lanes_part,), whole + (lanes,)
        dg[dg_at] = (grad_act * dg[dg_at].reshape(512, 256).astype(F32)).astype(BF16).reshape(dims)
        du_ref[du_at] = (grad_act * du_ref[du_at].reshape(512, 256).astype(F32)).astype(BF16).reshape(du_shape)
        grad = tn(low_ref[...], act[full + (lanes_part,)].reshape(512, 256))
        down_ref[whole + (lanes,)] = grad.astype(BF16).reshape(BLOCKS + (256,))
        return 0

    def round_first(items):
        def start(n):
            if n < len(items):
                items[n].credit()
                items[n].far()

        return start

    tiles(raise_back, round_first(down_s))

    def feed_back(tile, carry):
        weights = gate_ref[tile].reshape(256, 2304)
        part = nt(dgy_ref[...].reshape(512, LOW), weights[:, :LOW])
        part = part + nt(dgz_ref[...].reshape(512, REST), weights[:, LOW:])
        part = part + nt(du_ref[...].reshape(512, 2304), up_ref[tile].reshape(256, 2304))
        share(tile, part, part2_ref, pr0_ref, 2)
        return carry

    lax.fori_loop(0, 4, feed_back, 0)

    def up_grads(tile, carry):
        lanes = pl.ds(pl.multiple_of(tile * 256, 256), 256)
        grad = tn(h2_ref[...], du_ref[whole + (lanes,)].reshape(512, 256))
        up_ref[whole + (lanes,)] = grad.astype(BF16).reshape(BLOCKS + (256,))
        return carry

    lax.fori_loop(0, 9, up_grads, 0)
    for item in up_s:
        item.credit()
        item.far()
    shared(pr0_ref, 2)

    def second_back(step, carry):
        seq, half, at = step // 8, (step // 4) % 2, pl.ds((step % 4) * 32, 32)
        rows = pl.ds(step * 32, 32)
        grad = paired(rows, part2_ref, pr0_ref)
        diff = jnp.concatenate([part_ref[tile, rows, :] for tile in range(4)], axis=1)
        resid = h_ref[rows, :]
        scale = lax.rsqrt(jnp.mean(resid * resid, axis=-1, keepdims=True) + EPS)
        inner = grad * gains_ref[1:2, :]
        mean = jnp.mean(inner * resid, axis=-1, keepdims=True)
        result = diff + scale * inner - resid * (scale * scale * scale) * mean
        low_ref[rows, :] = result.astype(BF16)

        @pl.when(half == core)
        def _():
            tok_ref[seq, at, :] = result

        return carry + jnp.sum(grad * resid * scale, axis=0, keepdims=True)

    feed_sum = lax.fori_loop(0, 16, second_back, jnp.zeros((1, 1024), F32))

    for slot in range(8):
        sent_either(*to_heads(slot, *q_refs))
    for block in range(8):
        sent_either(*to_tokens(block, *o_refs))
    for kv in range(4):
        grad = nn(low_ref[...], columns(wout_ref, kv * 128, 128)).astype(BF16)
        for seq in range(2):
            ob_ref[kv * 2 + seq] = grad[seq * 256 : seq * 256 + 256]
            start_either(*to_heads(kv * 2 + seq, *do_refs))
    for item in down_s:
        item.near()
    for kv in range(4):
        grad = tn(low_ref[...], ot_ref[2 * kv : 2 * kv + 2].reshape(512, 128))
        wout_ref[whole + (pl.ds(kv * 128, 128),)] = grad.astype(BF16).reshape(BLOCKS + (128,))
    out_s.direct(0)

    def gate_grads(at, act, dg, at_part, dims, full):
        grad = tn(h2_ref[...], dg[full + (pl.ds(at_part, 256),)].reshape(512, 256))
        gate_ref[whole + (pl.ds(at, 256),)] = grad.astype(BF16).reshape(BLOCKS + (256,))
        return 0

    tiles(gate_grads, round_first(gate_s))

    rhs = (kk_ref, v0_ref, v1_ref, ot_ref)

    def prepare(block, carry):
        pltpu.make_async_copy(do_ref.at[block], do_ref.at[block], do_recv.at[block]).wait()
        query = qkv_ref[block, :, 0:128].astype(F32)
        grad = do_ref[block].astype(F32)
        zero = jnp.zeros_like(query)
        dd_ref[:, pl.ds(pl.multiple_of(block * 256, 256), 256)] = nt_high(spread, grad * oh_ref[block])
        kk_ref[block] = jnp.where(first_head, query, zero).astype(BF16)
        v0_ref[block] = jnp.where(first_head, pltpu.roll(query, 64, 1), zero).astype(BF16)
        v1_ref[block] = jnp.where(first_head, zero, pltpu.roll(grad, 64, 1)).astype(BF16)
        ot_ref[block] = jnp.where(first_head, zero, grad).astype(BF16)
        oh_ref[block] = zero
        return carry

    lax.fori_loop(0, 8, prepare, 0)
    for item in up_s:
        item.near()

    def attend_back(key_block):
        other = qkv_ref[key_block, :, 128:256].astype(F32)
        swapped = pltpu.roll(other, 64, 1)
        zero = jnp.zeros_like(other)
        keys0 = jnp.where(first_head, other, zero).astype(BF16)
        keys1 = jnp.where(first_head, zero, swapped).astype(BF16)
        values0 = jnp.where(first_head, swapped, zero).astype(BF16)
        values1 = jnp.where(first_head, zero, other).astype(BF16)
        keys = jnp.concatenate([keys0, keys1], axis=0)
        total = zero
        for low, high in chunks(key_block, 8):
            size = (high - low) * 256
            lanes = slice(low * 256, high * 256)
            query = qkv_ref[low:high, :, 0:128].reshape(size, 128)
            grad = do_ref[low:high].reshape(size, 128)
            chances, grads = [], []
            for head, keys_h, values_h in ((0, keys0, values0), (1, keys1, values1)):
                chance = jnp.exp2(nt(keys_h, query) * factor - lse_ref[head : head + 1, lanes])
                if low == key_block:
                    first_block = jnp.where(row <= column, chance[:, :256], 0.0)
                    chance = first_block if size == 256 else jnp.concatenate([first_block, chance[:, 256:]], axis=1)
                inner = nt(values_h, grad) - dd_ref[head : head + 1, lanes]
                chances.append(chance.astype(BF16))
                grads.append((chance * inner).astype(BF16))
            for left, ref in zip(grads + chances, rhs):
                total = total + nn(left, ref[low:high].reshape(size, 128))
            query_grad = tn(jnp.concatenate(grads, axis=0), keys)
            for block in range(low, high):
                at = (block - low) * 256
                oh_ref[block] = oh_ref[block] + query_grad[at : at + 256]
        send_ref[key_block, :, 0:128] = (oh_ref[key_block] * 0.125).astype(BF16)
        send_ref[key_block, :, 128:256] = jnp.where(first_head, total * 0.125, total).astype(BF16)
        start_either(*to_tokens(key_block, *g_refs))

    for key_block in range(8):
        attend_back(key_block)
        if key_block == 1:
            for item in down_s:
                item.own()
                item.direct(1)
            out_s.add(0)
            out_s.direct(1)
    for item in gate_s:
        item.near()

    for kv in range(4):
        for seq in range(2):
            landed = gr_ref.at[kv * 2 + seq]
            pltpu.make_async_copy(landed, landed, g_recv.at[kv, seq]).wait()

        def back(seq, carry, kv=kv):
            rows = pl.ds(pl.multiple_of(seq * 256, 256), 256)
            raws = mixed_ref[kv, rows, :]
            grads = gr_ref[kv * 2 + seq].astype(F32)
            results = []
            for part in range(2):
                lanes = slice(part * 128, part * 128 + 128)
                raw, grad = raws[:, lanes], grads[:, lanes]
                scale = lax.rsqrt(head_means(raw * raw) + EPS)
                grad_norm = grad * cos_ref[...] + turn(grad * sin_ref[...], low_half)
                gain_sum = jnp.sum(grad_norm * raw * scale, axis=0, keepdims=True)
                smalls_ref[part : part + 1, :] = smalls_ref[part : part + 1, :] + gain_sum
                inner = grad_norm * rows_ref[part : part + 1, :]
                result = scale * inner - raw * (scale * scale * scale) * head_means(inner * raw)
                if part == 1:
                    result = jnp.where(first_head, result, grad)
                results.append(result)
            h2_ref[rows, pl.ds(kv * 256, 256)] = jnp.concatenate(results, axis=1).astype(BF16)
            return carry

        lax.fori_loop(0, 2, back, 0)

    def mix_grads(kv, carry):
        at = pl.multiple_of(kv * 256, 256)
        grad = tn(h1_ref[...], h2_ref[:, pl.ds(at, 256)])
        win_ref[whole + (pl.ds(at, 256),)] = grad.astype(BF16).reshape(BLOCKS + (256,))
        return carry

    def mix_back(tile, carry):
        weights = win_ref[tile, :, :, :, :, pl.ds(0, 1024)].reshape(256, 1024)
        share(tile, nt(h2_ref[...], weights), part2_ref, pr1_ref, 3)
        return carry

    lax.fori_loop(0, 4, mix_back, 0)
    lax.fori_loop(0, 4, mix_grads, 0)
    for item in mix_s:
        item.direct(0)
    for item in up_s:
        item.own()
        item.direct(1)
    shared(pr1_ref, 3)

    def last(step, carry):
        seq, at = step // 4, (step % 4) * 32
        rows = pl.ds(seq * 256 + core * 128 + at, 32)
        at = pl.ds(at, 32)
        inputs = xp_ref[seq, core, at, :].astype(F32)
        scale = lax.rsqrt(jnp.mean(inputs * inputs, axis=-1, keepdims=True) + EPS)
        grad = paired(rows, part2_ref, pr1_ref)
        inner = grad * gains_ref[0:1, :]
        mean = jnp.mean(inner * inputs, axis=-1, keepdims=True)
        tok_ref[seq, at, :] = tok_ref[seq, at, :] + scale * inner - inputs * (scale * scale * scale) * mean
        return carry + jnp.sum(grad * inputs * scale, axis=0, keepdims=True)

    gain_grad = lax.fori_loop(0, 8, last, jnp.zeros((1, 1024), F32))
    both = jnp.concatenate([gain_grad, feed_sum, jnp.zeros((126, 1024), F32)], axis=0)
    win_ref[whole + (pl.ds(1024, 128),)] = jnp.transpose(both).astype(BF16).reshape(BLOCKS + (128,))
    gain_s.direct(0)

    pair_ref[core] = smalls_ref[...]
    pair_copy = to_sibling(smalls_ref, pair_ref.at[core], pair_sem.at[0], pair_sem.at[1])

    def ring_start(stage, value):
        axis = "xyz"[stage]
        here = {"x": place.x, "y": place.y, "z": place.z}[axis]
        ring_ref[stage, here] = value
        copies = []
        for step in (1, 3, 2):
            copy = pltpu.make_async_remote_copy(
                src_ref=ring_ref.at[stage, here],
                dst_ref=ring_ref.at[stage, here],
                send_sem=ring_send.at[stage, step - 1],
                recv_sem=ring_recv.at[stage, step - 1],
                device_id=place.moved(axis, step)[1],
                device_id_type=MESH,
            )
            copy.start()
            copies.append(copy)
        return copies

    def ring_sum(stage, copies):
        for copy in copies:
            copy.wait_recv()
        total = ring_ref[stage, 0]
        for other in range(1, 4):
            total = total + ring_ref[stage, other]
        return total

    pair_copy.wait_recv()
    rings = [ring_start(0, pair_ref[0] + pair_ref[1])]

    for item in gate_s:
        item.own()
        item.direct(1)
    for item in mix_s:
        item.add(0)
        item.direct(1)
    for item in [out_s] + down_s:
        item.add(1)
        item.direct(2)
    gain_s.add(0)
    gain_s.direct(1)
    rings.append(ring_start(1, ring_sum(0, rings[0])))
    for item in mix_s:
        item.add(1)
        item.direct(2)
    for item in [gain_s] + up_s + gate_s:
        item.add(1)
        item.direct(2)
    rings.append(ring_start(2, ring_sum(1, rings[1])))

    for i, (name, start, width, _) in reversed(list(enumerate(SCATTERED))):
        w_ref[:, :, pl.ds(STARTS[name] + start, width)] = scatters[i].final().reshape(2, 8, width)
    fin_copy = to_sibling(w_ref.at[1 - core], wr_ref, fin_sem.at[0], fin_sem.at[1])

    sums = ring_sum(2, rings[2])
    query_sum, key_sum, loss_sum, count = sums[0:1], sums[1:2], sums[2:3], sums[3:4]
    loss = jnp.sum(loss_sum, axis=1, keepdims=True) / (count * 1024.0)
    total_ref[...] = jnp.concatenate(
        [query_sum + pltpu.roll(query_sum, 64, 1), key_sum, loss, jnp.zeros((5, 128), F32)], axis=0
    )

    fin_copy.wait_recv()
    first = jnp.where(core == 0, 1.0, 0.0).astype(F32)

    def half_of(half, at, width):
        mine, theirs = w_ref[core, :, pl.ds(at, width)], wr_ref[:, pl.ds(at, width)]
        return jnp.where(first > 0.5, mine, theirs) if half == 0 else jnp.where(first > 0.5, theirs, mine)

    for half in range(2):
        gow_ref[:, pl.ds(half * 512, 512)] = half_of(half, STARTS["out"], 512)
        for name, ref in (("up", guw_ref), ("gate", ggw_ref), ("down", gdw_ref)):
            ref[:, pl.ds(half * 2304, 2304)] = half_of(half, STARTS[name], 2304)
        pairs = [half_of(half, kv * 256, 256) for kv in range(4)]
        for kv in range(4):
            giw_ref[:, pl.ds((half * 4 + kv) * 128, 128)] = pairs[kv][:, :128]
        for pair in range(2):
            even, odd = pairs[2 * pair][:, 128:], pairs[2 * pair + 1][:, 128:]
            at = (half * 2 + pair) * 128
            giw_ref[:, pl.ds(1024 + at, 128)] = jnp.where(low_lanes, even, pltpu.roll(odd, 64, 1))
            giw_ref[:, pl.ds(1536 + at, 128)] = jnp.where(low_lanes, pltpu.roll(even, 64, 1), odd)
    cols0, cols1 = w_ref[core, :, pl.ds(1024, 128)], wr_ref[:, pl.ds(1024, 128)]
    gain_columns = jnp.where(lanes_of(8) == 0, cols0 + cols1, cols0)
    gcols_ref[...] = nt_high(jnp.where(head_lane == head_row, 1.0, 0.0).astype(F32), gain_columns)

    for copy in [fin_copy, pair_copy] + pair_copies:
        copy.wait_send()
    for copies in rings:
        for copy in copies:
            copy.wait_send()
    for slot in range(8):
        sent_either(*to_heads(slot, *do_refs))
        sent_either(*to_tokens(slot, *g_refs))
    for item in scatters:
        item.sent()


def step_call(*operands):
    any_space = pl.BlockSpec(memory_space=pl.ANY)
    vmem = pl.BlockSpec(memory_space=pltpu.VMEM)
    smem = pl.BlockSpec(memory_space=pltpu.SMEM)

    def shape(dims, kind=F32):
        return jax.ShapeDtypeStruct(dims, kind)

    def room(dims, kind=BF16):
        return pltpu.VMEM(dims, kind)

    dma = pltpu.SemaphoreType.DMA
    lands = []
    for i, (_, _, n, order) in enumerate(SCATTERED):
        cut = "y" if order[0] == "x" else "x"
        if i < WIDE:
            lands.append(room((3,) + rest(order, 0) + (16, n)))
        else:
            lands.append(room((2,) + rest(order, 0, cut) + (16, n)))
        lands += [room((3,) + rest(order, 1) + (16, n)), room((3, 16, n))]
    heads, tokens = (8, 256, 128), (2, 2, 128, 1024)
    return pl.pallas_call(
        step_kernel,
        out_shape=(
            shape((2, 128, 1024), BF16), shape((2, 128, 1024)), shape((8, 2048)), shape((8, 1024)),
            shape((8, 4608)), shape((8, 4608)), shape((8, 4608)), shape((8, 8)), shape((8, 128)),
        ),
        in_specs=[smem, any_space, any_space] + [vmem] * 8,
        out_specs=(vmem,) * 9,
        scratch_shapes=[
            room(BLOCKS + (1152,)), room(BLOCKS + (512,)),
            room(BLOCKS + (2304,)), room(BLOCKS + (2304,)), room(BLOCKS + (2304,)),
            room((2, 8, PACKED), F32), room((8, PACKED), F32), room(tokens),
            room((8, 256, 256)), room((8, 256, 256)),
            room(heads), room(heads), room(heads), room(heads), room(heads), room(heads),
            room(heads, F32), room((8, 2048), F32), room((8, 2048), F32),
            room((4, 512, 256), F32), room((512, 1024)), room((8, 1024), F32), room((256, 128), F32), room((256, 128), F32),
            room((4, 512, 256), F32), room((4, 512, 256), F32), room((4, 512, 256)),
            room((4, 512, 256)), room((4, 512, 256)),
            room((512, 1024), F32), room((512, 1024)), room((512, 1024)),
            room((2, 4, 2, 2, 16, LOW)), room((2, 4, 4, 16, REST)),
            room((2, 4, 2, 2, 16, LOW)), room((2, 4, 4, 16, REST)), room((2, 2, 4, 2, 16, 2304)),
            room((8, 256, 256)), room((8, 128), F32), room((2, 8, 128), F32), room((3, 4, 8, 128), F32),
        ]
        + lands
        + [
            dma((10, 3, 4)), dma((10, 3, 4)), dma((PARTS, 3, 4)), dma((PARTS, 3, 4)), pltpu.SemaphoreType.REGULAR((PARTS, 2)),
            dma((2,)), dma((10,)), dma((10,)), dma((10,)), dma((8,)), dma((8,)), dma((8,)), dma((4, 2)),
            dma((4, 4)), dma((4, 4)), dma((8,)), dma((8,)), dma((8,)), dma((4, 2)),
            dma((2,)), dma((2,)), dma((3, 3)), dma((3, 3)),
        ],
        name="whole_step",
        compiler_params=pltpu.CompilerParams(
            collective_id=0, has_side_effects=True, vmem_limit_bytes=64 * 1024 * 1024 - 65536
        ),
    )(*operands)


def finish_kernel(
    bo_ref, tok_ref, giw_ref, gow_ref, ggw_ref, guw_ref, gdw_ref, gains_ref, sums_ref,
    bo_out, loss_out, tok_out, ag_out, iw_out, qg_out, kg_out, ow_out, fg_out, gw_out, uw_out, dw_out,
):
    for src, dst in (
        (bo_ref, bo_out), (tok_ref, tok_out), (giw_ref, iw_out), (gow_ref, ow_out),
        (ggw_ref, gw_out), (guw_ref, uw_out), (gdw_ref, dw_out),
    ):
        dst[...] = src[...]
    qg_out[...] = sums_ref[0:1, 0:64]
    kg_out[...] = sums_ref[1:2, 0:64]
    loss_out[...] = sums_ref[2:3, 0:1]
    ag_out[...] = gains_ref[0:1, :]
    fg_out[...] = gains_ref[1:2, :]


def finish(*operands):
    def shape(dims, kind=F32):
        return jax.ShapeDtypeStruct(dims, kind)

    vmem = pl.BlockSpec(memory_space=pltpu.VMEM)
    return pl.pallas_call(
        finish_kernel,
        out_shape=(
            shape((2, 128, 1024), BF16), shape((1, 1)), shape((2, 128, 1024)), shape((1, 8)), shape((8, 2048)),
            shape((1, 64)), shape((1, 64)), shape((8, 1024)), shape((1, 8)), shape((8, 4608)), shape((8, 4608)),
            shape((8, 4608)),
        ),
        in_specs=[vmem] * 9,
        out_specs=(vmem,) * 12,
        name="finish",
    )(*operands)


def body(
    tokens, teacher, lengths, attention_gain, input_weight, query_gain, key_gain,
    output_weight, feed_gain, gate_weight, up_weight, down_weight,
):
    columns_in = jnp.pad(jnp.stack([attention_gain, feed_gain], axis=-1).astype(F32), ((0, 0), (0, 126)))
    rows_in = jnp.stack([query_gain, key_gain]).astype(F32)
    rows_in = jnp.pad(jnp.concatenate([rows_in, rows_in], axis=-1), ((0, 6), (0, 0)))
    freqs = np.float64(THETA) ** (-(2.0 * np.arange(32)) / 64)
    freqs = jnp.asarray(np.tile(freqs.astype(np.float32), 4)[None])
    (
        block_out, token_grads, input_grad, output_grad, gate_grad, up_grad, down_grad, gain_grads, sums,
    ) = step_call(
        lengths, tokens, teacher, input_weight, output_weight.T, gate_weight, up_weight, down_weight.T,
        columns_in, rows_in, freqs,
    )
    (
        block_out, loss, token_grads, attention_gain_grad, input_grad, query_gain_grad, key_gain_grad, output_grad,
        feed_gain_grad, gate_grad, up_grad, down_grad,
    ) = finish(
        block_out, token_grads, input_grad, output_grad, gate_grad, up_grad, down_grad, gain_grads, sums
    )
    return (
        block_out, loss.reshape(()), token_grads, attention_gain_grad.reshape(8), input_grad,
        query_gain_grad.reshape(64), key_gain_grad.reshape(64),
        output_grad.T, feed_gain_grad.reshape(8), gate_grad, up_grad, down_grad.T,
    )


def solution(mesh):
    tokens, split = P("fsdp", "seq", None), P(("fsdp", "seq"))
    rows, columns = P(("fsdp", "seq"), None), P(None, ("fsdp", "seq"))
    return jax.shard_map(
        body,
        mesh=mesh,
        in_specs=(
            tokens, tokens, P("fsdp"), split, rows, P(), P(), columns, split, rows, rows, columns,
        ),
        out_specs=(
            tokens, P(), tokens, split, rows, P(), P(), columns, split, rows, rows, columns,
        ),
        check_vma=False,
    )
```

```python
import functools
import math

import jax
import jax.numpy as jnp
import numpy as np
from jax import lax
from jax.experimental import pallas as pl
from jax.experimental.pallas import tpu as pltpu
from jax.sharding import PartitionSpec as P

EPS = 1e-05
THETA = 1000000.0
MESH = pl.DeviceIdType.MESH
F32 = jnp.float32
BF16 = jnp.bfloat16
LOG2E = 1.4426950408889634
HIGH = lax.Precision.HIGHEST
BLOCKS = (4, 2, 4, 2, 16)
PACKED = 8576
IN_AT, OUT_AT, UP_AT, GATE_AT, DOWN_AT = 0, 1152, 1664, 3968, 6272


class Place:
    def __init__(self):
        self.fsdp = lax.axis_index("fsdp")
        self.seq = lax.axis_index("seq")
        self.x = self.fsdp // 2
        self.zh = self.fsdp % 2
        self.y = self.seq // 4
        self.zl = (self.seq // 2) % 2
        self.core = self.seq % 2
        self.chip = self.seq // 2
        self.z = self.zh * 2 + self.zl
        self.here = (self.x, self.zh, self.y, self.zl)

    def sibling(self):
        return (self.fsdp, self.seq + 1 - 2 * self.core)

    def moved(self, axis, step):
        x, y, z = self.x, self.y, self.z
        if axis == "x":
            x = (x + step) % 4
        elif axis == "y":
            y = (y + step) % 4
        else:
            z = (z + step) % 4
        zh, zl = z // 2, z % 2
        return (x, zh, y, zl), (x * 2 + zh, y * 4 + zl * 2 + self.core)


def greet(place):
    barrier = pltpu.get_barrier_semaphore()
    for step in range(1, 16):
        pl.semaphore_signal(
            barrier, inc=1, device_id=(place.fsdp, (place.seq + step) % 16), device_id_type=MESH
        )
    for step in range(1, 4):
        pl.semaphore_signal(barrier, inc=1, device_id=place.moved("x", step)[1], device_id_type=MESH)
    other = place.x * 2 + 1 - place.zh
    for low in range(2):
        pl.semaphore_signal(
            barrier,
            inc=1,
            device_id=(other, place.y * 4 + low * 2 + place.core),
            device_id_type=MESH,
        )


def greeted():
    pl.semaphore_wait(pltpu.get_barrier_semaphore(), 20)


def axes_index(order, stage, here, where, cut=None, half=0):
    index = []
    for axis, mine, other in zip("xzyz", here, where):
        if axis in order[:stage]:
            index.append(mine)
        elif axis == order[stage]:
            index.append(other)
        else:
            index.append(pl.ds(2 * half, 2) if axis == cut else slice(None))
    return tuple(index)


def rest(order, stage, cut=None):
    sizes = (("x", 4), ("z", 2), ("y", 4), ("z", 2))
    return tuple(2 if axis == cut else size for axis, size in sizes if axis not in order[: stage + 1])


def accumulate(sizes, target, others):
    def one(step, carry):
        index, left = [], step
        for size in reversed(sizes):
            index.insert(0, left % size)
            left = left // size
        index = tuple(index)
        total = target[index].astype(F32)
        for other in others:
            total = total + other[index].astype(F32)
        target[index] = total.astype(BF16)
        return carry

    lax.fori_loop(0, math.prod(sizes), one, 0)


class Scatter:
    def __init__(self, place, part, order, ref, lanes, lands, sems, wide=None):
        self.place, self.part, self.order, self.ref, self.lanes = place, part, order, ref, lanes
        self.lands = lands
        self.send, self.recv, self.free = sems
        self.cut = "y" if order[0] == "x" else "x"
        self.wide = wide
        self.copies = {}

    def at(self, stage, where, half=None):
        cut = None if half is None else self.cut
        index = axes_index(self.order, stage, self.place.here, where, cut, half)
        return self.ref.at[index + (slice(None), self.lanes)]

    def step(self, stage, step, half=None):
        return self.at(stage, self.place.moved(self.order[stage], step)[0], half)

    def copy(self, stage, slot, step, src, dst):
        copy = pltpu.make_async_remote_copy(
            src_ref=src,
            dst_ref=dst,
            send_sem=self.send.at[self.part, stage, slot],
            recv_sem=self.recv.at[self.part, stage, slot],
            device_id=self.place.moved(self.order[stage], step)[1],
            device_id_type=MESH,
        )
        copy.start()
        self.copies[stage, slot] = copy

    def direct(self, stage):
        for slot, step in enumerate((1, 3, 2)):
            self.copy(stage, slot, step, self.step(stage, step), self.lands[stage].at[slot])

    def add(self, stage):
        for slot in range(3):
            self.copies[stage, slot].wait_recv()
        others = [self.lands[stage].at[slot] for slot in range(3)]
        accumulate(rest(self.order, stage), self.at(stage, self.place.here), others)

    def far(self):
        for slot, step in enumerate((1, 3)):
            self.copy(0, slot, step, self.step(0, 2, slot), self.lands[0].at[slot])

    def credit(self):
        for slot, step in enumerate((3, 1)):
            pl.semaphore_signal(
                self.free.at[self.part, slot],
                inc=1,
                device_id=self.place.moved(self.order[0], step)[1],
                device_id_type=MESH,
            )

    def near(self):
        for slot, step in enumerate((1, 3)):
            self.copies[0, slot].wait_recv()
            sizes = rest(self.order, 0, self.cut)
            accumulate(sizes, self.step(0, step, slot), [self.lands[0].at[slot]])
            pl.semaphore_wait(self.free.at[self.part, slot], 1)
            self.copy(0, 2 + slot, step, self.step(0, step), self.wide.at[slot])

    def own(self):
        for slot in range(2):
            self.copies[0, 2 + slot].wait_recv()
        accumulate(rest(self.order, 0), self.at(0, self.place.here), [self.wide.at[0], self.wide.at[1]])

    def final(self):
        total = self.at(2, self.place.here)[...].astype(F32)
        for slot in range(3):
            self.copies[2, slot].wait_recv()
            total = total + self.lands[2][slot].astype(F32)
        return total

    def sent(self):
        for copy in self.copies.values():
            copy.wait_send()


class Gather:
    def __init__(self, place, part, order, ref, lanes, send, recv):
        self.place, self.part, self.order, self.ref, self.lanes = place, part, order, ref, lanes
        self.send, self.recv = send, recv
        self.copies = {}

    def at(self, stage, where, half=None):
        index = []
        cut = "y" if self.order[2] == "x" else "x"
        for axis, value in zip("xzyz", where):
            if axis in self.order[:stage]:
                index.append(slice(None) if half is None or axis != cut else pl.ds(2 * half, 2))
            else:
                index.append(value)
        return self.ref.at[tuple(index) + (slice(None), self.lanes)]

    def copy(self, stage, slot, step, block):
        copy = pltpu.make_async_remote_copy(
            src_ref=block,
            dst_ref=block,
            send_sem=self.send.at[self.part, stage, slot],
            recv_sem=self.recv.at[self.part, stage, slot],
            device_id=self.place.moved(self.order[stage], step)[1],
            device_id_type=MESH,
        )
        copy.start()
        self.copies[stage, slot] = copy

    def direct(self, stage):
        for slot, step in enumerate((1, 3, 2)):
            self.copy(stage, slot, step, self.at(stage, self.place.here))

    def near(self):
        for slot, step in enumerate((1, 3)):
            self.copy(2, slot, step, self.at(2, self.place.here))

    def far(self):
        for slot, step in enumerate((1, 3)):
            self.copies[2, slot].wait_recv()
            self.copy(2, 2 + slot, step, self.at(2, self.place.moved(self.order[2], 4 - step)[0], slot))

    def arrived(self, stage):
        for (of, slot), copy in self.copies.items():
            if of == stage and not (stage == 2 and slot < 2 and (2, 3) in self.copies):
                copy.wait_recv()

    def sent(self):
        for copy in self.copies.values():
            copy.wait_send()


def lanes_of(rows):
    return lax.broadcasted_iota(jnp.int32, (rows, 128), 1)


def head_means(squares):
    left = lax.broadcasted_iota(jnp.int32, (128, 128), 0) // 64
    right = lax.broadcasted_iota(jnp.int32, (128, 128), 1) // 64
    mean = jnp.where(left == right, 1.0 / 64, 0.0).astype(F32)
    return lax.dot_general(
        squares, mean, (((1,), (0,)), ((), ())), precision=HIGH, preferred_element_type=F32
    )


def nt(left, right):
    return lax.dot_general(left, right, (((1,), (1,)), ((), ())), preferred_element_type=F32)


def nn(left, right):
    return lax.dot_general(left, right, (((1,), (0,)), ((), ())), preferred_element_type=F32)


def tn(left, right):
    return lax.dot_general(left, right, (((0,), (0,)), ((), ())), preferred_element_type=F32)


def turn(values, low_half):
    return jnp.where(low_half, pltpu.roll(values, 96, 1), pltpu.roll(values, 32, 1))


def columns(ref, start, width):
    return ref[:, :, :, :, :, pl.ds(start, width)].reshape(1024, width)


LOW, REST = 1024, 1280
GATHERED = (
    ("in", 0, 384, "xyz"), ("in", 384, 384, "yzx"), ("in", 768, 384, "zxy"), ("out", 0, 512, "yzx"),
    ("up", 0, 1152, "yzx"), ("up", 1152, 1152, "zyx"), ("gate", 0, LOW, "zxy"), ("gate", LOW, REST, "yxz"),
    ("down", 0, LOW, "xzy"), ("down", LOW, REST, "xyz"),
)
SCATTERED = (
    ("in", 0, 384, "xyz"), ("in", 384, 384, "yzx"), ("in", 768, 256, "zyx"), ("in", 1024, 128, "zyx"),
    ("out", 0, 512, "xyz"), ("up", 0, 1152, "xyz"), ("up", 1152, 1152, "xzy"),
    ("gate", 0, LOW, "yxz"), ("gate", LOW, REST, "zxy"), ("down", 0, LOW, "yxz"), ("down", LOW, REST, "zyx"),
)
PARTS = len(SCATTERED)
WIDE = 5
STARTS = {"in": 0, "out": 1152, "up": 1664, "gate": 3968, "down": 6272}


def step_kernel(
    len_ref, x_ref, t_ref, iw_ref, ow_ref, gw_ref, uw_ref, dw_ref, cols_ref, rows_ref, freq_ref,
    bo_ref, tok_ref, giw_ref, gow_ref, ggw_ref, guw_ref, gdw_ref, gcols_ref, total_ref,
    win_ref, wout_ref, up_ref, gate_ref, down_ref, w_ref, wr_ref, xp_ref, send_ref, qkv_ref,
    kk_ref, v0_ref, v1_ref, ob_ref, ot_ref, do_ref, oh_ref, lse_ref, dd_ref, mixed_ref, h1_ref, gains_ref,
    cos_ref, sin_ref, part_ref, part2_ref, ps_ref, pr0_ref, pr1_ref, h_ref, h2_ref, low_ref,
    acty_ref, actz_ref, dgy_ref, dgz_ref, du_ref, gr_ref, smalls_ref, pair_ref, ring_ref, *others,
):
    lands = [others[3 * i : 3 * i + 3] for i in range(PARTS)]
    (
        ag_send, ag_recv, rs_send, rs_recv, free_sem, w_sem, x_send, x_recv, x_own, q_send, q_recv, o_send, o_recv,
        p_send, p_recv, do_send, do_recv, g_send, g_recv, fin_sem, pair_sem, ring_send, ring_recv,
    ) = others[3 * PARTS :]
    place = Place()
    core, chip = place.core, place.chip
    greet(place)
    sibling = place.sibling()
    gathered = {"in": win_ref, "out": wout_ref, "up": up_ref, "gate": gate_ref, "down": down_ref}

    low_lanes = lanes_of(8) < 64
    for half in range(2):
        for kv in range(4):
            head = half * 4 + kv
            at = kv * 256
            w_ref[half, :, pl.ds(at, 128)] = iw_ref[:, pl.ds(head * 128, 128)].astype(F32)
            keys = iw_ref[:, pl.ds(1024 + head // 2 * 128, 128)].astype(F32)
            values = iw_ref[:, pl.ds(1536 + head // 2 * 128, 128)].astype(F32)
            if head % 2 == 0:
                both = jnp.where(low_lanes, keys, pltpu.roll(values, 64, 1))
            else:
                both = jnp.where(low_lanes, pltpu.roll(keys, 64, 1), values)
            w_ref[half, :, pl.ds(at + 128, 128)] = both
        w_ref[half, :, pl.ds(1024, 128)] = cols_ref[...]
        w_ref[half, :, pl.ds(STARTS["out"], 512)] = ow_ref[:, pl.ds(half * 512, 512)].astype(F32)
        for name, ref in (("up", uw_ref), ("gate", gw_ref), ("down", dw_ref)):
            w_ref[half, :, pl.ds(STARTS[name], 2304)] = ref[:, pl.ds(half * 2304, 2304)].astype(F32)
    greeted()

    def to_sibling(src, dst, send, recv):
        copy = pltpu.make_async_remote_copy(
            src_ref=src, dst_ref=dst, send_sem=send, recv_sem=recv, device_id=sibling, device_id_type=MESH
        )
        copy.start()
        return copy

    w_copy = to_sibling(w_ref.at[1 - core], wr_ref, w_sem.at[0], w_sem.at[1])
    ends = [(x_ref.at[seq], xp_ref.at[seq, core]) for seq in range(2)]
    for seq in range(2):
        for tile in range(4):
            slab = gr_ref.at[(seq * 2 + core) * 2 + tile // 2, pl.ds(tile % 2 * 128, 128), :]
            ends.append((t_ref.at[seq, :, pl.ds(tile * 256, 256)], slab))
    pair_copies, own_copies = [], []
    for n, (src, dst) in enumerate(ends):
        pair_copies.append(to_sibling(src, dst, x_send.at[n], x_recv.at[n]))
        copy = pltpu.make_async_copy(src, dst, x_own.at[n])
        copy.start()
        own_copies.append(copy)

    gathers = [
        Gather(place, i, order, gathered[name], pl.ds(start, width), ag_send, ag_recv)
        for i, (name, start, width, order) in enumerate(GATHERED)
    ]
    mixing, output, ups, gates, downs = gathers[:3], gathers[3], gathers[4:6], gathers[6:8], gathers[8:]
    early = ups + gates

    w_copy.wait_recv()
    first = jnp.where(core == 0, 1.0, 0.0).astype(F32)
    for name, width in (("in", 1152), ("out", 512), ("up", 2304), ("gate", 2304), ("down", 2304)):
        lanes = pl.ds(STARTS[name], width)
        mine = w_ref[core, :, lanes]
        theirs = wr_ref[:, lanes]
        above = jnp.where(first > 0.5, mine, theirs)
        below = jnp.where(first > 0.5, theirs, mine)
        gathered[name][place.here] = jnp.concatenate([above, below], axis=0).astype(BF16)
        if name == "in":
            for item in mixing:
                item.direct(0)
    for item in early + [output] + downs:
        item.direct(0)
    for item in mixing:
        item.arrived(0)
        item.direct(1)
    for item in early + [output]:
        item.arrived(0)
        item.direct(1)

    slots = chip * 256 + lax.broadcasted_iota(jnp.int32, (256, 128), 0)
    angles = slots.astype(F32) * freq_ref[...]
    cos_ref[...] = jnp.cos(angles)
    sine = jnp.sin(angles)
    low_half = lanes_of(256) % 64 < 32
    first_head = lanes_of(256) < 64
    sin_ref[...] = jnp.where(low_half, -sine, sine)

    for item in mixing:
        item.arrived(1)
        item.direct(2)
    for item in downs:
        item.arrived(0)
        item.direct(1)
    output.arrived(1)
    output.direct(2)
    for item in early:
        item.arrived(1)
        item.near()
    for n in range(2):
        pair_copies[n].wait_recv()
        own_copies[n].wait()
    for item in mixing:
        item.arrived(2)

    gains_ref[...] = jnp.transpose(columns(win_ref, 1024, 128).astype(F32))[:8]

    def first_norm(step, carry):
        seq, half = step // 4, (step // 2) % 2
        rows = pl.ds((step % 2) * 64, 64)
        inputs = xp_ref[seq, half, rows, :].astype(F32)
        scale = lax.rsqrt(jnp.mean(inputs * inputs, axis=-1, keepdims=True) + EPS)
        h1_ref[pl.ds(step * 64, 64), :] = (inputs * scale * gains_ref[0:1, :]).astype(BF16)
        return carry

    lax.fori_loop(0, 8, first_norm, 0)

    def to_heads(slot, src_ref, dst_ref, send, recv):
        target = (4 * core + slot // 2) * 2 + slot % 2
        return target, pltpu.make_async_remote_copy(
            src_ref=src_ref.at[slot],
            dst_ref=dst_ref.at[chip],
            send_sem=send.at[slot],
            recv_sem=recv.at[chip],
            device_id=(place.fsdp, target),
            device_id_type=MESH,
        ), pltpu.make_async_copy(src_ref.at[slot], dst_ref.at[chip], recv.at[chip])

    def to_tokens(block, src_ref, dst_ref, send, recv):
        target = block * 2 + chip // 4
        return target, pltpu.make_async_remote_copy(
            src_ref=src_ref.at[block],
            dst_ref=dst_ref.at[chip % 4 * 2 + core],
            send_sem=send.at[block],
            recv_sem=recv.at[chip % 4, core],
            device_id=(place.fsdp, target),
            device_id_type=MESH,
        ), pltpu.make_async_copy(src_ref.at[block], dst_ref.at[chip % 4 * 2 + core], recv.at[chip % 4, core])

    def start_either(target, remote, local):
        @pl.when(target != place.seq)
        def _():
            remote.start()

        @pl.when(target == place.seq)
        def _():
            local.start()

    def sent_either(target, remote, local):
        @pl.when(target != place.seq)
        def _():
            remote.wait_send()

    q_refs = (send_ref, qkv_ref, q_send, q_recv)
    o_refs = (ob_ref, ot_ref, o_send, o_recv)
    do_refs = (ob_ref, do_ref, do_send, do_recv)
    g_refs = (send_ref, gr_ref, g_send, g_recv)

    for kv in range(4):
        weights = columns(win_ref, kv * 256, 256)

        def project(seq, carry, kv=kv, weights=weights):
            rows = pl.ds(pl.multiple_of(seq * 256, 256), 256)
            raw = nn(h1_ref[rows, :], weights)
            mixed_ref[kv, rows, :] = raw
            query, other = raw[:, :128], raw[:, 128:]
            query_norm = query * lax.rsqrt(head_means(query * query) + EPS) * rows_ref[0:1, :]
            other_norm = other * lax.rsqrt(head_means(other * other) + EPS) * rows_ref[1:2, :]
            query_rot = query_norm * cos_ref[...] + turn(query_norm, low_half) * sin_ref[...]
            other_rot = other_norm * cos_ref[...] + turn(other_norm, low_half) * sin_ref[...]
            slot = kv * 2 + seq
            send_ref[slot, :, 0:128] = query_rot.astype(BF16)
            send_ref[slot, :, 128:256] = jnp.where(first_head, other_rot, other).astype(BF16)
            start_either(*to_heads(slot, *q_refs))
            return carry

        lax.fori_loop(0, 2, project, 0)

    for item in gates:
        item.far()

    length = len_ref[core]
    factor = LOG2E / 8.0
    head_row = lax.broadcasted_iota(jnp.int32, (8, 128), 0)
    head_lane = lax.broadcasted_iota(jnp.int32, (8, 128), 1)
    pick = jnp.where(head_lane == head_row * 64, 1.0, 0.0).astype(F32)
    spread = jnp.where(head_lane // 64 == head_row, 1.0, 0.0).astype(F32)

    def nt_high(left, right):
        return lax.dot_general(
            left, right, (((1,), (1,)), ((), ())), precision=HIGH, preferred_element_type=F32
        )

    row = lax.broadcasted_iota(jnp.int32, (256, 256), 0)
    column = lax.broadcasted_iota(jnp.int32, (256, 256), 1)

    def chunks(low, high):
        return [(at, min(at + 4, high)) for at in range(low, high, 4)]

    for block in range(8):
        pltpu.make_async_copy(qkv_ref.at[block], qkv_ref.at[block], q_recv.at[block]).wait()
        other = qkv_ref[block, :, 128:256].astype(F32)
        swapped = pltpu.roll(other, 64, 1)
        there = block * 256 + lax.broadcasted_iota(jnp.int32, (256, 128), 0) < length
        kk_ref[block] = jnp.where(first_head, other, swapped).astype(BF16)
        v0_ref[block] = jnp.where(there, jnp.where(first_head, swapped, 1.0), 0.0).astype(BF16)
        v1_ref[block] = jnp.where(there, jnp.where(first_head, 1.0, other), 0.0).astype(BF16)
        query = qkv_ref[block, :, 0:128]
        nothing = jnp.zeros_like(query)
        sums = []
        for query_h, values in (
            (jnp.where(first_head, query, nothing), v0_ref),
            (jnp.where(first_head, nothing, query), v1_ref),
        ):
            total = jnp.zeros((256, 128), F32)
            for low, high in chunks(0, block + 1):
                size = (high - low) * 256
                weights = jnp.exp2(nt(query_h, kk_ref[low:high].reshape(size, 128)) * factor)
                if high == block + 1:
                    last = jnp.where(column <= row, weights[:, size - 256 :], 0.0)
                    weights = last if size == 256 else jnp.concatenate([weights[:, : size - 256], last], axis=1)
                total = total + nn(weights.astype(BF16), values[low:high].reshape(size, 128))
            sums.append(total)
        sum0, sum1 = sums
        total = jnp.where(first_head, pltpu.roll(sum0, 64, 1), pltpu.roll(sum1, 64, 1))
        mixed = jnp.where(first_head, sum0, sum1) / total
        oh_ref[block] = mixed
        lse_ref[:, block * 256 : block * 256 + 256] = jnp.log2(jnp.maximum(nt_high(pick, total), 1e-30))
        ob_ref[block] = mixed.astype(BF16)
        start_either(*to_tokens(block, *o_refs))

    for item in downs:
        item.arrived(1)
        item.near()
    ups[0].far()
    output.arrived(2)
    for slot in range(8):
        pltpu.make_async_copy(ot_ref.at[slot], ot_ref.at[slot], o_recv.at[slot // 2, slot % 2]).wait()
    attended = jnp.concatenate([ot_ref[2 * kv : 2 * kv + 2].reshape(512, 128) for kv in range(4)], axis=1)

    def send_part(tile, landing, number):
        return pltpu.make_async_remote_copy(
            src_ref=ps_ref.at[tile],
            dst_ref=landing.at[tile],
            send_sem=p_send.at[number, tile],
            recv_sem=p_recv.at[number, tile],
            device_id=sibling,
            device_id_type=MESH,
        )

    def share(tile, part, keep, landing, number):
        keep[tile] = part
        ps_ref[tile] = part.astype(BF16)
        send_part(tile, landing, number).start()

    def shared(landing, number):
        for tile in range(4):
            send_part(tile, landing, number).wait()

    for tile in range(4):
        share(tile, nt(attended, wout_ref[tile].reshape(256, 512)), part_ref, pr0_ref, 0)
    ups[1].far()
    shared(pr0_ref, 0)

    def paired(rows, keep, landing):
        return jnp.concatenate(
            [keep[tile, rows, :] + landing[tile, rows, :].astype(F32) for tile in range(4)], axis=1
        )

    def second_norm(step, carry):
        seq, half = step // 8, (step // 4) % 2
        inputs = xp_ref[seq, half, pl.ds((step % 4) * 32, 32), :].astype(F32)
        rows = pl.ds(step * 32, 32)
        resid = paired(rows, part_ref, pr0_ref) + inputs
        scale = lax.rsqrt(jnp.mean(resid * resid, axis=-1, keepdims=True) + EPS)
        h_ref[rows, :] = resid
        h2_ref[rows, :] = (resid * scale * gains_ref[1:2, :]).astype(BF16)
        return carry

    lax.fori_loop(0, 16, second_norm, 0)

    for item in ups + gates:
        item.arrived(2)

    def tiles(function, after=lambda n: None):
        def low_tile(tile, carry):
            at = pl.multiple_of(tile * 256, 256)
            return function(at, acty_ref, dgy_ref, at, (2, 4, 2, 2, 16, 256), (slice(None),) * 5)

        def rest_tile(tile, carry):
            at = pl.multiple_of(tile * 256, 256)
            at_all = pl.multiple_of(tile * 256 + LOW, 256)
            return function(at_all, actz_ref, dgz_ref, at, (2, 4, 4, 16, 256), (slice(None),) * 4)

        lax.fori_loop(0, LOW // 256, low_tile, 0)
        after(0)
        lax.fori_loop(0, REST // 256, rest_tile, 0)
        after(1)

    whole = (slice(None),) * 5
    du_shape = (2, 2, 4, 2, 16, 256)

    def feed(at, act, dg, at_part, dims, full):
        lanes, lanes_part = pl.ds(at, 256), pl.ds(at_part, 256)
        up = nn(h2_ref[...], columns(up_ref, at, 256))
        gate = nn(h2_ref[...], columns(gate_ref, at, 256))
        sigma = jax.nn.sigmoid(gate)
        silu = gate * sigma
        act[full + (lanes_part,)] = (silu * up).astype(BF16).reshape(dims)
        dg[full + (lanes_part,)] = (up * sigma * (1.0 + gate * (1.0 - sigma))).astype(BF16).reshape(dims)
        du_ref[whole + (lanes,)] = silu.astype(BF16).reshape(du_shape)
        return 0

    tiles(feed, lambda n: downs[n].far())
    for item in downs:
        item.arrived(2)

    def lower(tile, carry):
        weights = down_ref[tile].reshape(256, 2304)
        part = nt(acty_ref[...].reshape(512, LOW), weights[:, :LOW])
        part = part + nt(actz_ref[...].reshape(512, REST), weights[:, LOW:])
        share(tile, part, part_ref, pr1_ref, 1)
        return carry

    lax.fori_loop(0, 4, lower, 0)
    for n in range(2, 10):
        pair_copies[n].wait_recv()
        own_copies[n].wait()

    def errors(step, carry, tile):
        squares, counted = carry
        seq, half = step // 2, step % 2
        rows = pl.ds(pl.multiple_of(step * 128, 128), 128)
        lanes = pl.ds(tile * 256, 256)
        final = h_ref[rows, lanes] + part_ref[tile, rows, :] + pr1_ref[tile, rows, :].astype(F32)
        slot = chip * 256 + half * 128 + lax.broadcasted_iota(jnp.int32, (128, 256), 0)
        valid = jnp.where(slot < len_ref[seq], 1.0, 0.0).astype(F32)
        teacher = gr_ref[(seq * 2 + half) * 2 + tile // 2, pl.ds(tile % 2 * 128, 128), :].astype(F32)
        diff = (final - teacher) * valid
        low_ref[rows, lanes] = diff.astype(BF16)
        part_ref[tile, rows, :] = diff

        @pl.when(half == core)
        def _():
            bo_ref[seq, :, lanes] = final.astype(BF16)

        mine = jnp.where(half == core, 1.0, 0.0)
        squares = squares + mine * jnp.sum(diff * diff, axis=0, keepdims=True)
        counted = counted + mine * jnp.sum(valid[:, :128], axis=0, keepdims=True)
        return squares, counted

    sums = (jnp.zeros((1, 256), F32), jnp.zeros((1, 128), F32))
    for tile in range(4):
        send_part(tile, pr1_ref, 1).wait()
        sums = lax.fori_loop(0, 4, functools.partial(errors, tile=tile), sums)
    folded, counted = sums[0][:, :128] + sums[0][:, 128:], sums[1] * 0.25
    smalls_ref[...] = jnp.concatenate(
        [jnp.zeros((2, 128), F32), folded, counted, jnp.zeros((4, 128), F32)], axis=0
    )
    w_copy.wait_send()
    for item in gathers:
        item.sent()

    wides = {
        5: du_ref.at[:, :, :, :, :, pl.ds(0, 1152)], 6: du_ref.at[:, :, :, :, :, pl.ds(1152, 1152)],
        7: dgy_ref, 8: dgz_ref, 9: acty_ref, 10: actz_ref,
    }
    scatters = [
        Scatter(
            place, i, order, gathered[name], pl.ds(start, width), lands[i], (rs_send, rs_recv, free_sem), wides.get(i)
        )
        for i, (name, start, width, order) in enumerate(SCATTERED)
    ]
    mix_s, gain_s, out_s = scatters[:3], scatters[3], scatters[4]
    up_s, gate_s, down_s = scatters[5:7], scatters[7:9], scatters[9:]

    def raise_back(at, act, dg, at_part, dims, full):
        lanes, lanes_part = pl.ds(at, 256), pl.ds(at_part, 256)
        grad_act = nn(low_ref[...], columns(down_ref, at, 256))
        dg_at, du_at = full + (lanes_part,), whole + (lanes,)
        dg[dg_at] = (grad_act * dg[dg_at].reshape(512, 256).astype(F32)).astype(BF16).reshape(dims)
        du_ref[du_at] = (grad_act * du_ref[du_at].reshape(512, 256).astype(F32)).astype(BF16).reshape(du_shape)
        grad = tn(low_ref[...], act[full + (lanes_part,)].reshape(512, 256))
        down_ref[whole + (lanes,)] = grad.astype(BF16).reshape(BLOCKS + (256,))
        return 0

    def round_first(items):
        def start(n):
            if n < len(items):
                items[n].credit()
                items[n].far()

        return start

    tiles(raise_back, round_first(down_s))

    def feed_back(tile, carry):
        weights = gate_ref[tile].reshape(256, 2304)
        part = nt(dgy_ref[...].reshape(512, LOW), weights[:, :LOW])
        part = part + nt(dgz_ref[...].reshape(512, REST), weights[:, LOW:])
        part = part + nt(du_ref[...].reshape(512, 2304), up_ref[tile].reshape(256, 2304))
        share(tile, part, part2_ref, pr0_ref, 2)
        return carry

    lax.fori_loop(0, 4, feed_back, 0)

    def up_grads(tile, carry):
        lanes = pl.ds(pl.multiple_of(tile * 256, 256), 256)
        grad = tn(h2_ref[...], du_ref[whole + (lanes,)].reshape(512, 256))
        up_ref[whole + (lanes,)] = grad.astype(BF16).reshape(BLOCKS + (256,))
        return carry

    lax.fori_loop(0, 9, up_grads, 0)
    for item in up_s:
        item.credit()
        item.far()
    shared(pr0_ref, 2)

    def second_back(step, carry):
        seq, half, at = step // 8, (step // 4) % 2, pl.ds((step % 4) * 32, 32)
        rows = pl.ds(step * 32, 32)
        grad = paired(rows, part2_ref, pr0_ref)
        diff = jnp.concatenate([part_ref[tile, rows, :] for tile in range(4)], axis=1)
        resid = h_ref[rows, :]
        scale = lax.rsqrt(jnp.mean(resid * resid, axis=-1, keepdims=True) + EPS)
        inner = grad * gains_ref[1:2, :]
        mean = jnp.mean(inner * resid, axis=-1, keepdims=True)
        result = diff + scale * inner - resid * (scale * scale * scale) * mean
        low_ref[rows, :] = result.astype(BF16)

        @pl.when(half == core)
        def _():
            tok_ref[seq, at, :] = result

        return carry + jnp.sum(grad * resid * scale, axis=0, keepdims=True)

    feed_sum = lax.fori_loop(0, 16, second_back, jnp.zeros((1, 1024), F32))

    for slot in range(8):
        sent_either(*to_heads(slot, *q_refs))
    for block in range(8):
        sent_either(*to_tokens(block, *o_refs))
    for kv in range(4):
        grad = nn(low_ref[...], columns(wout_ref, kv * 128, 128)).astype(BF16)
        for seq in range(2):
            ob_ref[kv * 2 + seq] = grad[seq * 256 : seq * 256 + 256]
            start_either(*to_heads(kv * 2 + seq, *do_refs))
    for item in down_s:
        item.near()
    for kv in range(4):
        grad = tn(low_ref[...], ot_ref[2 * kv : 2 * kv + 2].reshape(512, 128))
        wout_ref[whole + (pl.ds(kv * 128, 128),)] = grad.astype(BF16).reshape(BLOCKS + (128,))
    out_s.direct(0)

    def gate_grads(at, act, dg, at_part, dims, full):
        grad = tn(h2_ref[...], dg[full + (pl.ds(at_part, 256),)].reshape(512, 256))
        gate_ref[whole + (pl.ds(at, 256),)] = grad.astype(BF16).reshape(BLOCKS + (256,))
        return 0

    tiles(gate_grads, round_first(gate_s))

    rhs = (kk_ref, v0_ref, v1_ref, ot_ref)

    def prepare(block, carry):
        pltpu.make_async_copy(do_ref.at[block], do_ref.at[block], do_recv.at[block]).wait()
        query = qkv_ref[block, :, 0:128].astype(F32)
        grad = do_ref[block].astype(F32)
        zero = jnp.zeros_like(query)
        dd_ref[:, pl.ds(pl.multiple_of(block * 256, 256), 256)] = nt_high(spread, grad * oh_ref[block])
        kk_ref[block] = jnp.where(first_head, query, zero).astype(BF16)
        v0_ref[block] = jnp.where(first_head, pltpu.roll(query, 64, 1), zero).astype(BF16)
        v1_ref[block] = jnp.where(first_head, zero, pltpu.roll(grad, 64, 1)).astype(BF16)
        ot_ref[block] = jnp.where(first_head, zero, grad).astype(BF16)
        oh_ref[block] = zero
        return carry

    lax.fori_loop(0, 8, prepare, 0)
    for item in up_s:
        item.near()

    def attend_back(key_block):
        other = qkv_ref[key_block, :, 128:256].astype(F32)
        swapped = pltpu.roll(other, 64, 1)
        zero = jnp.zeros_like(other)
        keys0 = jnp.where(first_head, other, zero).astype(BF16)
        keys1 = jnp.where(first_head, zero, swapped).astype(BF16)
        values0 = jnp.where(first_head, swapped, zero).astype(BF16)
        values1 = jnp.where(first_head, zero, other).astype(BF16)
        keys = jnp.concatenate([keys0, keys1], axis=0)
        total = zero
        for low, high in chunks(key_block, 8):
            size = (high - low) * 256
            lanes = slice(low * 256, high * 256)
            query = qkv_ref[low:high, :, 0:128].reshape(size, 128)
            grad = do_ref[low:high].reshape(size, 128)
            chances, grads = [], []
            for head, keys_h, values_h in ((0, keys0, values0), (1, keys1, values1)):
                chance = jnp.exp2(nt(keys_h, query) * factor - lse_ref[head : head + 1, lanes])
                if low == key_block:
                    first_block = jnp.where(row <= column, chance[:, :256], 0.0)
                    chance = first_block if size == 256 else jnp.concatenate([first_block, chance[:, 256:]], axis=1)
                inner = nt(values_h, grad) - dd_ref[head : head + 1, lanes]
                chances.append(chance.astype(BF16))
                grads.append((chance * inner).astype(BF16))
            for left, ref in zip(grads + chances, rhs):
                total = total + nn(left, ref[low:high].reshape(size, 128))
            query_grad = tn(jnp.concatenate(grads, axis=0), keys)
            for block in range(low, high):
                at = (block - low) * 256
                oh_ref[block] = oh_ref[block] + query_grad[at : at + 256]
        send_ref[key_block, :, 0:128] = (oh_ref[key_block] * 0.125).astype(BF16)
        send_ref[key_block, :, 128:256] = jnp.where(first_head, total * 0.125, total).astype(BF16)
        start_either(*to_tokens(key_block, *g_refs))

    for key_block in range(8):
        attend_back(key_block)
        if key_block == 1:
            for item in down_s:
                item.own()
                item.direct(1)
            out_s.add(0)
            out_s.direct(1)
    for item in gate_s:
        item.near()

    for kv in range(4):
        for seq in range(2):
            landed = gr_ref.at[kv * 2 + seq]
            pltpu.make_async_copy(landed, landed, g_recv.at[kv, seq]).wait()

        def back(seq, carry, kv=kv):
            rows = pl.ds(pl.multiple_of(seq * 256, 256), 256)
            raws = mixed_ref[kv, rows, :]
            grads = gr_ref[kv * 2 + seq].astype(F32)
            results = []
            for part in range(2):
                lanes = slice(part * 128, part * 128 + 128)
                raw, grad = raws[:, lanes], grads[:, lanes]
                scale = lax.rsqrt(head_means(raw * raw) + EPS)
                grad_norm = grad * cos_ref[...] + turn(grad * sin_ref[...], low_half)
                gain_sum = jnp.sum(grad_norm * raw * scale, axis=0, keepdims=True)
                smalls_ref[part : part + 1, :] = smalls_ref[part : part + 1, :] + gain_sum
                inner = grad_norm * rows_ref[part : part + 1, :]
                result = scale * inner - raw * (scale * scale * scale) * head_means(inner * raw)
                if part == 1:
                    result = jnp.where(first_head, result, grad)
                results.append(result)
            h2_ref[rows, pl.ds(kv * 256, 256)] = jnp.concatenate(results, axis=1).astype(BF16)
            return carry

        lax.fori_loop(0, 2, back, 0)

    def mix_grads(kv, carry):
        at = pl.multiple_of(kv * 256, 256)
        grad = tn(h1_ref[...], h2_ref[:, pl.ds(at, 256)])
        win_ref[whole + (pl.ds(at, 256),)] = grad.astype(BF16).reshape(BLOCKS + (256,))
        return carry

    def mix_back(tile, carry):
        weights = win_ref[tile, :, :, :, :, pl.ds(0, 1024)].reshape(256, 1024)
        share(tile, nt(h2_ref[...], weights), part2_ref, pr1_ref, 3)
        return carry

    lax.fori_loop(0, 4, mix_back, 0)
    lax.fori_loop(0, 4, mix_grads, 0)
    for item in mix_s:
        item.direct(0)
    for item in up_s:
        item.own()
        item.direct(1)
    shared(pr1_ref, 3)

    def last(step, carry):
        seq, at = step // 4, (step % 4) * 32
        rows = pl.ds(seq * 256 + core * 128 + at, 32)
        at = pl.ds(at, 32)
        inputs = xp_ref[seq, core, at, :].astype(F32)
        scale = lax.rsqrt(jnp.mean(inputs * inputs, axis=-1, keepdims=True) + EPS)
        grad = paired(rows, part2_ref, pr1_ref)
        inner = grad * gains_ref[0:1, :]
        mean = jnp.mean(inner * inputs, axis=-1, keepdims=True)
        tok_ref[seq, at, :] = tok_ref[seq, at, :] + scale * inner - inputs * (scale * scale * scale) * mean
        return carry + jnp.sum(grad * inputs * scale, axis=0, keepdims=True)

    gain_grad = lax.fori_loop(0, 8, last, jnp.zeros((1, 1024), F32))
    both = jnp.concatenate([gain_grad, feed_sum, jnp.zeros((126, 1024), F32)], axis=0)
    win_ref[whole + (pl.ds(1024, 128),)] = jnp.transpose(both).astype(BF16).reshape(BLOCKS + (128,))
    gain_s.direct(0)

    pair_ref[core] = smalls_ref[...]
    pair_copy = to_sibling(smalls_ref, pair_ref.at[core], pair_sem.at[0], pair_sem.at[1])

    def ring_start(stage, value):
        axis = "xyz"[stage]
        here = {"x": place.x, "y": place.y, "z": place.z}[axis]
        ring_ref[stage, here] = value
        copies = []
        for step in (1, 3, 2):
            copy = pltpu.make_async_remote_copy(
                src_ref=ring_ref.at[stage, here],
                dst_ref=ring_ref.at[stage, here],
                send_sem=ring_send.at[stage, step - 1],
                recv_sem=ring_recv.at[stage, step - 1],
                device_id=place.moved(axis, step)[1],
                device_id_type=MESH,
            )
            copy.start()
            copies.append(copy)
        return copies

    def ring_sum(stage, copies):
        for copy in copies:
            copy.wait_recv()
        total = ring_ref[stage, 0]
        for other in range(1, 4):
            total = total + ring_ref[stage, other]
        return total

    pair_copy.wait_recv()
    rings = [ring_start(0, pair_ref[0] + pair_ref[1])]

    for item in gate_s:
        item.own()
        item.direct(1)
    for item in mix_s:
        item.add(0)
        item.direct(1)
    for item in [out_s] + down_s:
        item.add(1)
        item.direct(2)
    gain_s.add(0)
    gain_s.direct(1)
    rings.append(ring_start(1, ring_sum(0, rings[0])))
    for item in mix_s:
        item.add(1)
        item.direct(2)
    for item in [gain_s] + up_s + gate_s:
        item.add(1)
        item.direct(2)
    rings.append(ring_start(2, ring_sum(1, rings[1])))

    for i, (name, start, width, _) in reversed(list(enumerate(SCATTERED))):
        w_ref[:, :, pl.ds(STARTS[name] + start, width)] = scatters[i].final().reshape(2, 8, width)
    fin_copy = to_sibling(w_ref.at[1 - core], wr_ref, fin_sem.at[0], fin_sem.at[1])

    sums = ring_sum(2, rings[2])
    query_sum, key_sum, loss_sum, count = sums[0:1], sums[1:2], sums[2:3], sums[3:4]
    loss = jnp.sum(loss_sum, axis=1, keepdims=True) / (count * 1024.0)
    total_ref[...] = jnp.concatenate(
        [query_sum + pltpu.roll(query_sum, 64, 1), key_sum, loss, jnp.zeros((5, 128), F32)], axis=0
    )

    fin_copy.wait_recv()
    first = jnp.where(core == 0, 1.0, 0.0).astype(F32)

    def half_of(half, at, width):
        mine, theirs = w_ref[core, :, pl.ds(at, width)], wr_ref[:, pl.ds(at, width)]
        return jnp.where(first > 0.5, mine, theirs) if half == 0 else jnp.where(first > 0.5, theirs, mine)

    for half in range(2):
        gow_ref[:, pl.ds(half * 512, 512)] = half_of(half, STARTS["out"], 512)
        for name, ref in (("up", guw_ref), ("gate", ggw_ref), ("down", gdw_ref)):
            ref[:, pl.ds(half * 2304, 2304)] = half_of(half, STARTS[name], 2304)
        pairs = [half_of(half, kv * 256, 256) for kv in range(4)]
        for kv in range(4):
            giw_ref[:, pl.ds((half * 4 + kv) * 128, 128)] = pairs[kv][:, :128]
        for pair in range(2):
            even, odd = pairs[2 * pair][:, 128:], pairs[2 * pair + 1][:, 128:]
            at = (half * 2 + pair) * 128
            giw_ref[:, pl.ds(1024 + at, 128)] = jnp.where(low_lanes, even, pltpu.roll(odd, 64, 1))
            giw_ref[:, pl.ds(1536 + at, 128)] = jnp.where(low_lanes, pltpu.roll(even, 64, 1), odd)
    cols0, cols1 = w_ref[core, :, pl.ds(1024, 128)], wr_ref[:, pl.ds(1024, 128)]
    gain_columns = jnp.where(lanes_of(8) == 0, cols0 + cols1, cols0)
    gcols_ref[...] = nt_high(jnp.where(head_lane == head_row, 1.0, 0.0).astype(F32), gain_columns)

    for copy in [fin_copy, pair_copy] + pair_copies:
        copy.wait_send()
    for copies in rings:
        for copy in copies:
            copy.wait_send()
    for slot in range(8):
        sent_either(*to_heads(slot, *do_refs))
        sent_either(*to_tokens(slot, *g_refs))
    for item in scatters:
        item.sent()


def step_call(*operands):
    any_space = pl.BlockSpec(memory_space=pl.ANY)
    vmem = pl.BlockSpec(memory_space=pltpu.VMEM)
    smem = pl.BlockSpec(memory_space=pltpu.SMEM)

    def shape(dims, kind=F32):
        return jax.ShapeDtypeStruct(dims, kind)

    def room(dims, kind=BF16):
        return pltpu.VMEM(dims, kind)

    dma = pltpu.SemaphoreType.DMA
    lands = []
    for i, (_, _, n, order) in enumerate(SCATTERED):
        cut = "y" if order[0] == "x" else "x"
        if i < WIDE:
            lands.append(room((3,) + rest(order, 0) + (16, n)))
        else:
            lands.append(room((2,) + rest(order, 0, cut) + (16, n)))
        lands += [room((3,) + rest(order, 1) + (16, n)), room((3, 16, n))]
    heads, tokens = (8, 256, 128), (2, 2, 128, 1024)
    return pl.pallas_call(
        step_kernel,
        out_shape=(
            shape((2, 128, 1024), BF16), shape((2, 128, 1024)), shape((8, 2048)), shape((8, 1024)),
            shape((8, 4608)), shape((8, 4608)), shape((8, 4608)), shape((8, 8)), shape((8, 128)),
        ),
        in_specs=[smem, any_space, any_space] + [vmem] * 8,
        out_specs=(vmem,) * 9,
        scratch_shapes=[
            room(BLOCKS + (1152,)), room(BLOCKS + (512,)),
            room(BLOCKS + (2304,)), room(BLOCKS + (2304,)), room(BLOCKS + (2304,)),
            room((2, 8, PACKED), F32), room((8, PACKED), F32), room(tokens),
            room((8, 256, 256)), room((8, 256, 256)),
            room(heads), room(heads), room(heads), room(heads), room(heads), room(heads),
            room(heads, F32), room((8, 2048), F32), room((8, 2048), F32),
            room((4, 512, 256), F32), room((512, 1024)), room((8, 1024), F32), room((256, 128), F32), room((256, 128), F32),
            room((4, 512, 256), F32), room((4, 512, 256), F32), room((4, 512, 256)),
            room((4, 512, 256)), room((4, 512, 256)),
            room((512, 1024), F32), room((512, 1024)), room((512, 1024)),
            room((2, 4, 2, 2, 16, LOW)), room((2, 4, 4, 16, REST)),
            room((2, 4, 2, 2, 16, LOW)), room((2, 4, 4, 16, REST)), room((2, 2, 4, 2, 16, 2304)),
            room((8, 256, 256)), room((8, 128), F32), room((2, 8, 128), F32), room((3, 4, 8, 128), F32),
        ]
        + lands
        + [
            dma((10, 3, 4)), dma((10, 3, 4)), dma((PARTS, 3, 4)), dma((PARTS, 3, 4)), pltpu.SemaphoreType.REGULAR((PARTS, 2)),
            dma((2,)), dma((10,)), dma((10,)), dma((10,)), dma((8,)), dma((8,)), dma((8,)), dma((4, 2)),
            dma((4, 4)), dma((4, 4)), dma((8,)), dma((8,)), dma((8,)), dma((4, 2)),
            dma((2,)), dma((2,)), dma((3, 3)), dma((3, 3)),
        ],
        name="whole_step",
        compiler_params=pltpu.CompilerParams(
            collective_id=0, has_side_effects=True, vmem_limit_bytes=64 * 1024 * 1024 - 65536
        ),
    )(*operands)


def finish_kernel(
    bo_ref, tok_ref, giw_ref, gow_ref, ggw_ref, guw_ref, gdw_ref, gains_ref, sums_ref,
    bo_out, loss_out, tok_out, ag_out, iw_out, qg_out, kg_out, ow_out, fg_out, gw_out, uw_out, dw_out,
):
    for src, dst in (
        (bo_ref, bo_out), (tok_ref, tok_out), (giw_ref, iw_out), (gow_ref, ow_out),
        (ggw_ref, gw_out), (guw_ref, uw_out), (gdw_ref, dw_out),
    ):
        dst[...] = src[...]
    qg_out[...] = sums_ref[0:1, 0:64]
    kg_out[...] = sums_ref[1:2, 0:64]
    loss_out[...] = sums_ref[2:3, 0:1]
    ag_out[...] = gains_ref[0:1, :]
    fg_out[...] = gains_ref[1:2, :]


def finish(*operands):
    def shape(dims, kind=F32):
        return jax.ShapeDtypeStruct(dims, kind)

    vmem = pl.BlockSpec(memory_space=pltpu.VMEM)
    return pl.pallas_call(
        finish_kernel,
        out_shape=(
            shape((2, 128, 1024), BF16), shape((1, 1)), shape((2, 128, 1024)), shape((1, 8)), shape((8, 2048)),
            shape((1, 64)), shape((1, 64)), shape((8, 1024)), shape((1, 8)), shape((8, 4608)), shape((8, 4608)),
            shape((8, 4608)),
        ),
        in_specs=[vmem] * 9,
        out_specs=(vmem,) * 12,
        name="finish",
    )(*operands)


def body(
    tokens, teacher, lengths, attention_gain, input_weight, query_gain, key_gain,
    output_weight, feed_gain, gate_weight, up_weight, down_weight,
):
    columns_in = jnp.pad(jnp.stack([attention_gain, feed_gain], axis=-1).astype(F32), ((0, 0), (0, 126)))
    rows_in = jnp.stack([query_gain, key_gain]).astype(F32)
    rows_in = jnp.pad(jnp.concatenate([rows_in, rows_in], axis=-1), ((0, 6), (0, 0)))
    freqs = np.float64(THETA) ** (-(2.0 * np.arange(32)) / 64)
    freqs = jnp.asarray(np.tile(freqs.astype(np.float32), 4)[None])
    (
        block_out, token_grads, input_grad, output_grad, gate_grad, up_grad, down_grad, gain_grads, sums,
    ) = step_call(
        lengths, tokens, teacher, input_weight, output_weight.T, gate_weight, up_weight, down_weight.T,
        columns_in, rows_in, freqs,
    )
    (
        block_out, loss, token_grads, attention_gain_grad, input_grad, query_gain_grad, key_gain_grad, output_grad,
        feed_gain_grad, gate_grad, up_grad, down_grad,
    ) = finish(
        block_out, token_grads, input_grad, output_grad, gate_grad, up_grad, down_grad, gain_grads, sums
    )
    return (
        block_out, loss.reshape(()), token_grads, attention_gain_grad.reshape(8), input_grad,
        query_gain_grad.reshape(64), key_gain_grad.reshape(64),
        output_grad.T, feed_gain_grad.reshape(8), gate_grad, up_grad, down_grad.T,
    )


def solution(mesh):
    tokens, split = P("fsdp", "seq", None), P(("fsdp", "seq"))
    rows, columns = P(("fsdp", "seq"), None), P(None, ("fsdp", "seq"))
    return jax.shard_map(
        body,
        mesh=mesh,
        in_specs=(
            tokens, tokens, P("fsdp"), split, rows, P(), P(), columns, split, rows, rows, columns,
        ),
        out_specs=(
            tokens, P(), tokens, split, rows, P(), P(), columns, split, rows, rows, columns,
        ),
        check_vma=False,
    )
```

```python
import functools
import math

import jax
import jax.numpy as jnp
import numpy as np
from jax import lax
from jax.experimental import pallas as pl
from jax.experimental.pallas import tpu as pltpu
from jax.sharding import PartitionSpec as P

EPS = 1e-05
THETA = 1000000.0
MESH = pl.DeviceIdType.MESH
F32 = jnp.float32
BF16 = jnp.bfloat16
LOG2E = 1.4426950408889634
HIGH = lax.Precision.HIGHEST
BLOCKS = (4, 2, 4, 2, 16)
PACKED = 8576
IN_AT, OUT_AT, UP_AT, GATE_AT, DOWN_AT = 0, 1152, 1664, 3968, 6272


class Place:
    def __init__(self):
        self.fsdp = lax.axis_index("fsdp")
        self.seq = lax.axis_index("seq")
        self.x = self.fsdp // 2
        self.zh = self.fsdp % 2
        self.y = self.seq // 4
        self.zl = (self.seq // 2) % 2
        self.core = self.seq % 2
        self.chip = self.seq // 2
        self.z = self.zh * 2 + self.zl
        self.here = (self.x, self.zh, self.y, self.zl)

    def sibling(self):
        return (self.fsdp, self.seq + 1 - 2 * self.core)

    def moved(self, axis, step):
        x, y, z = self.x, self.y, self.z
        if axis == "x":
            x = (x + step) % 4
        elif axis == "y":
            y = (y + step) % 4
        else:
            z = (z + step) % 4
        zh, zl = z // 2, z % 2
        return (x, zh, y, zl), (x * 2 + zh, y * 4 + zl * 2 + self.core)


def greet(place):
    barrier = pltpu.get_barrier_semaphore()
    for step in range(1, 16):
        pl.semaphore_signal(
            barrier, inc=1, device_id=(place.fsdp, (place.seq + step) % 16), device_id_type=MESH
        )
    for step in range(1, 4):
        pl.semaphore_signal(barrier, inc=1, device_id=place.moved("x", step)[1], device_id_type=MESH)
    other = place.x * 2 + 1 - place.zh
    for low in range(2):
        pl.semaphore_signal(
            barrier,
            inc=1,
            device_id=(other, place.y * 4 + low * 2 + place.core),
            device_id_type=MESH,
        )


def greeted():
    pl.semaphore_wait(pltpu.get_barrier_semaphore(), 20)


def axes_index(order, stage, here, where, cut=None, half=0):
    index = []
    for axis, mine, other in zip("xzyz", here, where):
        if axis in order[:stage]:
            index.append(mine)
        elif axis == order[stage]:
            index.append(other)
        else:
            index.append(pl.ds(2 * half, 2) if axis == cut else slice(None))
    return tuple(index)


def rest(order, stage, cut=None):
    sizes = (("x", 4), ("z", 2), ("y", 4), ("z", 2))
    return tuple(2 if axis == cut else size for axis, size in sizes if axis not in order[: stage + 1])


def accumulate(sizes, target, others):
    def one(step, carry):
        index, left = [], step
        for size in reversed(sizes):
            index.insert(0, left % size)
            left = left // size
        index = tuple(index)
        total = target[index].astype(F32)
        for other in others:
            total = total + other[index].astype(F32)
        target[index] = total.astype(BF16)
        return carry

    lax.fori_loop(0, math.prod(sizes), one, 0)


class Scatter:
    def __init__(self, place, part, order, ref, lanes, lands, sems, wide=None):
        self.place, self.part, self.order, self.ref, self.lanes = place, part, order, ref, lanes
        self.lands = lands
        self.send, self.recv, self.free = sems
        self.cut = "y" if order[0] == "x" else "x"
        self.wide = wide
        self.copies = {}

    def at(self, stage, where, half=None):
        cut = None if half is None else self.cut
        index = axes_index(self.order, stage, self.place.here, where, cut, half)
        return self.ref.at[index + (slice(None), self.lanes)]

    def step(self, stage, step, half=None):
        return self.at(stage, self.place.moved(self.order[stage], step)[0], half)

    def copy(self, stage, slot, step, src, dst):
        copy = pltpu.make_async_remote_copy(
            src_ref=src,
            dst_ref=dst,
            send_sem=self.send.at[self.part, stage, slot],
            recv_sem=self.recv.at[self.part, stage, slot],
            device_id=self.place.moved(self.order[stage], step)[1],
            device_id_type=MESH,
        )
        copy.start()
        self.copies[stage, slot] = copy

    def direct(self, stage):
        for slot, step in enumerate((1, 3, 2)):
            self.copy(stage, slot, step, self.step(stage, step), self.lands[stage].at[slot])

    def add(self, stage):
        for slot in range(3):
            self.copies[stage, slot].wait_recv()
        others = [self.lands[stage].at[slot] for slot in range(3)]
        accumulate(rest(self.order, stage), self.at(stage, self.place.here), others)

    def far(self):
        for slot, step in enumerate((1, 3)):
            self.copy(0, slot, step, self.step(0, 2, slot), self.lands[0].at[slot])

    def credit(self):
        for slot, step in enumerate((3, 1)):
            pl.semaphore_signal(
                self.free.at[self.part, slot],
                inc=1,
                device_id=self.place.moved(self.order[0], step)[1],
                device_id_type=MESH,
            )

    def near(self):
        for slot, step in enumerate((1, 3)):
            self.copies[0, slot].wait_recv()
            sizes = rest(self.order, 0, self.cut)
            accumulate(sizes, self.step(0, step, slot), [self.lands[0].at[slot]])
            pl.semaphore_wait(self.free.at[self.part, slot], 1)
            self.copy(0, 2 + slot, step, self.step(0, step), self.wide.at[slot])

    def own(self):
        for slot in range(2):
            self.copies[0, 2 + slot].wait_recv()
        accumulate(rest(self.order, 0), self.at(0, self.place.here), [self.wide.at[0], self.wide.at[1]])

    def final(self):
        total = self.at(2, self.place.here)[...].astype(F32)
        for slot in range(3):
            self.copies[2, slot].wait_recv()
            total = total + self.lands[2][slot].astype(F32)
        return total

    def sent(self):
        for copy in self.copies.values():
            copy.wait_send()


class Gather:
    def __init__(self, place, part, order, ref, lanes, send, recv):
        self.place, self.part, self.order, self.ref, self.lanes = place, part, order, ref, lanes
        self.send, self.recv = send, recv
        self.copies = {}

    def at(self, stage, where, half=None):
        index = []
        cut = "y" if self.order[2] == "x" else "x"
        for axis, value in zip("xzyz", where):
            if axis in self.order[:stage]:
                index.append(slice(None) if half is None or axis != cut else pl.ds(2 * half, 2))
            else:
                index.append(value)
        return self.ref.at[tuple(index) + (slice(None), self.lanes)]

    def copy(self, stage, slot, step, block):
        copy = pltpu.make_async_remote_copy(
            src_ref=block,
            dst_ref=block,
            send_sem=self.send.at[self.part, stage, slot],
            recv_sem=self.recv.at[self.part, stage, slot],
            device_id=self.place.moved(self.order[stage], step)[1],
            device_id_type=MESH,
        )
        copy.start()
        self.copies[stage, slot] = copy

    def direct(self, stage):
        for slot, step in enumerate((1, 3, 2)):
            self.copy(stage, slot, step, self.at(stage, self.place.here))

    def near(self):
        for slot, step in enumerate((1, 3)):
            self.copy(2, slot, step, self.at(2, self.place.here))

    def far(self):
        for slot, step in enumerate((1, 3)):
            self.copies[2, slot].wait_recv()
            self.copy(2, 2 + slot, step, self.at(2, self.place.moved(self.order[2], 4 - step)[0], slot))

    def arrived(self, stage):
        for (of, slot), copy in self.copies.items():
            if of == stage and not (stage == 2 and slot < 2 and (2, 3) in self.copies):
                copy.wait_recv()

    def sent(self):
        for copy in self.copies.values():
            copy.wait_send()


def lanes_of(rows):
    return lax.broadcasted_iota(jnp.int32, (rows, 128), 1)


def head_means(squares):
    left = lax.broadcasted_iota(jnp.int32, (128, 128), 0) // 64
    right = lax.broadcasted_iota(jnp.int32, (128, 128), 1) // 64
    mean = jnp.where(left == right, 1.0 / 64, 0.0).astype(F32)
    return lax.dot_general(
        squares, mean, (((1,), (0,)), ((), ())), precision=HIGH, preferred_element_type=F32
    )


def nt(left, right):
    return lax.dot_general(left, right, (((1,), (1,)), ((), ())), preferred_element_type=F32)


def nn(left, right):
    return lax.dot_general(left, right, (((1,), (0,)), ((), ())), preferred_element_type=F32)


def tn(left, right):
    return lax.dot_general(left, right, (((0,), (0,)), ((), ())), preferred_element_type=F32)


def turn(values, low_half):
    return jnp.where(low_half, pltpu.roll(values, 96, 1), pltpu.roll(values, 32, 1))


def columns(ref, start, width):
    return ref[:, :, :, :, :, pl.ds(start, width)].reshape(1024, width)


LOW, REST = 1024, 1280
GATHERED = (
    ("in", 0, 384, "xyz"), ("in", 384, 384, "yzx"), ("in", 768, 384, "zxy"), ("out", 0, 512, "yzx"),
    ("up", 0, 1152, "yzx"), ("up", 1152, 1152, "zyx"), ("gate", 0, LOW, "zxy"), ("gate", LOW, REST, "yxz"),
    ("down", 0, LOW, "xzy"), ("down", LOW, REST, "xyz"),
)
SCATTERED = (
    ("in", 0, 384, "xyz"), ("in", 384, 384, "yzx"), ("in", 768, 256, "zyx"), ("in", 1024, 128, "zyx"),
    ("out", 0, 512, "xyz"), ("up", 0, 1152, "xyz"), ("up", 1152, 1152, "xzy"),
    ("gate", 0, LOW, "yxz"), ("gate", LOW, REST, "zxy"), ("down", 0, LOW, "yxz"), ("down", LOW, REST, "zyx"),
)
PARTS = len(SCATTERED)
WIDE = 5
STARTS = {"in": 0, "out": 1152, "up": 1664, "gate": 3968, "down": 6272}


def step_kernel(
    len_ref, x_ref, t_ref, iw_ref, ow_ref, gw_ref, uw_ref, dw_ref, cols_ref, rows_ref, freq_ref,
    bo_ref, tok_ref, giw_ref, gow_ref, ggw_ref, guw_ref, gdw_ref, gcols_ref, total_ref,
    win_ref, wout_ref, up_ref, gate_ref, down_ref, w_ref, wr_ref, xp_ref, send_ref, qkv_ref,
    kk_ref, v0_ref, v1_ref, ob_ref, ot_ref, do_ref, oh_ref, lse_ref, dd_ref, mixed_ref, h1_ref, gains_ref,
    cos_ref, sin_ref, part_ref, part2_ref, ps_ref, pr0_ref, pr1_ref, h_ref, h2_ref, low_ref,
    acty_ref, actz_ref, dgy_ref, dgz_ref, du_ref, gr_ref, smalls_ref, pair_ref, ring_ref, *others,
):
    lands = [others[3 * i : 3 * i + 3] for i in range(PARTS)]
    (
        ag_send, ag_recv, rs_send, rs_recv, free_sem, w_sem, x_send, x_recv, x_own, q_send, q_recv, o_send, o_recv,
        p_send, p_recv, do_send, do_recv, g_send, g_recv, fin_sem, pair_sem, ring_send, ring_recv,
    ) = others[3 * PARTS :]
    place = Place()
    core, chip = place.core, place.chip
    greet(place)
    sibling = place.sibling()
    gathered = {"in": win_ref, "out": wout_ref, "up": up_ref, "gate": gate_ref, "down": down_ref}

    low_lanes = lanes_of(8) < 64
    for half in range(2):
        for kv in range(4):
            head = half * 4 + kv
            at = kv * 256
            w_ref[half, :, pl.ds(at, 128)] = iw_ref[:, pl.ds(head * 128, 128)].astype(F32)
            keys = iw_ref[:, pl.ds(1024 + head // 2 * 128, 128)].astype(F32)
            values = iw_ref[:, pl.ds(1536 + head // 2 * 128, 128)].astype(F32)
            if head % 2 == 0:
                both = jnp.where(low_lanes, keys, pltpu.roll(values, 64, 1))
            else:
                both = jnp.where(low_lanes, pltpu.roll(keys, 64, 1), values)
            w_ref[half, :, pl.ds(at + 128, 128)] = both
        w_ref[half, :, pl.ds(1024, 128)] = cols_ref[...]
        w_ref[half, :, pl.ds(STARTS["out"], 512)] = ow_ref[:, pl.ds(half * 512, 512)].astype(F32)
        for name, ref in (("up", uw_ref), ("gate", gw_ref), ("down", dw_ref)):
            w_ref[half, :, pl.ds(STARTS[name], 2304)] = ref[:, pl.ds(half * 2304, 2304)].astype(F32)
    greeted()

    def to_sibling(src, dst, send, recv):
        copy = pltpu.make_async_remote_copy(
            src_ref=src, dst_ref=dst, send_sem=send, recv_sem=recv, device_id=sibling, device_id_type=MESH
        )
        copy.start()
        return copy

    w_copy = to_sibling(w_ref.at[1 - core], wr_ref, w_sem.at[0], w_sem.at[1])
    ends = [(x_ref.at[seq], xp_ref.at[seq, core]) for seq in range(2)]
    for seq in range(2):
        for tile in range(4):
            slab = gr_ref.at[(seq * 2 + core) * 2 + tile // 2, pl.ds(tile % 2 * 128, 128), :]
            ends.append((t_ref.at[seq, :, pl.ds(tile * 256, 256)], slab))
    pair_copies, own_copies = [], []
    for n, (src, dst) in enumerate(ends):
        pair_copies.append(to_sibling(src, dst, x_send.at[n], x_recv.at[n]))
        copy = pltpu.make_async_copy(src, dst, x_own.at[n])
        copy.start()
        own_copies.append(copy)

    gathers = [
        Gather(place, i, order, gathered[name], pl.ds(start, width), ag_send, ag_recv)
        for i, (name, start, width, order) in enumerate(GATHERED)
    ]
    mixing, output, ups, gates, downs = gathers[:3], gathers[3], gathers[4:6], gathers[6:8], gathers[8:]
    early = ups + gates

    w_copy.wait_recv()
    first = jnp.where(core == 0, 1.0, 0.0).astype(F32)
    for name, width in (("in", 1152), ("out", 512), ("up", 2304), ("gate", 2304), ("down", 2304)):
        lanes = pl.ds(STARTS[name], width)
        mine = w_ref[core, :, lanes]
        theirs = wr_ref[:, lanes]
        above = jnp.where(first > 0.5, mine, theirs)
        below = jnp.where(first > 0.5, theirs, mine)
        gathered[name][place.here] = jnp.concatenate([above, below], axis=0).astype(BF16)
        if name == "in":
            for item in mixing:
                item.direct(0)
    for item in early + [output] + downs:
        item.direct(0)
    for item in mixing:
        item.arrived(0)
        item.direct(1)
    for item in early + [output]:
        item.arrived(0)
        item.direct(1)

    slots = chip * 256 + lax.broadcasted_iota(jnp.int32, (256, 128), 0)
    angles = slots.astype(F32) * freq_ref[...]
    cos_ref[...] = jnp.cos(angles)
    sine = jnp.sin(angles)
    low_half = lanes_of(256) % 64 < 32
    first_head = lanes_of(256) < 64
    sin_ref[...] = jnp.where(low_half, -sine, sine)

    for item in mixing:
        item.arrived(1)
        item.direct(2)
    for item in downs:
        item.arrived(0)
        item.direct(1)
    output.arrived(1)
    output.direct(2)
    for item in early:
        item.arrived(1)
        item.near()
    for n in range(2):
        pair_copies[n].wait_recv()
        own_copies[n].wait()
    for item in mixing:
        item.arrived(2)

    gains_ref[...] = jnp.transpose(columns(win_ref, 1024, 128).astype(F32))[:8]

    def first_norm(step, carry):
        seq, half = step // 4, (step // 2) % 2
        rows = pl.ds((step % 2) * 64, 64)
        inputs = xp_ref[seq, half, rows, :].astype(F32)
        scale = lax.rsqrt(jnp.mean(inputs * inputs, axis=-1, keepdims=True) + EPS)
        h1_ref[pl.ds(step * 64, 64), :] = (inputs * scale * gains_ref[0:1, :]).astype(BF16)
        return carry

    lax.fori_loop(0, 8, first_norm, 0)

    def to_heads(slot, src_ref, dst_ref, send, recv):
        target = (4 * core + slot // 2) * 2 + slot % 2
        return target, pltpu.make_async_remote_copy(
            src_ref=src_ref.at[slot],
            dst_ref=dst_ref.at[chip],
            send_sem=send.at[slot],
            recv_sem=recv.at[chip],
            device_id=(place.fsdp, target),
            device_id_type=MESH,
        ), pltpu.make_async_copy(src_ref.at[slot], dst_ref.at[chip], recv.at[chip])

    def to_tokens(block, src_ref, dst_ref, send, recv):
        target = block * 2 + chip // 4
        return target, pltpu.make_async_remote_copy(
            src_ref=src_ref.at[block],
            dst_ref=dst_ref.at[chip % 4 * 2 + core],
            send_sem=send.at[block],
            recv_sem=recv.at[chip % 4, core],
            device_id=(place.fsdp, target),
            device_id_type=MESH,
        ), pltpu.make_async_copy(src_ref.at[block], dst_ref.at[chip % 4 * 2 + core], recv.at[chip % 4, core])

    def start_either(target, remote, local):
        @pl.when(target != place.seq)
        def _():
            remote.start()

        @pl.when(target == place.seq)
        def _():
            local.start()

    def sent_either(target, remote, local):
        @pl.when(target != place.seq)
        def _():
            remote.wait_send()

    q_refs = (send_ref, qkv_ref, q_send, q_recv)
    o_refs = (ob_ref, ot_ref, o_send, o_recv)
    do_refs = (ob_ref, do_ref, do_send, do_recv)
    g_refs = (send_ref, gr_ref, g_send, g_recv)

    for kv in range(4):
        weights = columns(win_ref, kv * 256, 256)

        def project(seq, carry, kv=kv, weights=weights):
            rows = pl.ds(pl.multiple_of(seq * 256, 256), 256)
            raw = nn(h1_ref[rows, :], weights)
            mixed_ref[kv, rows, :] = raw
            query, other = raw[:, :128], raw[:, 128:]
            query_norm = query * lax.rsqrt(head_means(query * query) + EPS) * rows_ref[0:1, :]
            other_norm = other * lax.rsqrt(head_means(other * other) + EPS) * rows_ref[1:2, :]
            query_rot = query_norm * cos_ref[...] + turn(query_norm, low_half) * sin_ref[...]
            other_rot = other_norm * cos_ref[...] + turn(other_norm, low_half) * sin_ref[...]
            slot = kv * 2 + seq
            send_ref[slot, :, 0:128] = query_rot.astype(BF16)
            send_ref[slot, :, 128:256] = jnp.where(first_head, other_rot, other).astype(BF16)
            start_either(*to_heads(slot, *q_refs))
            return carry

        lax.fori_loop(0, 2, project, 0)

    for item in gates:
        item.far()

    length = len_ref[core]
    factor = LOG2E / 8.0
    head_row = lax.broadcasted_iota(jnp.int32, (8, 128), 0)
    head_lane = lax.broadcasted_iota(jnp.int32, (8, 128), 1)
    pick = jnp.where(head_lane == head_row * 64, 1.0, 0.0).astype(F32)
    spread = jnp.where(head_lane // 64 == head_row, 1.0, 0.0).astype(F32)

    def nt_high(left, right):
        return lax.dot_general(
            left, right, (((1,), (1,)), ((), ())), precision=HIGH, preferred_element_type=F32
        )

    wide_row = lax.broadcasted_iota(jnp.int32, (256, 1024), 0)
    wide_column = lax.broadcasted_iota(jnp.int32, (256, 1024), 1)

    for ref in (kk_ref, v0_ref, v1_ref):
        ref[...] = jnp.zeros_like(ref)

    def attend(block, ranges):
        pltpu.make_async_copy(qkv_ref.at[block], qkv_ref.at[block], q_recv.at[block]).wait()
        other = qkv_ref[block, :, 128:256].astype(F32)
        swapped = pltpu.roll(other, 64, 1)
        there = block * 256 + lax.broadcasted_iota(jnp.int32, (256, 128), 0) < length
        kk_ref[block] = jnp.where(first_head, other, swapped).astype(BF16)
        v0_ref[block] = jnp.where(there, jnp.where(first_head, swapped, 1.0), 0.0).astype(BF16)
        v1_ref[block] = jnp.where(there, jnp.where(first_head, 1.0, other), 0.0).astype(BF16)
        query = qkv_ref[block, :, 0:128]
        nothing = jnp.zeros_like(query)
        sums = []
        for query_h, values in (
            (jnp.where(first_head, query, nothing), v0_ref),
            (jnp.where(first_head, nothing, query), v1_ref),
        ):
            total = jnp.zeros((256, 128), F32)
            for low, high, masked in ranges:
                size = (high - low) * 256
                weights = jnp.exp2(nt(query_h, kk_ref[low:high].reshape(size, 128)) * factor)
                if masked:
                    weights = jnp.where(wide_column - wide_row <= (block - low) * 256, weights, 0.0)
                total = total + nn(weights.astype(BF16), values[low:high].reshape(size, 128))
            sums.append(total)
        sum0, sum1 = sums
        total = jnp.where(first_head, pltpu.roll(sum0, 64, 1), pltpu.roll(sum1, 64, 1))
        mixed = jnp.where(first_head, sum0, sum1) / total
        oh_ref[block] = mixed
        lse_ref[:, pl.ds(pl.multiple_of(block * 256, 256), 256)] = jnp.log2(jnp.maximum(nt_high(pick, total), 1e-30))
        ob_ref[block] = mixed.astype(BF16)
        start_either(*to_tokens(block, *o_refs))

    def early_queries(block, carry):
        attend(block, ((0, 4, True),))
        return carry

    def late_queries(block, carry):
        attend(block, ((0, 4, False), (4, 8, True)))
        return carry

    lax.fori_loop(0, 4, early_queries, 0)
    lax.fori_loop(4, 8, late_queries, 0)

    for item in downs:
        item.arrived(1)
        item.near()
    ups[0].far()
    output.arrived(2)
    for slot in range(8):
        pltpu.make_async_copy(ot_ref.at[slot], ot_ref.at[slot], o_recv.at[slot // 2, slot % 2]).wait()
    attended = jnp.concatenate([ot_ref[2 * kv : 2 * kv + 2].reshape(512, 128) for kv in range(4)], axis=1)

    def send_part(tile, landing, number):
        return pltpu.make_async_remote_copy(
            src_ref=ps_ref.at[tile],
            dst_ref=landing.at[tile],
            send_sem=p_send.at[number, tile],
            recv_sem=p_recv.at[number, tile],
            device_id=sibling,
            device_id_type=MESH,
        )

    def share(tile, part, keep, landing, number):
        keep[tile] = part
        ps_ref[tile] = part.astype(BF16)
        send_part(tile, landing, number).start()

    def shared(landing, number):
        for tile in range(4):
            send_part(tile, landing, number).wait()

    for tile in range(4):
        share(tile, nt(attended, wout_ref[tile].reshape(256, 512)), part_ref, pr0_ref, 0)
    ups[1].far()
    shared(pr0_ref, 0)

    def paired(rows, keep, landing):
        return jnp.concatenate(
            [keep[tile, rows, :] + landing[tile, rows, :].astype(F32) for tile in range(4)], axis=1
        )

    def second_norm(step, carry):
        seq, half = step // 8, (step // 4) % 2
        inputs = xp_ref[seq, half, pl.ds((step % 4) * 32, 32), :].astype(F32)
        rows = pl.ds(step * 32, 32)
        resid = paired(rows, part_ref, pr0_ref) + inputs
        scale = lax.rsqrt(jnp.mean(resid * resid, axis=-1, keepdims=True) + EPS)
        h_ref[rows, :] = resid
        h2_ref[rows, :] = (resid * scale * gains_ref[1:2, :]).astype(BF16)
        return carry

    lax.fori_loop(0, 16, second_norm, 0)

    for item in ups + gates:
        item.arrived(2)

    def tiles(function, after=lambda n: None):
        def low_tile(tile, carry):
            at = pl.multiple_of(tile * 256, 256)
            return function(at, acty_ref, dgy_ref, at, (2, 4, 2, 2, 16, 256), (slice(None),) * 5)

        def rest_tile(tile, carry):
            at = pl.multiple_of(tile * 256, 256)
            at_all = pl.multiple_of(tile * 256 + LOW, 256)
            return function(at_all, actz_ref, dgz_ref, at, (2, 4, 4, 16, 256), (slice(None),) * 4)

        lax.fori_loop(0, LOW // 256, low_tile, 0)
        after(0)
        lax.fori_loop(0, REST // 256, rest_tile, 0)
        after(1)

    whole = (slice(None),) * 5
    du_shape = (2, 2, 4, 2, 16, 256)

    def feed(at, act, dg, at_part, dims, full):
        lanes, lanes_part = pl.ds(at, 256), pl.ds(at_part, 256)
        up = nn(h2_ref[...], columns(up_ref, at, 256))
        gate = nn(h2_ref[...], columns(gate_ref, at, 256))
        sigma = jax.nn.sigmoid(gate)
        silu = gate * sigma
        act[full + (lanes_part,)] = (silu * up).astype(BF16).reshape(dims)
        dg[full + (lanes_part,)] = (up * sigma * (1.0 + gate * (1.0 - sigma))).astype(BF16).reshape(dims)
        du_ref[whole + (lanes,)] = silu.astype(BF16).reshape(du_shape)
        return 0

    tiles(feed, lambda n: downs[n].far())
    for item in downs:
        item.arrived(2)

    def lower(tile, carry):
        weights = down_ref[tile].reshape(256, 2304)
        part = nt(acty_ref[...].reshape(512, LOW), weights[:, :LOW])
        part = part + nt(actz_ref[...].reshape(512, REST), weights[:, LOW:])
        share(tile, part, part_ref, pr1_ref, 1)
        return carry

    lax.fori_loop(0, 4, lower, 0)
    for n in range(2, 10):
        pair_copies[n].wait_recv()
        own_copies[n].wait()

    def errors(step, carry, tile):
        squares, counted = carry
        seq, half = step // 2, step % 2
        rows = pl.ds(pl.multiple_of(step * 128, 128), 128)
        lanes = pl.ds(tile * 256, 256)
        final = h_ref[rows, lanes] + part_ref[tile, rows, :] + pr1_ref[tile, rows, :].astype(F32)
        slot = chip * 256 + half * 128 + lax.broadcasted_iota(jnp.int32, (128, 256), 0)
        valid = jnp.where(slot < len_ref[seq], 1.0, 0.0).astype(F32)
        teacher = gr_ref[(seq * 2 + half) * 2 + tile // 2, pl.ds(tile % 2 * 128, 128), :].astype(F32)
        diff = (final - teacher) * valid
        low_ref[rows, lanes] = diff.astype(BF16)
        part_ref[tile, rows, :] = diff

        @pl.when(half == core)
        def _():
            bo_ref[seq, :, lanes] = final.astype(BF16)

        mine = jnp.where(half == core, 1.0, 0.0)
        squares = squares + mine * jnp.sum(diff * diff, axis=0, keepdims=True)
        counted = counted + mine * jnp.sum(valid[:, :128], axis=0, keepdims=True)
        return squares, counted

    sums = (jnp.zeros((1, 256), F32), jnp.zeros((1, 128), F32))
    for tile in range(4):
        send_part(tile, pr1_ref, 1).wait()
        sums = lax.fori_loop(0, 4, functools.partial(errors, tile=tile), sums)
    folded, counted = sums[0][:, :128] + sums[0][:, 128:], sums[1] * 0.25
    smalls_ref[...] = jnp.concatenate(
        [jnp.zeros((2, 128), F32), folded, counted, jnp.zeros((4, 128), F32)], axis=0
    )
    w_copy.wait_send()
    for item in gathers:
        item.sent()

    wides = {
        5: du_ref.at[:, :, :, :, :, pl.ds(0, 1152)], 6: du_ref.at[:, :, :, :, :, pl.ds(1152, 1152)],
        7: dgy_ref, 8: dgz_ref, 9: acty_ref, 10: actz_ref,
    }
    scatters = [
        Scatter(
            place, i, order, gathered[name], pl.ds(start, width), lands[i], (rs_send, rs_recv, free_sem), wides.get(i)
        )
        for i, (name, start, width, order) in enumerate(SCATTERED)
    ]
    mix_s, gain_s, out_s = scatters[:3], scatters[3], scatters[4]
    up_s, gate_s, down_s = scatters[5:7], scatters[7:9], scatters[9:]

    def raise_back(at, act, dg, at_part, dims, full):
        lanes, lanes_part = pl.ds(at, 256), pl.ds(at_part, 256)
        grad_act = nn(low_ref[...], columns(down_ref, at, 256))
        dg_at, du_at = full + (lanes_part,), whole + (lanes,)
        dg[dg_at] = (grad_act * dg[dg_at].reshape(512, 256).astype(F32)).astype(BF16).reshape(dims)
        du_ref[du_at] = (grad_act * du_ref[du_at].reshape(512, 256).astype(F32)).astype(BF16).reshape(du_shape)
        grad = tn(low_ref[...], act[full + (lanes_part,)].reshape(512, 256))
        down_ref[whole + (lanes,)] = grad.astype(BF16).reshape(BLOCKS + (256,))
        return 0

    def round_first(items):
        def start(n):
            if n < len(items):
                items[n].credit()
                items[n].far()

        return start

    tiles(raise_back, round_first(down_s))

    def feed_back(tile, carry):
        weights = gate_ref[tile].reshape(256, 2304)
        part = nt(dgy_ref[...].reshape(512, LOW), weights[:, :LOW])
        part = part + nt(dgz_ref[...].reshape(512, REST), weights[:, LOW:])
        part = part + nt(du_ref[...].reshape(512, 2304), up_ref[tile].reshape(256, 2304))
        share(tile, part, part2_ref, pr0_ref, 2)
        return carry

    lax.fori_loop(0, 4, feed_back, 0)

    def up_grads(tile, carry):
        lanes = pl.ds(pl.multiple_of(tile * 256, 256), 256)
        grad = tn(h2_ref[...], du_ref[whole + (lanes,)].reshape(512, 256))
        up_ref[whole + (lanes,)] = grad.astype(BF16).reshape(BLOCKS + (256,))
        return carry

    lax.fori_loop(0, 9, up_grads, 0)
    for item in up_s:
        item.credit()
        item.far()
    shared(pr0_ref, 2)

    def second_back(step, carry):
        seq, half, at = step // 8, (step // 4) % 2, pl.ds((step % 4) * 32, 32)
        rows = pl.ds(step * 32, 32)
        grad = paired(rows, part2_ref, pr0_ref)
        diff = jnp.concatenate([part_ref[tile, rows, :] for tile in range(4)], axis=1)
        resid = h_ref[rows, :]
        scale = lax.rsqrt(jnp.mean(resid * resid, axis=-1, keepdims=True) + EPS)
        inner = grad * gains_ref[1:2, :]
        mean = jnp.mean(inner * resid, axis=-1, keepdims=True)
        result = diff + scale * inner - resid * (scale * scale * scale) * mean
        low_ref[rows, :] = result.astype(BF16)

        @pl.when(half == core)
        def _():
            tok_ref[seq, at, :] = result

        return carry + jnp.sum(grad * resid * scale, axis=0, keepdims=True)

    feed_sum = lax.fori_loop(0, 16, second_back, jnp.zeros((1, 1024), F32))

    for slot in range(8):
        sent_either(*to_heads(slot, *q_refs))
    for block in range(8):
        sent_either(*to_tokens(block, *o_refs))
    for kv in range(4):
        grad = nn(low_ref[...], columns(wout_ref, kv * 128, 128)).astype(BF16)
        for seq in range(2):
            ob_ref[kv * 2 + seq] = grad[seq * 256 : seq * 256 + 256]
            start_either(*to_heads(kv * 2 + seq, *do_refs))
    for item in down_s:
        item.near()
    for kv in range(4):
        grad = tn(low_ref[...], ot_ref[2 * kv : 2 * kv + 2].reshape(512, 128))
        wout_ref[whole + (pl.ds(kv * 128, 128),)] = grad.astype(BF16).reshape(BLOCKS + (128,))
    out_s.direct(0)

    def gate_grads(at, act, dg, at_part, dims, full):
        grad = tn(h2_ref[...], dg[full + (pl.ds(at_part, 256),)].reshape(512, 256))
        gate_ref[whole + (pl.ds(at, 256),)] = grad.astype(BF16).reshape(BLOCKS + (256,))
        return 0

    tiles(gate_grads, round_first(gate_s))

    rhs = (kk_ref, v0_ref, v1_ref, ot_ref)

    def prepare(block, carry):
        pltpu.make_async_copy(do_ref.at[block], do_ref.at[block], do_recv.at[block]).wait()
        query = qkv_ref[block, :, 0:128].astype(F32)
        grad = do_ref[block].astype(F32)
        zero = jnp.zeros_like(query)
        dd_ref[:, pl.ds(pl.multiple_of(block * 256, 256), 256)] = nt_high(spread, grad * oh_ref[block])
        kk_ref[block] = jnp.where(first_head, query, zero).astype(BF16)
        v0_ref[block] = jnp.where(first_head, pltpu.roll(query, 64, 1), zero).astype(BF16)
        v1_ref[block] = jnp.where(first_head, zero, pltpu.roll(grad, 64, 1)).astype(BF16)
        ot_ref[block] = jnp.where(first_head, zero, grad).astype(BF16)
        oh_ref[block] = zero
        return carry

    lax.fori_loop(0, 8, prepare, 0)
    for item in up_s:
        item.near()

    def attend_back(key_block, ranges):
        other = qkv_ref[key_block, :, 128:256].astype(F32)
        swapped = pltpu.roll(other, 64, 1)
        zero = jnp.zeros_like(other)
        keys0 = jnp.where(first_head, other, zero).astype(BF16)
        keys1 = jnp.where(first_head, zero, swapped).astype(BF16)
        values0 = jnp.where(first_head, swapped, zero).astype(BF16)
        values1 = jnp.where(first_head, zero, other).astype(BF16)
        keys = jnp.concatenate([keys0, keys1], axis=0)
        total = zero
        for low, high, masked in ranges:
            size = (high - low) * 256
            lanes = slice(low * 256, high * 256)
            query = qkv_ref[low:high, :, 0:128].reshape(size, 128)
            grad = do_ref[low:high].reshape(size, 128)
            chances, grads = [], []
            for head, keys_h, values_h in ((0, keys0, values0), (1, keys1, values1)):
                chance = jnp.exp2(nt(keys_h, query) * factor - lse_ref[head : head + 1, lanes])
                if masked:
                    chance = jnp.where(wide_row - wide_column <= (low - key_block) * 256, chance, 0.0)
                inner = nt(values_h, grad) - dd_ref[head : head + 1, lanes]
                chances.append(chance.astype(BF16))
                grads.append((chance * inner).astype(BF16))
            for left, ref in zip(grads + chances, rhs):
                total = total + nn(left, ref[low:high].reshape(size, 128))
            query_grad = tn(jnp.concatenate(grads, axis=0), keys)
            for block in range(low, high):
                at = (block - low) * 256
                oh_ref[block] = oh_ref[block] + query_grad[at : at + 256]
        send_ref[key_block, :, 0:128] = (oh_ref[key_block] * 0.125).astype(BF16)
        send_ref[key_block, :, 128:256] = jnp.where(first_head, total * 0.125, total).astype(BF16)
        start_either(*to_tokens(key_block, *g_refs))

    def early_keys(key_block, carry):
        attend_back(key_block, ((0, 4, True), (4, 8, False)))
        return carry

    def late_keys(key_block, carry):
        attend_back(key_block, ((4, 8, True),))
        return carry

    lax.fori_loop(0, 4, early_keys, 0)
    for item in down_s:
        item.own()
        item.direct(1)
    out_s.add(0)
    out_s.direct(1)
    lax.fori_loop(4, 8, late_keys, 0)
    for item in gate_s:
        item.near()

    for kv in range(4):
        for seq in range(2):
            landed = gr_ref.at[kv * 2 + seq]
            pltpu.make_async_copy(landed, landed, g_recv.at[kv, seq]).wait()

        def back(seq, carry, kv=kv):
            rows = pl.ds(pl.multiple_of(seq * 256, 256), 256)
            raws = mixed_ref[kv, rows, :]
            grads = gr_ref[kv * 2 + seq].astype(F32)
            results = []
            for part in range(2):
                lanes = slice(part * 128, part * 128 + 128)
                raw, grad = raws[:, lanes], grads[:, lanes]
                scale = lax.rsqrt(head_means(raw * raw) + EPS)
                grad_norm = grad * cos_ref[...] + turn(grad * sin_ref[...], low_half)
                gain_sum = jnp.sum(grad_norm * raw * scale, axis=0, keepdims=True)
                smalls_ref[part : part + 1, :] = smalls_ref[part : part + 1, :] + gain_sum
                inner = grad_norm * rows_ref[part : part + 1, :]
                result = scale * inner - raw * (scale * scale * scale) * head_means(inner * raw)
                if part == 1:
                    result = jnp.where(first_head, result, grad)
                results.append(result)
            h2_ref[rows, pl.ds(kv * 256, 256)] = jnp.concatenate(results, axis=1).astype(BF16)
            return carry

        lax.fori_loop(0, 2, back, 0)

    def mix_grads(kv, carry):
        at = pl.multiple_of(kv * 256, 256)
        grad = tn(h1_ref[...], h2_ref[:, pl.ds(at, 256)])
        win_ref[whole + (pl.ds(at, 256),)] = grad.astype(BF16).reshape(BLOCKS + (256,))
        return carry

    def mix_back(tile, carry):
        weights = win_ref[tile, :, :, :, :, pl.ds(0, 1024)].reshape(256, 1024)
        share(tile, nt(h2_ref[...], weights), part2_ref, pr1_ref, 3)
        return carry

    lax.fori_loop(0, 4, mix_back, 0)
    lax.fori_loop(0, 4, mix_grads, 0)
    for item in mix_s:
        item.direct(0)
    for item in up_s:
        item.own()
        item.direct(1)
    shared(pr1_ref, 3)

    def last(step, carry):
        seq, at = step // 4, (step % 4) * 32
        rows = pl.ds(seq * 256 + core * 128 + at, 32)
        at = pl.ds(at, 32)
        inputs = xp_ref[seq, core, at, :].astype(F32)
        scale = lax.rsqrt(jnp.mean(inputs * inputs, axis=-1, keepdims=True) + EPS)
        grad = paired(rows, part2_ref, pr1_ref)
        inner = grad * gains_ref[0:1, :]
        mean = jnp.mean(inner * inputs, axis=-1, keepdims=True)
        tok_ref[seq, at, :] = tok_ref[seq, at, :] + scale * inner - inputs * (scale * scale * scale) * mean
        return carry + jnp.sum(grad * inputs * scale, axis=0, keepdims=True)

    gain_grad = lax.fori_loop(0, 8, last, jnp.zeros((1, 1024), F32))
    both = jnp.concatenate([gain_grad, feed_sum, jnp.zeros((126, 1024), F32)], axis=0)
    win_ref[whole + (pl.ds(1024, 128),)] = jnp.transpose(both).astype(BF16).reshape(BLOCKS + (128,))
    gain_s.direct(0)

    pair_ref[core] = smalls_ref[...]
    pair_copy = to_sibling(smalls_ref, pair_ref.at[core], pair_sem.at[0], pair_sem.at[1])

    def ring_start(stage, value):
        axis = "xyz"[stage]
        here = {"x": place.x, "y": place.y, "z": place.z}[axis]
        ring_ref[stage, here] = value
        copies = []
        for step in (1, 3, 2):
            copy = pltpu.make_async_remote_copy(
                src_ref=ring_ref.at[stage, here],
                dst_ref=ring_ref.at[stage, here],
                send_sem=ring_send.at[stage, step - 1],
                recv_sem=ring_recv.at[stage, step - 1],
                device_id=place.moved(axis, step)[1],
                device_id_type=MESH,
            )
            copy.start()
            copies.append(copy)
        return copies

    def ring_sum(stage, copies):
        for copy in copies:
            copy.wait_recv()
        total = ring_ref[stage, 0]
        for other in range(1, 4):
            total = total + ring_ref[stage, other]
        return total

    pair_copy.wait_recv()
    rings = [ring_start(0, pair_ref[0] + pair_ref[1])]

    for item in gate_s:
        item.own()
        item.direct(1)
    for item in mix_s:
        item.add(0)
        item.direct(1)
    for item in [out_s] + down_s:
        item.add(1)
        item.direct(2)
    gain_s.add(0)
    gain_s.direct(1)
    rings.append(ring_start(1, ring_sum(0, rings[0])))
    for item in mix_s:
        item.add(1)
        item.direct(2)
    for item in [gain_s] + up_s + gate_s:
        item.add(1)
        item.direct(2)
    rings.append(ring_start(2, ring_sum(1, rings[1])))

    for i, (name, start, width, _) in reversed(list(enumerate(SCATTERED))):
        w_ref[:, :, pl.ds(STARTS[name] + start, width)] = scatters[i].final().reshape(2, 8, width)
    fin_copy = to_sibling(w_ref.at[1 - core], wr_ref, fin_sem.at[0], fin_sem.at[1])

    sums = ring_sum(2, rings[2])
    query_sum, key_sum, loss_sum, count = sums[0:1], sums[1:2], sums[2:3], sums[3:4]
    loss = jnp.sum(loss_sum, axis=1, keepdims=True) / (count * 1024.0)
    total_ref[...] = jnp.concatenate(
        [query_sum + pltpu.roll(query_sum, 64, 1), key_sum, loss, jnp.zeros((5, 128), F32)], axis=0
    )

    fin_copy.wait_recv()
    first = jnp.where(core == 0, 1.0, 0.0).astype(F32)

    def half_of(half, at, width):
        mine, theirs = w_ref[core, :, pl.ds(at, width)], wr_ref[:, pl.ds(at, width)]
        return jnp.where(first > 0.5, mine, theirs) if half == 0 else jnp.where(first > 0.5, theirs, mine)

    for half in range(2):
        gow_ref[:, pl.ds(half * 512, 512)] = half_of(half, STARTS["out"], 512)
        for name, ref in (("up", guw_ref), ("gate", ggw_ref), ("down", gdw_ref)):
            ref[:, pl.ds(half * 2304, 2304)] = half_of(half, STARTS[name], 2304)
        pairs = [half_of(half, kv * 256, 256) for kv in range(4)]
        for kv in range(4):
            giw_ref[:, pl.ds((half * 4 + kv) * 128, 128)] = pairs[kv][:, :128]
        for pair in range(2):
            even, odd = pairs[2 * pair][:, 128:], pairs[2 * pair + 1][:, 128:]
            at = (half * 2 + pair) * 128
            giw_ref[:, pl.ds(1024 + at, 128)] = jnp.where(low_lanes, even, pltpu.roll(odd, 64, 1))
            giw_ref[:, pl.ds(1536 + at, 128)] = jnp.where(low_lanes, pltpu.roll(even, 64, 1), odd)
    cols0, cols1 = w_ref[core, :, pl.ds(1024, 128)], wr_ref[:, pl.ds(1024, 128)]
    gain_columns = jnp.where(lanes_of(8) == 0, cols0 + cols1, cols0)
    gcols_ref[...] = nt_high(jnp.where(head_lane == head_row, 1.0, 0.0).astype(F32), gain_columns)

    for copy in [fin_copy, pair_copy] + pair_copies:
        copy.wait_send()
    for copies in rings:
        for copy in copies:
            copy.wait_send()
    for slot in range(8):
        sent_either(*to_heads(slot, *do_refs))
        sent_either(*to_tokens(slot, *g_refs))
    for item in scatters:
        item.sent()


def step_call(*operands):
    any_space = pl.BlockSpec(memory_space=pl.ANY)
    vmem = pl.BlockSpec(memory_space=pltpu.VMEM)
    smem = pl.BlockSpec(memory_space=pltpu.SMEM)

    def shape(dims, kind=F32):
        return jax.ShapeDtypeStruct(dims, kind)

    def room(dims, kind=BF16):
        return pltpu.VMEM(dims, kind)

    dma = pltpu.SemaphoreType.DMA
    lands = []
    for i, (_, _, n, order) in enumerate(SCATTERED):
        cut = "y" if order[0] == "x" else "x"
        if i < WIDE:
            lands.append(room((3,) + rest(order, 0) + (16, n)))
        else:
            lands.append(room((2,) + rest(order, 0, cut) + (16, n)))
        lands += [room((3,) + rest(order, 1) + (16, n)), room((3, 16, n))]
    heads, tokens = (8, 256, 128), (2, 2, 128, 1024)
    return pl.pallas_call(
        step_kernel,
        out_shape=(
            shape((2, 128, 1024), BF16), shape((2, 128, 1024)), shape((8, 2048)), shape((8, 1024)),
            shape((8, 4608)), shape((8, 4608)), shape((8, 4608)), shape((8, 8)), shape((8, 128)),
        ),
        in_specs=[smem, any_space, any_space] + [vmem] * 8,
        out_specs=(vmem,) * 9,
        scratch_shapes=[
            room(BLOCKS + (1152,)), room(BLOCKS + (512,)),
            room(BLOCKS + (2304,)), room(BLOCKS + (2304,)), room(BLOCKS + (2304,)),
            room((2, 8, PACKED), F32), room((8, PACKED), F32), room(tokens),
            room((8, 256, 256)), room((8, 256, 256)),
            room(heads), room(heads), room(heads), room(heads), room(heads), room(heads),
            room(heads, F32), room((8, 2048), F32), room((8, 2048), F32),
            room((4, 512, 256), F32), room((512, 1024)), room((8, 1024), F32), room((256, 128), F32), room((256, 128), F32),
            room((4, 512, 256), F32), room((4, 512, 256), F32), room((4, 512, 256)),
            room((4, 512, 256)), room((4, 512, 256)),
            room((512, 1024), F32), room((512, 1024)), room((512, 1024)),
            room((2, 4, 2, 2, 16, LOW)), room((2, 4, 4, 16, REST)),
            room((2, 4, 2, 2, 16, LOW)), room((2, 4, 4, 16, REST)), room((2, 2, 4, 2, 16, 2304)),
            room((8, 256, 256)), room((8, 128), F32), room((2, 8, 128), F32), room((3, 4, 8, 128), F32),
        ]
        + lands
        + [
            dma((10, 3, 4)), dma((10, 3, 4)), dma((PARTS, 3, 4)), dma((PARTS, 3, 4)), pltpu.SemaphoreType.REGULAR((PARTS, 2)),
            dma((2,)), dma((10,)), dma((10,)), dma((10,)), dma((8,)), dma((8,)), dma((8,)), dma((4, 2)),
            dma((4, 4)), dma((4, 4)), dma((8,)), dma((8,)), dma((8,)), dma((4, 2)),
            dma((2,)), dma((2,)), dma((3, 3)), dma((3, 3)),
        ],
        name="whole_step",
        compiler_params=pltpu.CompilerParams(
            collective_id=0, has_side_effects=True, vmem_limit_bytes=64 * 1024 * 1024 - 65536
        ),
    )(*operands)


def finish_kernel(
    bo_ref, tok_ref, giw_ref, gow_ref, ggw_ref, guw_ref, gdw_ref, gains_ref, sums_ref,
    bo_out, loss_out, tok_out, ag_out, iw_out, qg_out, kg_out, ow_out, fg_out, gw_out, uw_out, dw_out,
):
    for src, dst in (
        (bo_ref, bo_out), (tok_ref, tok_out), (giw_ref, iw_out), (gow_ref, ow_out),
        (ggw_ref, gw_out), (guw_ref, uw_out), (gdw_ref, dw_out),
    ):
        dst[...] = src[...]
    qg_out[...] = sums_ref[0:1, 0:64]
    kg_out[...] = sums_ref[1:2, 0:64]
    loss_out[...] = sums_ref[2:3, 0:1]
    ag_out[...] = gains_ref[0:1, :]
    fg_out[...] = gains_ref[1:2, :]


def finish(*operands):
    def shape(dims, kind=F32):
        return jax.ShapeDtypeStruct(dims, kind)

    vmem = pl.BlockSpec(memory_space=pltpu.VMEM)
    return pl.pallas_call(
        finish_kernel,
        out_shape=(
            shape((2, 128, 1024), BF16), shape((1, 1)), shape((2, 128, 1024)), shape((1, 8)), shape((8, 2048)),
            shape((1, 64)), shape((1, 64)), shape((8, 1024)), shape((1, 8)), shape((8, 4608)), shape((8, 4608)),
            shape((8, 4608)),
        ),
        in_specs=[vmem] * 9,
        out_specs=(vmem,) * 12,
        name="finish",
    )(*operands)


def body(
    tokens, teacher, lengths, attention_gain, input_weight, query_gain, key_gain,
    output_weight, feed_gain, gate_weight, up_weight, down_weight,
):
    columns_in = jnp.pad(jnp.stack([attention_gain, feed_gain], axis=-1).astype(F32), ((0, 0), (0, 126)))
    rows_in = jnp.stack([query_gain, key_gain]).astype(F32)
    rows_in = jnp.pad(jnp.concatenate([rows_in, rows_in], axis=-1), ((0, 6), (0, 0)))
    freqs = np.float64(THETA) ** (-(2.0 * np.arange(32)) / 64)
    freqs = jnp.asarray(np.tile(freqs.astype(np.float32), 4)[None])
    (
        block_out, token_grads, input_grad, output_grad, gate_grad, up_grad, down_grad, gain_grads, sums,
    ) = step_call(
        lengths, tokens, teacher, input_weight, output_weight.T, gate_weight, up_weight, down_weight.T,
        columns_in, rows_in, freqs,
    )
    (
        block_out, loss, token_grads, attention_gain_grad, input_grad, query_gain_grad, key_gain_grad, output_grad,
        feed_gain_grad, gate_grad, up_grad, down_grad,
    ) = finish(
        block_out, token_grads, input_grad, output_grad, gate_grad, up_grad, down_grad, gain_grads, sums
    )
    return (
        block_out, loss.reshape(()), token_grads, attention_gain_grad.reshape(8), input_grad,
        query_gain_grad.reshape(64), key_gain_grad.reshape(64),
        output_grad.T, feed_gain_grad.reshape(8), gate_grad, up_grad, down_grad.T,
    )


def solution(mesh):
    tokens, split = P("fsdp", "seq", None), P(("fsdp", "seq"))
    rows, columns = P(("fsdp", "seq"), None), P(None, ("fsdp", "seq"))
    return jax.shard_map(
        body,
        mesh=mesh,
        in_specs=(
            tokens, tokens, P("fsdp"), split, rows, P(), P(), columns, split, rows, rows, columns,
        ),
        out_specs=(
            tokens, P(), tokens, split, rows, P(), P(), columns, split, rows, rows, columns,
        ),
        check_vma=False,
    )
```
